32 devices in a mesh: blk: 4 (over z), fft: 8 (over y, x, core).
Axes of the slice: x: 2, y: 2, z: 4, core: 2. Of those that a mesh axis runs over, the one named last changes fastest.
Arguments:
- tokens: bfloat16 [4096, 1024], P(('blk', 'fft')), may hold values from -6 to 6
- w_in: bfloat16 [1024, 1536], replicated, may hold values from -0.1875 to 0.1875
- conv_taps: float32 [3, 1536], replicated, may hold values from -3 to 3
- causal_taps: bfloat16 [4096, 512], P(('blk', 'fft')), may hold values from -0.15625 to 0.15625
- anticausal_taps: bfloat16 [4096, 512], P(('blk', 'fft')), may hold values from -0.15625 to 0.15625
- skip_gain: float32 [512], replicated, may hold values from 0.1 to 1.9
- w_out: bfloat16 [512, 1024], replicated, may hold values from -0.25 to 0.25
Outputs:
- mixed_out: bfloat16 [4096, 1024], P(('blk', 'fft'))
The draws below stay inside these ranges and needn't reach their ends.
All inputs are finite; a program needn't handle non-finite values.
Results may differ from the reference program's by a relative error of at most 0.013.
Values may be sent and summed in bfloat16 or wider, within the bound.
A program may use at most 64 MiB of HBM per device.

```python
import jax
import jax.numpy as jnp

D = 1024
CH = 512
SEQ = 4096


def block_scale(stream_key, dims, split, smallest, largest):
    def one(dim, shards_of):
        draws = jax.random.uniform(jax.random.fold_in(jax.random.fold_in(stream_key, 6), dim), (shards_of,), jnp.float32, smallest / len(split), largest / len(split))
        return jnp.repeat(jnp.exp(draws), dims[dim] // shards_of).reshape((-1,) + (1,) * (len(dims) - dim - 1))

    factor_of = one(*split[0])
    for cut in split[1:]:
        factor_of = factor_of * one(*cut)
    return factor_of


def scatter_about(rng, dims, width, most, shards=(), kind=jnp.bfloat16):
    result = jax.random.normal(rng, dims, jnp.float32) * width
    if len(shards) > 0:
        result = block_scale(rng, dims, shards, -0.22, 0.18) * result
    return jnp.clip(result, min=-most, max=most).astype(kind)


def setup_inputs(seed: int = 0) -> dict:
    seeds = jax.random.split(jax.random.key(seed), 8)
    return {
        "tokens": scatter_about(seeds[0], (SEQ, D), 1.0, 6.0, ((0, 32),)),
        "w_in": scatter_about(seeds[1], (D, 3 * CH), D ** -0.5, 0.1875),
        "conv_taps": scatter_about(seeds[2], (3, 3 * CH), 0.6, 3.0, (), jnp.float32),
        "causal_taps": scatter_about(seeds[3], (SEQ, CH), (1.0 / (2 * SEQ) ** 0.5), 0.15625, ((0, 32),)),
        "anticausal_taps": scatter_about(seeds[4], (SEQ, CH), (1.0 / (2 * SEQ) ** 0.5), 0.15625, ((0, 32),)),
        "skip_gain": jnp.clip(1.0 + 0.18 * jax.random.normal(seeds[5], (CH,), jnp.float32), 0.1, 1.9),
        "w_out": scatter_about(seeds[6], (CH, D), CH ** -0.5, 0.25),
    }


def reference(tokens, w_in, conv_taps, causal_taps, anticausal_taps, skip_gain, w_out):
    proj = jnp.dot(tokens, w_in, preferred_element_type=jnp.float32).astype(jnp.bfloat16)
    framed = jnp.pad(proj.astype(jnp.float32), ((1, 1), (0, 0)))
    short = conv_taps[0] * framed[:-2] + conv_taps[1] * framed[1:-1] + conv_taps[2] * framed[2:]
    first = short[:, :CH]
    second = short[:, CH:2 * CH]
    value_part = short[:, 2 * CH:]
    signal = first * value_part
    position = jnp.arange(SEQ, dtype=jnp.int32)
    anticausal = jnp.where(position[:, None] > 0, anticausal_taps.astype(jnp.float32), 0.0)
    circular = jnp.concatenate([causal_taps.astype(jnp.float32), anticausal], axis=0)
    padded = jnp.concatenate([signal, jnp.zeros_like(signal)], axis=0)
    spectrum = jnp.fft.rfft(padded, axis=0) * jnp.fft.rfft(circular, axis=0)
    convolved = jnp.fft.irfft(spectrum, n=2 * SEQ, axis=0)[:SEQ]
    convolved = convolved + skip_gain * signal
    gated = (second * convolved).astype(jnp.bfloat16)
    return jnp.dot(gated, w_out, preferred_element_type=jnp.float32).astype(jnp.bfloat16)
```

```python
import functools
import math

import jax
import jax.numpy as jnp
import ml_dtypes
import numpy as np
from jax import lax
from jax.experimental import pallas as pl
from jax.experimental.pallas import tpu as pltpu
from jax.sharding import PartitionSpec as P

MESH = pl.DeviceIdType.MESH


def with_halo(cells, sides, width):
    for axis, dim in sides:
        count = lax.axis_size(axis)
        ends = count - 1
        head = lax.slice_in_dim(cells, 0, width, axis=dim)
        tail = lax.slice_in_dim(cells, cells.shape[dim] - width, cells.shape[dim], axis=dim)
        cells = jnp.concatenate(
            [
                lax.ppermute(tail, axis, [(i, (i + 1) % count) for i in range(ends)]),
                cells,
                lax.ppermute(head, axis, [((i + 1) % count, i) for i in range(ends)]),
            ],
            axis=dim,
        )
    return cells


def shortened(x):

    def short(part):
        return part.astype(jnp.bfloat16) if part.dtype == jnp.float32 else part

    return jax.tree.map(short, x)


def log_count(count):
    return count.bit_length() - 1


def dft_matrix(count, sign, scale):
    grid = jnp.arange(count, dtype=jnp.int32)
    angle = (
        sign * 2.0 * math.pi * (grid[:, None] * grid[None, :] % count).astype(jnp.float32) / count
    )
    return (jnp.cos(angle) * scale, jnp.sin(angle) * scale)


def local_convolution(signal_cols, causal_cols, anti_cols):
    seq_len = signal_cols.shape[0]
    width = signal_cols.shape[1]
    length = 2 * seq_len
    rows_p = 2 ** (log_count(length) // 2)
    cols_q = length // rows_p
    high = lax.Precision.HIGHEST
    p_real, p_imag = dft_matrix(rows_p, -1.0, 1.0)
    q_real, q_imag = dft_matrix(cols_q, -1.0, 1.0)
    pp_real, pp_imag = dft_matrix(rows_p, 1.0, 1.0 / length)
    qp_real, qp_imag = dft_matrix(cols_q, 1.0, 1.0)
    k_grid = jnp.arange(rows_p, dtype=jnp.int32)
    n_grid = jnp.arange(cols_q, dtype=jnp.int32)
    tw_angle = (
        -2.0 * math.pi * (k_grid[:, None] * n_grid[None, :] % length).astype(jnp.float32) / length
    )
    tw_cos = jnp.cos(tw_angle)
    tw_sin = jnp.sin(tw_angle)

    def forward(grid_rows):
        half = grid_rows.shape[1]
        b_real = jnp.einsum("kp,cpq->ckq", p_real[:, :half], grid_rows, precision=high)
        b_imag = jnp.einsum("kp,cpq->ckq", p_imag[:, :half], grid_rows, precision=high)
        c_real = b_real * tw_cos - b_imag * tw_sin
        c_imag = b_real * tw_sin + b_imag * tw_cos
        x_real = jnp.einsum("ckq,qr->ckr", c_real, q_real, precision=high) - jnp.einsum(
            "ckq,qr->ckr", c_imag, q_imag, precision=high
        )
        x_imag = jnp.einsum("ckq,qr->ckr", c_real, q_imag, precision=high) + jnp.einsum(
            "ckq,qr->ckr", c_imag, q_real, precision=high
        )
        return (x_real, x_imag)

    sig_grid = signal_cols.T.reshape(width, rows_p // 2, cols_q)
    filt_grid = jnp.concatenate([causal_cols, anti_cols], axis=0).T.reshape(width, rows_p, cols_q)
    s_real, s_imag = forward(sig_grid)
    f_real, f_imag = forward(filt_grid)
    y_real = s_real * f_real - s_imag * f_imag
    y_imag = s_real * f_imag + s_imag * f_real
    d_real = jnp.einsum("ckq,qr->ckr", y_real, qp_real, precision=high) - jnp.einsum(
        "ckq,qr->ckr", y_imag, qp_imag, precision=high
    )
    d_imag = jnp.einsum("ckq,qr->ckr", y_real, qp_imag, precision=high) + jnp.einsum(
        "ckq,qr->ckr", y_imag, qp_real, precision=high
    )
    e_real = d_real * tw_cos + d_imag * tw_sin
    e_imag = d_imag * tw_cos - d_real * tw_sin
    half_rows = rows_p // 2
    out_grid = jnp.einsum("nk,ckq->cnq", pp_real[:half_rows], e_real, precision=high) - jnp.einsum(
        "nk,ckq->cnq", pp_imag[:half_rows], e_imag, precision=high
    )
    return out_grid.reshape(width, seq_len).T


def body(tokens, w_in, conv_taps, causal_taps, anticausal_taps, skip_gain, w_out):
    tok_rows = tokens.shape[0]
    channels = w_out.shape[0]
    groups = lax.axis_size("fft")
    blk_index = lax.axis_index("blk")
    fft_index = lax.axis_index("fft")
    device_index = blk_index * groups + fft_index
    position = device_index * tok_rows + jnp.arange(tok_rows, dtype=jnp.int32)
    proj = jnp.dot(tokens, w_in, preferred_element_type=jnp.float32).astype(jnp.bfloat16)
    framed = with_halo(proj, ((("blk", "fft"), 0),), 1).astype(jnp.float32)
    short = conv_taps[0] * framed[:-2] + conv_taps[1] * framed[1:-1] + conv_taps[2] * framed[2:]
    first = short[:, :channels]
    second = short[:, channels : 2 * channels]
    value_part = short[:, 2 * channels :]
    signal = first * value_part
    anticausal = jnp.where(position[:, None] > 0, anticausal_taps.astype(jnp.float32), 0.0)
    causal = causal_taps.astype(jnp.float32)
    moved = (
        lax.all_to_all(
            signal.astype(jnp.bfloat16), "fft", split_axis=1, concat_axis=0, tiled=True
        ).astype(signal.dtype),
        lax.all_to_all(
            causal.astype(jnp.bfloat16), "fft", split_axis=1, concat_axis=0, tiled=True
        ).astype(causal.dtype),
        lax.all_to_all(
            anticausal.astype(jnp.bfloat16), "fft", split_axis=1, concat_axis=0, tiled=True
        ).astype(anticausal.dtype),
    )
    moved = (
        lax.all_to_all(
            moved[0].astype(jnp.bfloat16), "blk", split_axis=1, concat_axis=0, tiled=True
        ).astype(jnp.float32),
        lax.all_to_all(
            moved[1].astype(jnp.bfloat16), "blk", split_axis=1, concat_axis=0, tiled=True
        ).astype(jnp.float32),
        lax.all_to_all(
            moved[2].astype(jnp.bfloat16), "blk", split_axis=1, concat_axis=0, tiled=True
        ).astype(jnp.float32),
    )
    conv_cols = local_convolution(moved[0], moved[1], moved[2])
    returned = lax.all_to_all(
        shortened(conv_cols), "blk", split_axis=0, concat_axis=1, tiled=True
    ).astype(conv_cols.dtype)
    convolved = lax.all_to_all(
        shortened(returned), "fft", split_axis=0, concat_axis=1, tiled=True
    ).astype(returned.dtype)
    convolved = convolved + skip_gain * signal
    gated = (second * convolved).astype(jnp.bfloat16)
    return jnp.dot(gated, w_out, preferred_element_type=jnp.float32).astype(jnp.bfloat16)


def grid_constants(blocks, width):
    length = 2 * blocks * width
    half_freq = np.arange(blocks) + 0.5

    def split(mat):
        high = mat.astype(ml_dtypes.bfloat16)
        low = (mat - high.astype(np.float64)).astype(ml_dtypes.bfloat16)
        return high, low

    rows = np.outer(half_freq, np.arange(2 * blocks)) * (2.0 * np.pi / (2 * blocks))
    flip = np.where(np.arange(2 * blocks) < blocks, 1.0, -1.0)
    across = np.concatenate([np.cos(rows), -np.sin(rows)], axis=0) * flip
    across = np.concatenate(split(across), axis=0)
    turn = np.outer(half_freq, np.arange(width)) * (2.0 * np.pi / length)
    twist = np.stack([np.cos(turn), np.sin(turn)]).astype(np.float32)
    grid = np.outer(np.arange(width), np.arange(width)) % width * (2.0 * np.pi / width)
    cos, sin = np.cos(grid), np.sin(grid)
    within = np.stack(split(np.block([[cos, -sin], [sin, cos]])))
    within_back = np.stack(split(np.block([[cos, sin], [-sin, cos]])))
    back = rows[:, :blocks].T
    back = np.concatenate([np.cos(back), -np.sin(back)], axis=1) * (2.0 / length)
    back = np.concatenate(split(back), axis=0)
    return across, twist, within, within_back, back


def dot32(a, b):
    return jnp.dot(a, b, preferred_element_type=jnp.float32)


def halves(x):
    high = x.astype(jnp.bfloat16)
    low = (x - high.astype(jnp.float32)).astype(jnp.bfloat16)
    return high, low


def mixer_kernel(
    blocks,
    groups,
    tokens,
    causal,
    anti,
    conv_taps,
    skip_gain,
    across,
    twist,
    back,
    w_in_hbm,
    w_out_hbm,
    within_hbm,
    within_back_hbm,
    out,
    w_in,
    w_out,
    within,
    within_back,
    framed,
    edge_out,
    edge_in,
    filt_out,
    filt_in,
    sig_out,
    sig_in,
    ret_out,
    ret_in,
    spread,
    spectrum,
    load_sem,
    edge_send,
    edge_recv,
    filt_send,
    filt_recv,
    sig_send,
    sig_recv,
    ret_send,
    ret_recv,
):
    f32, bf16 = jnp.float32, jnp.bfloat16
    width, depth = tokens.shape
    channels = w_out.shape[0]
    mine = channels // blocks
    me = lax.axis_index("blk") * groups + lax.axis_index("fft")

    def place(peer):
        return (peer // groups, peer % groups)

    loads = [
        pltpu.make_async_copy(src, dst, load_sem.at[i])
        for i, (src, dst) in enumerate(
            (
                (w_in_hbm, w_in),
                (within_hbm, within),
                (within_back_hbm, within_back),
                (w_out_hbm, w_out),
            )
        )
    ]
    for load in loads:
        load.start()

    barrier = pltpu.get_barrier_semaphore()

    @pl.loop(1, blocks)
    def _(i):
        pl.semaphore_signal(
            barrier, inc=1, device_id=place((me + i) % blocks), device_id_type=MESH
        )

    def send_all(src, dst, send_sem, recv_sem):
        @pl.loop(1, blocks)
        def _(i):
            peer = (me + i) % blocks
            pltpu.make_async_remote_copy(
                src_ref=src.at[peer],
                dst_ref=dst.at[me],
                send_sem=send_sem,
                recv_sem=recv_sem,
                device_id=place(peer),
                device_id_type=MESH,
            ).start()

        pltpu.make_async_copy(src.at[me], dst.at[me], recv_sem).start()

    def arrived(dst, recv_sem):
        pltpu.make_async_copy(dst, dst, recv_sem).wait()

    def sent(src, send_sem):
        most = src.at[pl.ds(0, blocks - 1)]
        pltpu.make_async_copy(most, most, send_sem).wait()

    edge_out[0] = tokens[width - 16 :, :].astype(f32)[15:16]
    edge_out[1] = tokens[0:16, :].astype(f32)[0:1]
    filt_out[:, 0:mine, :] = (
        causal[...].astype(f32).T.astype(bf16).reshape(blocks, mine, width)
    )
    unused = (lax.broadcasted_iota(jnp.int32, anti.shape, 0) == 0) & (me == 0)
    filt_out[:, mine:, :] = (
        jnp.where(unused, 0.0, anti[...].astype(f32))
        .T.astype(bf16)
        .reshape(blocks, mine, width)
    )
    pl.semaphore_wait(barrier, blocks - 1)
    edges = [
        pltpu.make_async_remote_copy(
            src_ref=edge_out.at[i],
            dst_ref=edge_in.at[i],
            send_sem=edge_send.at[i],
            recv_sem=edge_recv.at[i],
            device_id=place((me + step) % blocks),
            device_id_type=MESH,
        )
        for i, step in ((0, 1), (1, blocks - 1))
    ]
    for edge in edges:
        edge.start()
    send_all(filt_out, filt_in, filt_send, filt_recv)

    framed[0:width, :] = tokens[...]
    loads[0].wait()
    for edge in edges:
        edge.wait()
    row16 = lax.broadcasted_iota(jnp.int32, (16, depth), 0)
    prev = jnp.where(me == 0, 0.0, edge_in[0])
    following = jnp.where(me == blocks - 1, 0.0, edge_in[1])
    framed[width:, :] = jnp.where(
        row16 == 0, prev, jnp.where(row16 == 1, following, 0.0)
    ).astype(bf16)

    row = lax.broadcasted_iota(jnp.int32, (width, channels), 0)

    def stream(part):
        cols = slice(part * channels, (part + 1) * channels)
        proj = dot32(framed[...], w_in[:, cols]).astype(bf16).astype(f32)
        here = proj[:width]
        before = jnp.where(row == 0, proj[width : width + 1], pltpu.roll(here, 1, 0))
        after = jnp.where(
            row == width - 1, proj[width + 1 : width + 2], pltpu.roll(here, width - 1, 0)
        )
        taps = conv_taps[:, cols]
        return taps[0:1] * before + taps[1:2] * here + taps[2:3] * after

    signal = stream(0) * stream(2)
    sig_out[...] = signal.T.astype(bf16).reshape(blocks, mine, width)
    send_all(sig_out, sig_in, sig_send, sig_recv)
    second = stream(1)

    cos, sin = twist[0], twist[1]

    def lane(x, c):
        return x[:, c * width : (c + 1) * width]

    def times(x, mats):
        high, low = halves(x)
        return dot32(high, mats[0]) + dot32(low, mats[0]) + dot32(high, mats[1])

    def forward(grid, mats):
        both = dot32(mats, grid)
        freq = both[: 2 * blocks] + both[2 * blocks :]
        parts = []
        for c in range(mine):
            real, imag = lane(freq[:blocks], c), lane(freq[blocks:], c)
            parts.append(
                jnp.concatenate([real * cos + imag * sin, imag * cos - real * sin], axis=1)
            )
        return times(jnp.concatenate(parts, axis=0), within)

    loads[1].wait()
    loads[2].wait()
    arrived(filt_in, filt_recv)
    spread[...] = filt_in[...].astype(f32).reshape(2 * blocks * mine, width)
    grid = jnp.concatenate(
        [
            jnp.concatenate(
                [
                    spread[pl.ds(c, blocks, stride=2 * mine), :],
                    spread[pl.ds(mine + c, blocks, stride=2 * mine), :],
                ],
                axis=0,
            ).astype(bf16)
            for c in range(mine)
        ],
        axis=1,
    )
    spectrum[...] = forward(grid, across[...])

    arrived(sig_in, sig_recv)
    spread[0 : blocks * mine, :] = sig_in[...].astype(f32).reshape(blocks * mine, width)
    grid = jnp.concatenate(
        [spread[pl.ds(c, blocks, stride=mine), :].astype(bf16) for c in range(mine)], axis=1
    )
    sig = forward(grid, across[:, 0:blocks])
    s_real, s_imag = sig[:, :width], sig[:, width:]
    f_real, f_imag = spectrum[:, :width], spectrum[:, width:]
    product = jnp.concatenate(
        [s_real * f_real - s_imag * f_imag, s_real * f_imag + s_imag * f_real], axis=1
    )
    turned = times(product, within_back)
    parts = []
    for c in range(mine):
        rows = turned[c * blocks : (c + 1) * blocks]
        real, imag = rows[:, :width], rows[:, width:]
        parts.append(
            jnp.concatenate([real * cos - imag * sin, imag * cos + real * sin], axis=0)
        )
    high, low = halves(jnp.concatenate(parts, axis=1))
    both = dot32(back[...], high)
    conv = both[:blocks] + both[blocks:] + dot32(back[0:blocks, :], low)
    for c in range(mine):
        spread[pl.ds(c, blocks, stride=mine), :] = lane(conv, c)
    ret_out[...] = spread[0 : blocks * mine, :].astype(bf16).reshape(blocks, mine, width)
    send_all(ret_out, ret_in, ret_send, ret_recv)

    direct = skip_gain[...] * signal
    loads[3].wait()
    arrived(ret_in, ret_recv)
    convolved = ret_in[...].astype(f32).reshape(channels, width).T + direct
    gated = (second * convolved).astype(bf16)
    out[...] = dot32(gated, w_out[...]).astype(bf16)
    sent(filt_out, filt_send)
    sent(sig_out, sig_send)
    sent(ret_out, ret_send)


def one_kernel(tokens, w_in, conv_taps, causal_taps, anticausal_taps, skip_gain, w_out):
    width, depth = tokens.shape
    channels = w_out.shape[0]
    groups = lax.axis_size("fft")
    blocks = lax.axis_size("blk") * groups
    mine = channels // blocks
    across, twist, within, within_back, back = grid_constants(blocks, width)
    f32, bf16 = jnp.float32, jnp.bfloat16
    vmem = pl.BlockSpec(memory_space=pltpu.VMEM)
    whole = pl.BlockSpec(memory_space=pl.ANY)
    one = pltpu.SemaphoreType.DMA
    return pl.pallas_call(
        functools.partial(mixer_kernel, blocks, groups),
        out_shape=jax.ShapeDtypeStruct((width, w_out.shape[1]), bf16),
        in_specs=[vmem] * 8 + [whole] * 4,
        out_specs=vmem,
        scratch_shapes=[
            pltpu.VMEM(w_in.shape, bf16),
            pltpu.VMEM(w_out.shape, bf16),
            pltpu.VMEM(within.shape, bf16),
            pltpu.VMEM(within_back.shape, bf16),
            pltpu.VMEM((width + 16, depth), bf16),
            pltpu.VMEM((2, 1, depth), f32),
            pltpu.VMEM((2, 1, depth), f32),
            pltpu.VMEM((blocks, 2 * mine, width), bf16),
            pltpu.VMEM((blocks, 2 * mine, width), bf16),
            pltpu.VMEM((blocks, mine, width), bf16),
            pltpu.VMEM((blocks, mine, width), bf16),
            pltpu.VMEM((blocks, mine, width), bf16),
            pltpu.VMEM((blocks, mine, width), bf16),
            pltpu.VMEM((2 * blocks * mine, width), f32),
            pltpu.VMEM((blocks * mine, 2 * width), f32),
            one((4,)),
            one((2,)),
            one((2,)),
            one,
            one,
            one,
            one,
            one,
            one,
        ],
        compiler_params=pltpu.CompilerParams(
            collective_id=0, has_side_effects=True, vmem_limit_bytes=48 * 2**20
        ),
    )(
        tokens,
        causal_taps,
        anticausal_taps,
        conv_taps,
        skip_gain[None, :],
        jnp.asarray(across),
        jnp.asarray(twist),
        jnp.asarray(back),
        w_in,
        w_out,
        jnp.asarray(within),
        jnp.asarray(within_back),
    )


def mixer(tokens, w_in, conv_taps, causal_taps, anticausal_taps, skip_gain, w_out):
    devices = lax.axis_size("blk") * lax.axis_size("fft")
    fits = tokens.shape[0] == 128 and w_out.shape[0] == 16 * devices
    chosen = one_kernel if fits else body
    return chosen(tokens, w_in, conv_taps, causal_taps, anticausal_taps, skip_gain, w_out)


def solution(mesh):
    in_specs = (
        P(("blk", "fft"), None),
        P(),
        P(),
        P(("blk", "fft"), None),
        P(("blk", "fft"), None),
        P(),
        P(),
    )
    out_specs = P(("blk", "fft"), None)
    return jax.shard_map(mixer, mesh=mesh, in_specs=in_specs, out_specs=out_specs, check_vma=False)
```

```python
import functools
import math

import jax
import jax.numpy as jnp
import ml_dtypes
import numpy as np
from jax import lax
from jax.experimental import pallas as pl
from jax.experimental.pallas import tpu as pltpu
from jax.sharding import PartitionSpec as P

MESH = pl.DeviceIdType.MESH


def with_halo(cells, sides, width):
    for axis, dim in sides:
        count = lax.axis_size(axis)
        ends = count - 1
        head = lax.slice_in_dim(cells, 0, width, axis=dim)
        tail = lax.slice_in_dim(cells, cells.shape[dim] - width, cells.shape[dim], axis=dim)
        cells = jnp.concatenate(
            [
                lax.ppermute(tail, axis, [(i, (i + 1) % count) for i in range(ends)]),
                cells,
                lax.ppermute(head, axis, [((i + 1) % count, i) for i in range(ends)]),
            ],
            axis=dim,
        )
    return cells


def shortened(x):

    def short(part):
        return part.astype(jnp.bfloat16) if part.dtype == jnp.float32 else part

    return jax.tree.map(short, x)


def log_count(count):
    return count.bit_length() - 1


def dft_matrix(count, sign, scale):
    grid = jnp.arange(count, dtype=jnp.int32)
    angle = (
        sign * 2.0 * math.pi * (grid[:, None] * grid[None, :] % count).astype(jnp.float32) / count
    )
    return (jnp.cos(angle) * scale, jnp.sin(angle) * scale)


def local_convolution(signal_cols, causal_cols, anti_cols):
    seq_len = signal_cols.shape[0]
    width = signal_cols.shape[1]
    length = 2 * seq_len
    rows_p = 2 ** (log_count(length) // 2)
    cols_q = length // rows_p
    high = lax.Precision.HIGHEST
    p_real, p_imag = dft_matrix(rows_p, -1.0, 1.0)
    q_real, q_imag = dft_matrix(cols_q, -1.0, 1.0)
    pp_real, pp_imag = dft_matrix(rows_p, 1.0, 1.0 / length)
    qp_real, qp_imag = dft_matrix(cols_q, 1.0, 1.0)
    k_grid = jnp.arange(rows_p, dtype=jnp.int32)
    n_grid = jnp.arange(cols_q, dtype=jnp.int32)
    tw_angle = (
        -2.0 * math.pi * (k_grid[:, None] * n_grid[None, :] % length).astype(jnp.float32) / length
    )
    tw_cos = jnp.cos(tw_angle)
    tw_sin = jnp.sin(tw_angle)

    def forward(grid_rows):
        half = grid_rows.shape[1]
        b_real = jnp.einsum("kp,cpq->ckq", p_real[:, :half], grid_rows, precision=high)
        b_imag = jnp.einsum("kp,cpq->ckq", p_imag[:, :half], grid_rows, precision=high)
        c_real = b_real * tw_cos - b_imag * tw_sin
        c_imag = b_real * tw_sin + b_imag * tw_cos
        x_real = jnp.einsum("ckq,qr->ckr", c_real, q_real, precision=high) - jnp.einsum(
            "ckq,qr->ckr", c_imag, q_imag, precision=high
        )
        x_imag = jnp.einsum("ckq,qr->ckr", c_real, q_imag, precision=high) + jnp.einsum(
            "ckq,qr->ckr", c_imag, q_real, precision=high
        )
        return (x_real, x_imag)

    sig_grid = signal_cols.T.reshape(width, rows_p // 2, cols_q)
    filt_grid = jnp.concatenate([causal_cols, anti_cols], axis=0).T.reshape(width, rows_p, cols_q)
    s_real, s_imag = forward(sig_grid)
    f_real, f_imag = forward(filt_grid)
    y_real = s_real * f_real - s_imag * f_imag
    y_imag = s_real * f_imag + s_imag * f_real
    d_real = jnp.einsum("ckq,qr->ckr", y_real, qp_real, precision=high) - jnp.einsum(
        "ckq,qr->ckr", y_imag, qp_imag, precision=high
    )
    d_imag = jnp.einsum("ckq,qr->ckr", y_real, qp_imag, precision=high) + jnp.einsum(
        "ckq,qr->ckr", y_imag, qp_real, precision=high
    )
    e_real = d_real * tw_cos + d_imag * tw_sin
    e_imag = d_imag * tw_cos - d_real * tw_sin
    half_rows = rows_p // 2
    out_grid = jnp.einsum("nk,ckq->cnq", pp_real[:half_rows], e_real, precision=high) - jnp.einsum(
        "nk,ckq->cnq", pp_imag[:half_rows], e_imag, precision=high
    )
    return out_grid.reshape(width, seq_len).T


def body(tokens, w_in, conv_taps, causal_taps, anticausal_taps, skip_gain, w_out):
    tok_rows = tokens.shape[0]
    channels = w_out.shape[0]
    groups = lax.axis_size("fft")
    blk_index = lax.axis_index("blk")
    fft_index = lax.axis_index("fft")
    device_index = blk_index * groups + fft_index
    position = device_index * tok_rows + jnp.arange(tok_rows, dtype=jnp.int32)
    proj = jnp.dot(tokens, w_in, preferred_element_type=jnp.float32).astype(jnp.bfloat16)
    framed = with_halo(proj, ((("blk", "fft"), 0),), 1).astype(jnp.float32)
    short = conv_taps[0] * framed[:-2] + conv_taps[1] * framed[1:-1] + conv_taps[2] * framed[2:]
    first = short[:, :channels]
    second = short[:, channels : 2 * channels]
    value_part = short[:, 2 * channels :]
    signal = first * value_part
    anticausal = jnp.where(position[:, None] > 0, anticausal_taps.astype(jnp.float32), 0.0)
    causal = causal_taps.astype(jnp.float32)
    moved = (
        lax.all_to_all(
            signal.astype(jnp.bfloat16), "fft", split_axis=1, concat_axis=0, tiled=True
        ).astype(signal.dtype),
        lax.all_to_all(
            causal.astype(jnp.bfloat16), "fft", split_axis=1, concat_axis=0, tiled=True
        ).astype(causal.dtype),
        lax.all_to_all(
            anticausal.astype(jnp.bfloat16), "fft", split_axis=1, concat_axis=0, tiled=True
        ).astype(anticausal.dtype),
    )
    moved = (
        lax.all_to_all(
            moved[0].astype(jnp.bfloat16), "blk", split_axis=1, concat_axis=0, tiled=True
        ).astype(jnp.float32),
        lax.all_to_all(
            moved[1].astype(jnp.bfloat16), "blk", split_axis=1, concat_axis=0, tiled=True
        ).astype(jnp.float32),
        lax.all_to_all(
            moved[2].astype(jnp.bfloat16), "blk", split_axis=1, concat_axis=0, tiled=True
        ).astype(jnp.float32),
    )
    conv_cols = local_convolution(moved[0], moved[1], moved[2])
    returned = lax.all_to_all(
        shortened(conv_cols), "blk", split_axis=0, concat_axis=1, tiled=True
    ).astype(conv_cols.dtype)
    convolved = lax.all_to_all(
        shortened(returned), "fft", split_axis=0, concat_axis=1, tiled=True
    ).astype(returned.dtype)
    convolved = convolved + skip_gain * signal
    gated = (second * convolved).astype(jnp.bfloat16)
    return jnp.dot(gated, w_out, preferred_element_type=jnp.float32).astype(jnp.bfloat16)


def grid_constants(blocks, width):
    length = 2 * blocks * width
    half_freq = np.arange(blocks) + 0.5

    def split(mat):
        high = mat.astype(ml_dtypes.bfloat16)
        low = (mat - high.astype(np.float64)).astype(ml_dtypes.bfloat16)
        return high, low

    rows = np.outer(half_freq, np.arange(2 * blocks)) * (2.0 * np.pi / (2 * blocks))
    flip = np.where(np.arange(2 * blocks) < blocks, 1.0, -1.0)
    across = np.concatenate([np.cos(rows), -np.sin(rows)], axis=0) * flip
    across = np.concatenate(split(across), axis=0)
    turn = np.outer(half_freq, np.arange(width)) * (2.0 * np.pi / length)
    twist = np.stack([np.cos(turn), np.sin(turn)]).astype(np.float32)
    grid = np.outer(np.arange(width), np.arange(width)) % width * (2.0 * np.pi / width)
    cos, sin = np.cos(grid), np.sin(grid)
    within = np.block([[cos, -sin], [sin, cos]]).astype(np.float32)
    back = rows[:, :blocks].T
    back = np.concatenate([np.cos(back), np.sin(back)], axis=1) * (2.0 / length)
    back = np.concatenate(split(back), axis=0)
    return across, twist, within, back


def dot32(a, b):
    return jnp.dot(a, b, preferred_element_type=jnp.float32)


def halves(x):
    high = x.astype(jnp.bfloat16)
    low = (x - high.astype(jnp.float32)).astype(jnp.bfloat16)
    return high, low


def mixer_kernel(
    blocks,
    groups,
    tokens_hbm,
    causal_hbm,
    anti_hbm,
    conv_taps_hbm,
    skip_gain_hbm,
    across_hbm,
    twist_hbm,
    back_hbm,
    w_in_hbm,
    w_out_hbm,
    within_hbm,
    out,
    causal,
    anti,
    conv_taps,
    skip_gain,
    across,
    twist,
    back,
    w_in,
    w_out,
    within_whole,
    within,
    framed,
    edge_out,
    edge_in,
    filt_out,
    filt_in,
    sig_out,
    sig_in,
    ret_out,
    ret_in,
    spread,
    spectrum,
    load_sem,
    edge_send,
    edge_recv,
    filt_send,
    filt_recv,
    sig_send,
    sig_recv,
    ret_send,
    ret_recv,
):
    f32, bf16 = jnp.float32, jnp.bfloat16
    width, depth = tokens_hbm.shape
    channels = w_out.shape[0]
    mine = channels // blocks
    tokens = framed.at[0:width]
    me = lax.axis_index("blk") * groups + lax.axis_index("fft")

    def place(peer):
        return (peer // groups, peer % groups)

    loads = [
        pltpu.make_async_copy(src, dst, load_sem.at[i])
        for i, (src, dst) in enumerate(
            (
                (causal_hbm, causal),
                (anti_hbm, anti),
                (tokens_hbm, tokens),
                (w_in_hbm, w_in),
                (conv_taps_hbm, conv_taps),
                (across_hbm, across),
                (twist_hbm, twist),
                (within_hbm, within_whole),
                (back_hbm, back),
                (w_out_hbm, w_out),
                (skip_gain_hbm, skip_gain),
            )
        )
    ]
    for load in loads:
        load.start()

    barrier = pltpu.get_barrier_semaphore()

    @pl.loop(1, blocks)
    def _(i):
        pl.semaphore_signal(
            barrier, inc=1, device_id=place((me + i) % blocks), device_id_type=MESH
        )

    def send_all(src, dst, send_sem, recv_sem):
        @pl.loop(1, blocks)
        def _(i):
            peer = (me + i) % blocks
            pltpu.make_async_remote_copy(
                src_ref=src.at[peer],
                dst_ref=dst.at[me],
                send_sem=send_sem,
                recv_sem=recv_sem,
                device_id=place(peer),
                device_id_type=MESH,
            ).start()

        pltpu.make_async_copy(src.at[me], dst.at[me], recv_sem).start()

    def arrived(dst, recv_sem):
        pltpu.make_async_copy(dst, dst, recv_sem).wait()

    def sent(src, send_sem):
        most = src.at[pl.ds(0, blocks - 1)]
        pltpu.make_async_copy(most, most, send_sem).wait()

    for load in loads[:3]:
        load.wait()
    edge_out[0] = tokens[width - 16 :, :].astype(f32)[15:16]
    edge_out[1] = tokens[0:16, :].astype(f32)[0:1]
    filt_out[:, 0:mine, :] = (
        causal[...].astype(f32).T.astype(bf16).reshape(blocks, mine, width)
    )
    unused = (lax.broadcasted_iota(jnp.int32, anti.shape, 0) == 0) & (me == 0)
    filt_out[:, mine:, :] = (
        jnp.where(unused, 0.0, anti[...].astype(f32))
        .T.astype(bf16)
        .reshape(blocks, mine, width)
    )
    pl.semaphore_wait(barrier, blocks - 1)
    edges = [
        pltpu.make_async_remote_copy(
            src_ref=edge_out.at[i],
            dst_ref=edge_in.at[i],
            send_sem=edge_send.at[i],
            recv_sem=edge_recv.at[i],
            device_id=place((me + step) % blocks),
            device_id_type=MESH,
        )
        for i, step in ((0, 1), (1, blocks - 1))
    ]
    for edge in edges:
        edge.start()
    send_all(filt_out, filt_in, filt_send, filt_recv)

    for edge in edges:
        edge.wait()
    row16 = lax.broadcasted_iota(jnp.int32, (16, depth), 0)
    prev = jnp.where(me == 0, 0.0, edge_in[0])
    following = jnp.where(me == blocks - 1, 0.0, edge_in[1])
    framed[width:, :] = jnp.where(
        row16 == 0, prev, jnp.where(row16 == 1, following, 0.0)
    ).astype(bf16)

    for load in loads[3:5]:
        load.wait()
    row = lax.broadcasted_iota(jnp.int32, (width, channels), 0)

    def stream(part):
        cols = slice(part * channels, (part + 1) * channels)
        proj = dot32(framed[...], w_in[:, cols]).astype(bf16).astype(f32)
        here = proj[:width]
        before = jnp.where(row == 0, proj[width : width + 1], pltpu.roll(here, 1, 0))
        after = jnp.where(
            row == width - 1, proj[width + 1 : width + 2], pltpu.roll(here, width - 1, 0)
        )
        taps = conv_taps[:, cols]
        return taps[0:1] * before + taps[1:2] * here + taps[2:3] * after

    signal = stream(0) * stream(2)
    sig_out[...] = signal.T.astype(bf16).reshape(blocks, mine, width)
    send_all(sig_out, sig_in, sig_send, sig_recv)
    second = stream(1)

    for load in loads[5:9]:
        load.wait()
    within[0], within[1] = halves(within_whole[...])
    cos, sin = twist[0], twist[1]

    def lane(x, c):
        return x[:, c * width : (c + 1) * width]

    def twisted(real, imag):
        return [real * cos + imag * sin, imag * cos - real * sin]

    def along(x):
        high, low = halves(x)
        return dot32(high, within[0]) + dot32(low, within[0]) + dot32(high, within[1])

    def forward(grid, mats):
        both = dot32(mats, grid)
        freq = both[: 2 * blocks] + both[2 * blocks :]
        parts = []
        for c in range(mine):
            pair = twisted(lane(freq[:blocks], c), lane(freq[blocks:], c))
            parts.append(jnp.concatenate(pair, axis=1))
        return along(jnp.concatenate(parts, axis=0))

    arrived(filt_in, filt_recv)
    spread[...] = filt_in[...].astype(f32).reshape(2 * blocks * mine, width)
    grid = jnp.concatenate(
        [
            jnp.concatenate(
                [
                    spread[pl.ds(c, blocks, stride=2 * mine), :],
                    spread[pl.ds(mine + c, blocks, stride=2 * mine), :],
                ],
                axis=0,
            ).astype(bf16)
            for c in range(mine)
        ],
        axis=1,
    )
    spectrum[...] = forward(grid, across[...])

    arrived(sig_in, sig_recv)
    spread[0 : blocks * mine, :] = sig_in[...].astype(f32).reshape(blocks * mine, width)
    grid = jnp.concatenate(
        [spread[pl.ds(c, blocks, stride=mine), :].astype(bf16) for c in range(mine)], axis=1
    )
    sig = forward(grid, across[:, 0:blocks])
    s_real, s_imag = sig[:, :width], sig[:, width:]
    f_real, f_imag = spectrum[:, :width], spectrum[:, width:]
    product = jnp.concatenate(
        [s_real * f_real - s_imag * f_imag, -(s_real * f_imag + s_imag * f_real)], axis=1
    )
    turned = along(product)
    parts = []
    for c in range(mine):
        rows = turned[c * blocks : (c + 1) * blocks]
        parts.append(jnp.concatenate(twisted(rows[:, :width], rows[:, width:]), axis=0))
    high, low = halves(jnp.concatenate(parts, axis=1))
    both = dot32(back[...], high)
    conv = both[:blocks] + both[blocks:] + dot32(back[0:blocks, :], low)
    for c in range(mine):
        spread[pl.ds(c, blocks, stride=mine), :] = lane(conv, c)
    ret_out[...] = spread[0 : blocks * mine, :].astype(bf16).reshape(blocks, mine, width)
    send_all(ret_out, ret_in, ret_send, ret_recv)

    for load in loads[9:]:
        load.wait()
    direct = skip_gain[...] * signal
    arrived(ret_in, ret_recv)
    convolved = ret_in[...].astype(f32).reshape(channels, width).T + direct
    gated = (second * convolved).astype(bf16)
    out[...] = dot32(gated, w_out[...]).astype(bf16)
    sent(filt_out, filt_send)
    sent(sig_out, sig_send)
    sent(ret_out, ret_send)


def one_kernel(tokens, w_in, conv_taps, causal_taps, anticausal_taps, skip_gain, w_out):
    width, depth = tokens.shape
    channels = w_out.shape[0]
    groups = lax.axis_size("fft")
    blocks = lax.axis_size("blk") * groups
    mine = channels // blocks
    across, twist, within, back = grid_constants(blocks, width)
    f32, bf16 = jnp.float32, jnp.bfloat16
    vmem = pl.BlockSpec(memory_space=pltpu.VMEM)
    whole = pl.BlockSpec(memory_space=pl.ANY)
    one = pltpu.SemaphoreType.DMA
    return pl.pallas_call(
        functools.partial(mixer_kernel, blocks, groups),
        out_shape=jax.ShapeDtypeStruct((width, w_out.shape[1]), bf16),
        in_specs=[whole] * 11,
        out_specs=vmem,
        scratch_shapes=[
            pltpu.VMEM(causal_taps.shape, bf16),
            pltpu.VMEM(anticausal_taps.shape, bf16),
            pltpu.VMEM(conv_taps.shape, f32),
            pltpu.VMEM((1, channels), f32),
            pltpu.VMEM(across.shape, bf16),
            pltpu.VMEM(twist.shape, f32),
            pltpu.VMEM(back.shape, bf16),
            pltpu.VMEM(w_in.shape, bf16),
            pltpu.VMEM(w_out.shape, bf16),
            pltpu.VMEM(within.shape, f32),
            pltpu.VMEM((2,) + within.shape, bf16),
            pltpu.VMEM((width + 16, depth), bf16),
            pltpu.VMEM((2, 1, depth), f32),
            pltpu.VMEM((2, 1, depth), f32),
            pltpu.VMEM((blocks, 2 * mine, width), bf16),
            pltpu.VMEM((blocks, 2 * mine, width), bf16),
            pltpu.VMEM((blocks, mine, width), bf16),
            pltpu.VMEM((blocks, mine, width), bf16),
            pltpu.VMEM((blocks, mine, width), bf16),
            pltpu.VMEM((blocks, mine, width), bf16),
            pltpu.VMEM((2 * blocks * mine, width), f32),
            pltpu.VMEM((blocks * mine, 2 * width), f32),
            one((11,)),
            one((2,)),
            one((2,)),
            one,
            one,
            one,
            one,
            one,
            one,
        ],
        compiler_params=pltpu.CompilerParams(
            collective_id=0, has_side_effects=True, vmem_limit_bytes=63 * 2**20
        ),
    )(
        tokens,
        causal_taps,
        anticausal_taps,
        conv_taps,
        skip_gain[None, :],
        jnp.asarray(across),
        jnp.asarray(twist),
        jnp.asarray(back),
        w_in,
        w_out,
        jnp.asarray(within),
    )


def mixer(tokens, w_in, conv_taps, causal_taps, anticausal_taps, skip_gain, w_out):
    devices = lax.axis_size("blk") * lax.axis_size("fft")
    fits = tokens.shape[0] == 128 and w_out.shape[0] == 16 * devices
    chosen = one_kernel if fits else body
    return chosen(tokens, w_in, conv_taps, causal_taps, anticausal_taps, skip_gain, w_out)


def solution(mesh):
    in_specs = (
        P(("blk", "fft"), None),
        P(),
        P(),
        P(("blk", "fft"), None),
        P(("blk", "fft"), None),
        P(),
        P(),
    )
    out_specs = P(("blk", "fft"), None)
    return jax.shard_map(mixer, mesh=mesh, in_specs=in_specs, out_specs=out_specs, check_vma=False)
```

```python
import functools
import math

import jax
import jax.numpy as jnp
import ml_dtypes
import numpy as np
from jax import lax
from jax.experimental import pallas as pl
from jax.experimental.pallas import tpu as pltpu
from jax.sharding import PartitionSpec as P

MESH = pl.DeviceIdType.MESH


def with_halo(cells, sides, width):
    for axis, dim in sides:
        count = lax.axis_size(axis)
        ends = count - 1
        head = lax.slice_in_dim(cells, 0, width, axis=dim)
        tail = lax.slice_in_dim(cells, cells.shape[dim] - width, cells.shape[dim], axis=dim)
        cells = jnp.concatenate(
            [
                lax.ppermute(tail, axis, [(i, (i + 1) % count) for i in range(ends)]),
                cells,
                lax.ppermute(head, axis, [((i + 1) % count, i) for i in range(ends)]),
            ],
            axis=dim,
        )
    return cells


def shortened(x):

    def short(part):
        return part.astype(jnp.bfloat16) if part.dtype == jnp.float32 else part

    return jax.tree.map(short, x)


def log_count(count):
    return count.bit_length() - 1


def dft_matrix(count, sign, scale):
    grid = jnp.arange(count, dtype=jnp.int32)
    angle = (
        sign * 2.0 * math.pi * (grid[:, None] * grid[None, :] % count).astype(jnp.float32) / count
    )
    return (jnp.cos(angle) * scale, jnp.sin(angle) * scale)


def local_convolution(signal_cols, causal_cols, anti_cols):
    seq_len = signal_cols.shape[0]
    width = signal_cols.shape[1]
    length = 2 * seq_len
    rows_p = 2 ** (log_count(length) // 2)
    cols_q = length // rows_p
    high = lax.Precision.HIGHEST
    p_real, p_imag = dft_matrix(rows_p, -1.0, 1.0)
    q_real, q_imag = dft_matrix(cols_q, -1.0, 1.0)
    pp_real, pp_imag = dft_matrix(rows_p, 1.0, 1.0 / length)
    qp_real, qp_imag = dft_matrix(cols_q, 1.0, 1.0)
    k_grid = jnp.arange(rows_p, dtype=jnp.int32)
    n_grid = jnp.arange(cols_q, dtype=jnp.int32)
    tw_angle = (
        -2.0 * math.pi * (k_grid[:, None] * n_grid[None, :] % length).astype(jnp.float32) / length
    )
    tw_cos = jnp.cos(tw_angle)
    tw_sin = jnp.sin(tw_angle)

    def forward(grid_rows):
        half = grid_rows.shape[1]
        b_real = jnp.einsum("kp,cpq->ckq", p_real[:, :half], grid_rows, precision=high)
        b_imag = jnp.einsum("kp,cpq->ckq", p_imag[:, :half], grid_rows, precision=high)
        c_real = b_real * tw_cos - b_imag * tw_sin
        c_imag = b_real * tw_sin + b_imag * tw_cos
        x_real = jnp.einsum("ckq,qr->ckr", c_real, q_real, precision=high) - jnp.einsum(
            "ckq,qr->ckr", c_imag, q_imag, precision=high
        )
        x_imag = jnp.einsum("ckq,qr->ckr", c_real, q_imag, precision=high) + jnp.einsum(
            "ckq,qr->ckr", c_imag, q_real, precision=high
        )
        return (x_real, x_imag)

    sig_grid = signal_cols.T.reshape(width, rows_p // 2, cols_q)
    filt_grid = jnp.concatenate([causal_cols, anti_cols], axis=0).T.reshape(width, rows_p, cols_q)
    s_real, s_imag = forward(sig_grid)
    f_real, f_imag = forward(filt_grid)
    y_real = s_real * f_real - s_imag * f_imag
    y_imag = s_real * f_imag + s_imag * f_real
    d_real = jnp.einsum("ckq,qr->ckr", y_real, qp_real, precision=high) - jnp.einsum(
        "ckq,qr->ckr", y_imag, qp_imag, precision=high
    )
    d_imag = jnp.einsum("ckq,qr->ckr", y_real, qp_imag, precision=high) + jnp.einsum(
        "ckq,qr->ckr", y_imag, qp_real, precision=high
    )
    e_real = d_real * tw_cos + d_imag * tw_sin
    e_imag = d_imag * tw_cos - d_real * tw_sin
    half_rows = rows_p // 2
    out_grid = jnp.einsum("nk,ckq->cnq", pp_real[:half_rows], e_real, precision=high) - jnp.einsum(
        "nk,ckq->cnq", pp_imag[:half_rows], e_imag, precision=high
    )
    return out_grid.reshape(width, seq_len).T


def body(tokens, w_in, conv_taps, causal_taps, anticausal_taps, skip_gain, w_out):
    tok_rows = tokens.shape[0]
    channels = w_out.shape[0]
    groups = lax.axis_size("fft")
    blk_index = lax.axis_index("blk")
    fft_index = lax.axis_index("fft")
    device_index = blk_index * groups + fft_index
    position = device_index * tok_rows + jnp.arange(tok_rows, dtype=jnp.int32)
    proj = jnp.dot(tokens, w_in, preferred_element_type=jnp.float32).astype(jnp.bfloat16)
    framed = with_halo(proj, ((("blk", "fft"), 0),), 1).astype(jnp.float32)
    short = conv_taps[0] * framed[:-2] + conv_taps[1] * framed[1:-1] + conv_taps[2] * framed[2:]
    first = short[:, :channels]
    second = short[:, channels : 2 * channels]
    value_part = short[:, 2 * channels :]
    signal = first * value_part
    anticausal = jnp.where(position[:, None] > 0, anticausal_taps.astype(jnp.float32), 0.0)
    causal = causal_taps.astype(jnp.float32)
    moved = (
        lax.all_to_all(
            signal.astype(jnp.bfloat16), "fft", split_axis=1, concat_axis=0, tiled=True
        ).astype(signal.dtype),
        lax.all_to_all(
            causal.astype(jnp.bfloat16), "fft", split_axis=1, concat_axis=0, tiled=True
        ).astype(causal.dtype),
        lax.all_to_all(
            anticausal.astype(jnp.bfloat16), "fft", split_axis=1, concat_axis=0, tiled=True
        ).astype(anticausal.dtype),
    )
    moved = (
        lax.all_to_all(
            moved[0].astype(jnp.bfloat16), "blk", split_axis=1, concat_axis=0, tiled=True
        ).astype(jnp.float32),
        lax.all_to_all(
            moved[1].astype(jnp.bfloat16), "blk", split_axis=1, concat_axis=0, tiled=True
        ).astype(jnp.float32),
        lax.all_to_all(
            moved[2].astype(jnp.bfloat16), "blk", split_axis=1, concat_axis=0, tiled=True
        ).astype(jnp.float32),
    )
    conv_cols = local_convolution(moved[0], moved[1], moved[2])
    returned = lax.all_to_all(
        shortened(conv_cols), "blk", split_axis=0, concat_axis=1, tiled=True
    ).astype(conv_cols.dtype)
    convolved = lax.all_to_all(
        shortened(returned), "fft", split_axis=0, concat_axis=1, tiled=True
    ).astype(returned.dtype)
    convolved = convolved + skip_gain * signal
    gated = (second * convolved).astype(jnp.bfloat16)
    return jnp.dot(gated, w_out, preferred_element_type=jnp.float32).astype(jnp.bfloat16)


def grid_constants(blocks, width):
    length = 2 * blocks * width
    half_freq = np.arange(blocks) + 0.5

    def split(mat):
        high = mat.astype(ml_dtypes.bfloat16)
        low = (mat - high.astype(np.float64)).astype(ml_dtypes.bfloat16)
        return high, low

    rows = np.outer(half_freq, np.arange(2 * blocks)) * (2.0 * np.pi / (2 * blocks))
    flip = np.where(np.arange(2 * blocks) < blocks, 1.0, -1.0)
    across = np.concatenate([np.cos(rows), -np.sin(rows)], axis=0) * flip
    across = np.concatenate(split(across), axis=0)
    turn = np.outer(half_freq, np.arange(width)) * (2.0 * np.pi / length)
    twist = np.stack([np.cos(turn), np.sin(turn)]).astype(np.float32)
    grid = np.outer(np.arange(width), np.arange(width)) % width * (2.0 * np.pi / width)
    cos, sin = np.cos(grid), np.sin(grid)
    within = np.block([[cos, -sin], [sin, cos]]).astype(np.float32)
    back = rows[:, :blocks].T
    back = np.concatenate([np.cos(back), np.sin(back)], axis=1) * (2.0 / length)
    back = np.concatenate(split(back), axis=0)
    return across, twist, within, back


def dot32(a, b):
    return jnp.dot(a, b, preferred_element_type=jnp.float32)


def halves(x):
    high = x.astype(jnp.bfloat16)
    low = (x - high.astype(jnp.float32)).astype(jnp.bfloat16)
    return high, low


def mixer_kernel(
    blocks,
    groups,
    tokens_hbm,
    causal_hbm,
    anti_hbm,
    conv_taps_hbm,
    skip_gain_hbm,
    across_hbm,
    twist_hbm,
    back_hbm,
    w_in_hbm,
    w_out_hbm,
    within_hbm,
    out,
    causal,
    anti,
    conv_taps,
    skip_gain,
    across,
    twist,
    back,
    w_in,
    w_out,
    within_whole,
    within,
    framed,
    edge_out,
    edge_in,
    filt_out,
    filt_in,
    sig_out,
    sig_in,
    ret_out,
    ret_in,
    spread,
    spectrum,
    load_sem,
    edge_send,
    edge_recv,
    filt_send,
    filt_recv,
    sig_send,
    sig_recv,
    ret_send,
    ret_recv,
):
    f32, bf16 = jnp.float32, jnp.bfloat16
    width, depth = tokens_hbm.shape
    channels = w_out.shape[0]
    mine = channels // blocks
    tokens = framed.at[0:width]
    blk, fft = lax.axis_index("blk"), lax.axis_index("fft")
    me = blk * groups + fft
    levels = blocks // groups
    peers = []
    for turn in range(levels - 1, -1, -1):
        level = blk ^ turn
        for step in range(groups):
            if turn > 0 or step > 0:
                other = (fft + step) & (groups - 1)
                peers.append((level * groups + other, (level, other)))

    barrier = pltpu.get_barrier_semaphore()
    for _, coords in peers:
        pl.semaphore_signal(barrier, inc=1, device_id=coords, device_id_type=MESH)

    loads = [
        pltpu.make_async_copy(src, dst, load_sem.at[i])
        for i, (src, dst) in enumerate(
            (
                (causal_hbm, causal),
                (anti_hbm, anti),
                (tokens_hbm, tokens),
                (w_in_hbm, w_in),
                (conv_taps_hbm, conv_taps),
                (across_hbm, across),
                (twist_hbm, twist),
                (within_hbm, within_whole),
                (back_hbm, back),
                (w_out_hbm, w_out),
                (skip_gain_hbm, skip_gain),
            )
        )
    ]
    for load in loads:
        load.start()

    def send_all(src, dst, send_sem, recv_sem):
        for peer, coords in peers:
            pltpu.make_async_remote_copy(
                src_ref=src.at[peer],
                dst_ref=dst.at[me],
                send_sem=send_sem,
                recv_sem=recv_sem,
                device_id=coords,
                device_id_type=MESH,
            ).start()

        pltpu.make_async_copy(src.at[me], dst.at[me], recv_sem).start()

    def arrived(dst, recv_sem):
        pltpu.make_async_copy(dst, dst, recv_sem).wait()

    def sent(src, send_sem):
        most = src.at[pl.ds(0, blocks - 1)]
        pltpu.make_async_copy(most, most, send_sem).wait()

    for load in loads[:3]:
        load.wait()
    edge_out[0] = tokens[width - 16 :, :].astype(f32)[15:16]
    edge_out[1] = tokens[0:16, :].astype(f32)[0:1]
    filt_out[:, 0:mine, :] = (
        causal[...].astype(f32).T.astype(bf16).reshape(blocks, mine, width)
    )
    unused = (lax.broadcasted_iota(jnp.int32, anti.shape, 0) == 0) & (me == 0)
    filt_out[:, mine:, :] = (
        jnp.where(unused, 0.0, anti[...].astype(f32))
        .T.astype(bf16)
        .reshape(blocks, mine, width)
    )
    pl.semaphore_wait(barrier, blocks - 1)
    edges = [
        pltpu.make_async_remote_copy(
            src_ref=edge_out.at[i],
            dst_ref=edge_in.at[i],
            send_sem=edge_send.at[i],
            recv_sem=edge_recv.at[i],
            device_id=(at // groups, at % groups),
            device_id_type=MESH,
        )
        for i, at in enumerate(((me + 1) % blocks, (me + blocks - 1) % blocks))
    ]
    for edge in edges:
        edge.start()
    send_all(filt_out, filt_in, filt_send, filt_recv)

    for edge in edges:
        edge.wait()
    row16 = lax.broadcasted_iota(jnp.int32, (16, depth), 0)
    prev = jnp.where(me == 0, 0.0, edge_in[0])
    following = jnp.where(me == blocks - 1, 0.0, edge_in[1])
    framed[width:, :] = jnp.where(
        row16 == 0, prev, jnp.where(row16 == 1, following, 0.0)
    ).astype(bf16)

    for load in loads[3:5]:
        load.wait()
    row = lax.broadcasted_iota(jnp.int32, (width, channels), 0)

    def stream(part):
        cols = slice(part * channels, (part + 1) * channels)
        proj = dot32(framed[...], w_in[:, cols]).astype(bf16).astype(f32)
        here = proj[:width]
        before = jnp.where(row == 0, proj[width : width + 1], pltpu.roll(here, 1, 0))
        after = jnp.where(
            row == width - 1, proj[width + 1 : width + 2], pltpu.roll(here, width - 1, 0)
        )
        taps = conv_taps[:, cols]
        return taps[0:1] * before + taps[1:2] * here + taps[2:3] * after

    signal = stream(0) * stream(2)
    sig_out[...] = signal.T.astype(bf16).reshape(blocks, mine, width)
    send_all(sig_out, sig_in, sig_send, sig_recv)
    second = stream(1)

    for load in loads[5:9]:
        load.wait()
    within[0], within[1] = halves(within_whole[...])
    cos, sin = twist[0], twist[1]

    def lane(x, c):
        return x[:, c * width : (c + 1) * width]

    def twisted(real, imag):
        return [real * cos + imag * sin, imag * cos - real * sin]

    def along(x):
        high, low = halves(x)
        return dot32(high, within[0]) + dot32(low, within[0]) + dot32(high, within[1])

    def forward(grid, mats):
        both = dot32(mats, grid)
        freq = both[: 2 * blocks] + both[2 * blocks :]
        parts = []
        for c in range(mine):
            pair = twisted(lane(freq[:blocks], c), lane(freq[blocks:], c))
            parts.append(jnp.concatenate(pair, axis=1))
        return along(jnp.concatenate(parts, axis=0))

    arrived(filt_in, filt_recv)
    spread[...] = filt_in[...].astype(f32).reshape(2 * blocks * mine, width)
    grid = jnp.concatenate(
        [
            jnp.concatenate(
                [
                    spread[pl.ds(c, blocks, stride=2 * mine), :],
                    spread[pl.ds(mine + c, blocks, stride=2 * mine), :],
                ],
                axis=0,
            ).astype(bf16)
            for c in range(mine)
        ],
        axis=1,
    )
    spectrum[...] = forward(grid, across[...])

    arrived(sig_in, sig_recv)
    spread[0 : blocks * mine, :] = sig_in[...].astype(f32).reshape(blocks * mine, width)
    grid = jnp.concatenate(
        [spread[pl.ds(c, blocks, stride=mine), :].astype(bf16) for c in range(mine)], axis=1
    )
    sig = forward(grid, across[:, 0:blocks])
    s_real, s_imag = sig[:, :width], sig[:, width:]
    f_real, f_imag = spectrum[:, :width], spectrum[:, width:]
    product = jnp.concatenate(
        [s_real * f_real - s_imag * f_imag, -(s_real * f_imag + s_imag * f_real)], axis=1
    )
    turned = along(product)
    parts = []
    for c in range(mine):
        rows = turned[c * blocks : (c + 1) * blocks]
        parts.append(jnp.concatenate(twisted(rows[:, :width], rows[:, width:]), axis=0))
    high, low = halves(jnp.concatenate(parts, axis=1))
    both = dot32(back[...], high)
    conv = both[:blocks] + both[blocks:] + dot32(back[0:blocks, :], low)
    for c in range(mine):
        spread[pl.ds(c, blocks, stride=mine), :] = lane(conv, c)
    ret_out[...] = spread[0 : blocks * mine, :].astype(bf16).reshape(blocks, mine, width)
    send_all(ret_out, ret_in, ret_send, ret_recv)

    for load in loads[9:]:
        load.wait()
    direct = skip_gain[...] * signal
    arrived(ret_in, ret_recv)
    convolved = ret_in[...].astype(f32).reshape(channels, width).T + direct
    gated = (second * convolved).astype(bf16)
    out[...] = dot32(gated, w_out[...]).astype(bf16)
    sent(filt_out, filt_send)
    sent(sig_out, sig_send)
    sent(ret_out, ret_send)


def one_kernel(tokens, w_in, conv_taps, causal_taps, anticausal_taps, skip_gain, w_out):
    width, depth = tokens.shape
    channels = w_out.shape[0]
    groups = lax.axis_size("fft")
    blocks = lax.axis_size("blk") * groups
    mine = channels // blocks
    across, twist, within, back = grid_constants(blocks, width)
    f32, bf16 = jnp.float32, jnp.bfloat16
    vmem = pl.BlockSpec(memory_space=pltpu.VMEM)
    hbm = pl.BlockSpec(memory_space=pl.ANY)
    one = pltpu.SemaphoreType.DMA
    return pl.pallas_call(
        functools.partial(mixer_kernel, blocks, groups),
        out_shape=jax.ShapeDtypeStruct((width, w_out.shape[1]), bf16),
        in_specs=[hbm] * 11,
        out_specs=vmem,
        scratch_shapes=[
            pltpu.VMEM(causal_taps.shape, bf16),
            pltpu.VMEM(anticausal_taps.shape, bf16),
            pltpu.VMEM(conv_taps.shape, f32),
            pltpu.VMEM((1, channels), f32),
            pltpu.VMEM(across.shape, bf16),
            pltpu.VMEM(twist.shape, f32),
            pltpu.VMEM(back.shape, bf16),
            pltpu.VMEM(w_in.shape, bf16),
            pltpu.VMEM(w_out.shape, bf16),
            pltpu.VMEM(within.shape, f32),
            pltpu.VMEM((2,) + within.shape, bf16),
            pltpu.VMEM((width + 16, depth), bf16),
            pltpu.VMEM((2, 1, depth), f32),
            pltpu.VMEM((2, 1, depth), f32),
            pltpu.VMEM((blocks, 2 * mine, width), bf16),
            pltpu.VMEM((blocks, 2 * mine, width), bf16),
            pltpu.VMEM((blocks, mine, width), bf16),
            pltpu.VMEM((blocks, mine, width), bf16),
            pltpu.VMEM((blocks, mine, width), bf16),
            pltpu.VMEM((blocks, mine, width), bf16),
            pltpu.VMEM((2 * blocks * mine, width), f32),
            pltpu.VMEM((blocks * mine, 2 * width), f32),
            one((11,)),
            one((2,)),
            one((2,)),
            one,
            one,
            one,
            one,
            one,
            one,
        ],
        compiler_params=pltpu.CompilerParams(
            collective_id=0, has_side_effects=True, vmem_limit_bytes=63 * 2**20
        ),
    )(
        tokens,
        causal_taps,
        anticausal_taps,
        conv_taps,
        skip_gain[None, :],
        jnp.asarray(across),
        jnp.asarray(twist),
        jnp.asarray(back),
        w_in,
        w_out,
        jnp.asarray(within),
    )


def mixer(tokens, w_in, conv_taps, causal_taps, anticausal_taps, skip_gain, w_out):
    devices = lax.axis_size("blk") * lax.axis_size("fft")
    fits = tokens.shape[0] == 128 and w_out.shape[0] == 16 * devices
    chosen = one_kernel if fits else body
    return chosen(tokens, w_in, conv_taps, causal_taps, anticausal_taps, skip_gain, w_out)


def solution(mesh):
    in_specs = (
        P(("blk", "fft"), None),
        P(),
        P(),
        P(("blk", "fft"), None),
        P(("blk", "fft"), None),
        P(),
        P(),
    )
    out_specs = P(("blk", "fft"), None)
    return jax.shard_map(mixer, mesh=mesh, in_specs=in_specs, out_specs=out_specs, check_vma=False)
```

```python
import functools
import math

import jax
import jax.numpy as jnp
import ml_dtypes
import numpy as np
from jax import lax
from jax.experimental import pallas as pl
from jax.experimental.pallas import tpu as pltpu
from jax.sharding import PartitionSpec as P

MESH = pl.DeviceIdType.MESH


def with_halo(cells, sides, width):
    for axis, dim in sides:
        count = lax.axis_size(axis)
        ends = count - 1
        head = lax.slice_in_dim(cells, 0, width, axis=dim)
        tail = lax.slice_in_dim(cells, cells.shape[dim] - width, cells.shape[dim], axis=dim)
        cells = jnp.concatenate(
            [
                lax.ppermute(tail, axis, [(i, (i + 1) % count) for i in range(ends)]),
                cells,
                lax.ppermute(head, axis, [((i + 1) % count, i) for i in range(ends)]),
            ],
            axis=dim,
        )
    return cells


def shortened(x):

    def short(part):
        return part.astype(jnp.bfloat16) if part.dtype == jnp.float32 else part

    return jax.tree.map(short, x)


def log_count(count):
    return count.bit_length() - 1


def dft_matrix(count, sign, scale):
    grid = jnp.arange(count, dtype=jnp.int32)
    angle = (
        sign * 2.0 * math.pi * (grid[:, None] * grid[None, :] % count).astype(jnp.float32) / count
    )
    return (jnp.cos(angle) * scale, jnp.sin(angle) * scale)


def local_convolution(signal_cols, causal_cols, anti_cols):
    seq_len = signal_cols.shape[0]
    width = signal_cols.shape[1]
    length = 2 * seq_len
    rows_p = 2 ** (log_count(length) // 2)
    cols_q = length // rows_p
    high = lax.Precision.HIGHEST
    p_real, p_imag = dft_matrix(rows_p, -1.0, 1.0)
    q_real, q_imag = dft_matrix(cols_q, -1.0, 1.0)
    pp_real, pp_imag = dft_matrix(rows_p, 1.0, 1.0 / length)
    qp_real, qp_imag = dft_matrix(cols_q, 1.0, 1.0)
    k_grid = jnp.arange(rows_p, dtype=jnp.int32)
    n_grid = jnp.arange(cols_q, dtype=jnp.int32)
    tw_angle = (
        -2.0 * math.pi * (k_grid[:, None] * n_grid[None, :] % length).astype(jnp.float32) / length
    )
    tw_cos = jnp.cos(tw_angle)
    tw_sin = jnp.sin(tw_angle)

    def forward(grid_rows):
        half = grid_rows.shape[1]
        b_real = jnp.einsum("kp,cpq->ckq", p_real[:, :half], grid_rows, precision=high)
        b_imag = jnp.einsum("kp,cpq->ckq", p_imag[:, :half], grid_rows, precision=high)
        c_real = b_real * tw_cos - b_imag * tw_sin
        c_imag = b_real * tw_sin + b_imag * tw_cos
        x_real = jnp.einsum("ckq,qr->ckr", c_real, q_real, precision=high) - jnp.einsum(
            "ckq,qr->ckr", c_imag, q_imag, precision=high
        )
        x_imag = jnp.einsum("ckq,qr->ckr", c_real, q_imag, precision=high) + jnp.einsum(
            "ckq,qr->ckr", c_imag, q_real, precision=high
        )
        return (x_real, x_imag)

    sig_grid = signal_cols.T.reshape(width, rows_p // 2, cols_q)
    filt_grid = jnp.concatenate([causal_cols, anti_cols], axis=0).T.reshape(width, rows_p, cols_q)
    s_real, s_imag = forward(sig_grid)
    f_real, f_imag = forward(filt_grid)
    y_real = s_real * f_real - s_imag * f_imag
    y_imag = s_real * f_imag + s_imag * f_real
    d_real = jnp.einsum("ckq,qr->ckr", y_real, qp_real, precision=high) - jnp.einsum(
        "ckq,qr->ckr", y_imag, qp_imag, precision=high
    )
    d_imag = jnp.einsum("ckq,qr->ckr", y_real, qp_imag, precision=high) + jnp.einsum(
        "ckq,qr->ckr", y_imag, qp_real, precision=high
    )
    e_real = d_real * tw_cos + d_imag * tw_sin
    e_imag = d_imag * tw_cos - d_real * tw_sin
    half_rows = rows_p // 2
    out_grid = jnp.einsum("nk,ckq->cnq", pp_real[:half_rows], e_real, precision=high) - jnp.einsum(
        "nk,ckq->cnq", pp_imag[:half_rows], e_imag, precision=high
    )
    return out_grid.reshape(width, seq_len).T


def body(tokens, w_in, conv_taps, causal_taps, anticausal_taps, skip_gain, w_out):
    tok_rows = tokens.shape[0]
    channels = w_out.shape[0]
    groups = lax.axis_size("fft")
    blk_index = lax.axis_index("blk")
    fft_index = lax.axis_index("fft")
    device_index = blk_index * groups + fft_index
    position = device_index * tok_rows + jnp.arange(tok_rows, dtype=jnp.int32)
    proj = jnp.dot(tokens, w_in, preferred_element_type=jnp.float32).astype(jnp.bfloat16)
    framed = with_halo(proj, ((("blk", "fft"), 0),), 1).astype(jnp.float32)
    short = conv_taps[0] * framed[:-2] + conv_taps[1] * framed[1:-1] + conv_taps[2] * framed[2:]
    first = short[:, :channels]
    second = short[:, channels : 2 * channels]
    value_part = short[:, 2 * channels :]
    signal = first * value_part
    anticausal = jnp.where(position[:, None] > 0, anticausal_taps.astype(jnp.float32), 0.0)
    causal = causal_taps.astype(jnp.float32)
    moved = (
        lax.all_to_all(
            signal.astype(jnp.bfloat16), "fft", split_axis=1, concat_axis=0, tiled=True
        ).astype(signal.dtype),
        lax.all_to_all(
            causal.astype(jnp.bfloat16), "fft", split_axis=1, concat_axis=0, tiled=True
        ).astype(causal.dtype),
        lax.all_to_all(
            anticausal.astype(jnp.bfloat16), "fft", split_axis=1, concat_axis=0, tiled=True
        ).astype(anticausal.dtype),
    )
    moved = (
        lax.all_to_all(
            moved[0].astype(jnp.bfloat16), "blk", split_axis=1, concat_axis=0, tiled=True
        ).astype(jnp.float32),
        lax.all_to_all(
            moved[1].astype(jnp.bfloat16), "blk", split_axis=1, concat_axis=0, tiled=True
        ).astype(jnp.float32),
        lax.all_to_all(
            moved[2].astype(jnp.bfloat16), "blk", split_axis=1, concat_axis=0, tiled=True
        ).astype(jnp.float32),
    )
    conv_cols = local_convolution(moved[0], moved[1], moved[2])
    returned = lax.all_to_all(
        shortened(conv_cols), "blk", split_axis=0, concat_axis=1, tiled=True
    ).astype(conv_cols.dtype)
    convolved = lax.all_to_all(
        shortened(returned), "fft", split_axis=0, concat_axis=1, tiled=True
    ).astype(returned.dtype)
    convolved = convolved + skip_gain * signal
    gated = (second * convolved).astype(jnp.bfloat16)
    return jnp.dot(gated, w_out, preferred_element_type=jnp.float32).astype(jnp.bfloat16)


def grid_constants(blocks, width):
    length = 2 * blocks * width
    half_freq = np.arange(blocks) + 0.5

    def split(mat):
        high = mat.astype(ml_dtypes.bfloat16)
        low = (mat - high.astype(np.float64)).astype(ml_dtypes.bfloat16)
        return high, low

    rows = np.outer(half_freq, np.arange(2 * blocks)) * (2.0 * np.pi / (2 * blocks))
    flip = np.where(np.arange(2 * blocks) < blocks, 1.0, -1.0)
    across = np.concatenate([np.cos(rows), -np.sin(rows)], axis=0) * flip
    across = np.concatenate(split(across), axis=0)
    turn = np.outer(half_freq, np.arange(width)) * (2.0 * np.pi / length)
    twist = np.stack([np.cos(turn), np.sin(turn)]).astype(np.float32)
    grid = np.outer(np.arange(width), np.arange(width)) % width * (2.0 * np.pi / width)
    cos, sin = np.cos(grid), np.sin(grid)
    within = np.block([[cos, -sin], [sin, cos]]).astype(np.float32)
    back = rows[:, :blocks].T
    back = np.concatenate([np.cos(back), np.sin(back)], axis=1) * (2.0 / length)
    back = np.concatenate(split(back), axis=0)
    return across, twist, within, back


def dot32(a, b):
    return jnp.dot(a, b, preferred_element_type=jnp.float32)


def halves(x):
    high = x.astype(jnp.bfloat16)
    low = (x - high.astype(jnp.float32)).astype(jnp.bfloat16)
    return high, low


def mixer_kernel(
    blocks,
    groups,
    tokens_hbm,
    causal_hbm,
    anti_hbm,
    conv_taps_hbm,
    skip_gain_hbm,
    across_hbm,
    twist_hbm,
    back_hbm,
    w_in_hbm,
    w_out_hbm,
    within_hbm,
    out,
    causal,
    anti,
    conv_taps,
    skip_gain,
    across,
    twist,
    back,
    w_in,
    w_out,
    within_whole,
    within,
    framed,
    edge_out,
    edge_in,
    filt_out,
    filt_in,
    sig_out,
    sig_in,
    ret_out,
    ret_in,
    spread,
    spectrum,
    load_sem,
    edge_send,
    edge_recv,
    filt_send,
    filt_recv,
    sig_send,
    sig_recv,
    ret_send,
    ret_recv,
):
    f32, bf16 = jnp.float32, jnp.bfloat16
    width, depth = tokens_hbm.shape
    channels = w_out.shape[0]
    mine = channels // blocks
    tokens = framed.at[0:width]
    blk, fft = lax.axis_index("blk"), lax.axis_index("fft")
    me = blk * groups + fft
    levels = blocks // groups
    peers = []
    for turn in range(levels - 1, -1, -1):
        level = blk ^ turn
        for step in range(groups):
            if turn > 0 or step > 0:
                other = (fft + step) & (groups - 1)
                peers.append((level * groups + other, (level, other)))

    barrier = pltpu.get_barrier_semaphore()
    for _, coords in peers:
        pl.semaphore_signal(barrier, inc=1, device_id=coords, device_id_type=MESH)

    loads = [
        pltpu.make_async_copy(src, dst, load_sem.at[i])
        for i, (src, dst) in enumerate(
            (
                (causal_hbm, causal),
                (anti_hbm, anti),
                (tokens_hbm, tokens),
                (w_in_hbm, w_in),
                (conv_taps_hbm, conv_taps),
                (across_hbm, across),
                (twist_hbm, twist),
                (within_hbm, within_whole),
                (back_hbm, back),
                (w_out_hbm, w_out),
                (skip_gain_hbm, skip_gain),
            )
        )
    ]
    for load in loads:
        load.start()

    def send_all(src, dst, send_sem, recv_sem):
        for peer, coords in peers:
            pltpu.make_async_remote_copy(
                src_ref=src.at[peer],
                dst_ref=dst.at[me],
                send_sem=send_sem,
                recv_sem=recv_sem,
                device_id=coords,
                device_id_type=MESH,
            ).start()

        pltpu.make_async_copy(src.at[me], dst.at[me], recv_sem).start()

    def arrived(dst, recv_sem):
        pltpu.make_async_copy(dst, dst, recv_sem).wait()

    def sent(src, send_sem):
        most = src.at[pl.ds(0, blocks - 1)]
        pltpu.make_async_copy(most, most, send_sem).wait()

    for load in loads[:3]:
        load.wait()
    edge_out[0] = tokens[width - 16 :, :].astype(f32)[15:16]
    edge_out[1] = tokens[0:16, :].astype(f32)[0:1]
    filt_out[:, 0:mine, :] = (
        causal[...].astype(f32).T.astype(bf16).reshape(blocks, mine, width)
    )
    unused = (lax.broadcasted_iota(jnp.int32, anti.shape, 0) == 0) & (me == 0)
    filt_out[:, mine:, :] = (
        jnp.where(unused, 0.0, anti[...].astype(f32))
        .T.astype(bf16)
        .reshape(blocks, mine, width)
    )
    pl.semaphore_wait(barrier, blocks - 1)
    edges = [
        pltpu.make_async_remote_copy(
            src_ref=edge_out.at[i],
            dst_ref=edge_in.at[i],
            send_sem=edge_send.at[i],
            recv_sem=edge_recv.at[i],
            device_id=(at // groups, at % groups),
            device_id_type=MESH,
        )
        for i, at in enumerate(((me + 1) % blocks, (me + blocks - 1) % blocks))
    ]
    for edge in edges:
        edge.start()
    send_all(filt_out, filt_in, filt_send, filt_recv)

    for edge in edges:
        edge.wait()
    row16 = lax.broadcasted_iota(jnp.int32, (16, depth), 0)
    prev = jnp.where(me == 0, 0.0, edge_in[0])
    following = jnp.where(me == blocks - 1, 0.0, edge_in[1])
    framed[width:, :] = jnp.where(
        row16 == 0, prev, jnp.where(row16 == 1, following, 0.0)
    ).astype(bf16)

    for load in loads[3:5]:
        load.wait()
    row = lax.broadcasted_iota(jnp.int32, (width, channels), 0)

    def stream(part):
        cols = slice(part * channels, (part + 1) * channels)
        proj = dot32(framed[...], w_in[:, cols]).astype(bf16).astype(f32)
        here = proj[:width]
        before = jnp.where(row == 0, proj[width : width + 1], pltpu.roll(here, 1, 0))
        after = jnp.where(
            row == width - 1, proj[width + 1 : width + 2], pltpu.roll(here, width - 1, 0)
        )
        taps = conv_taps[:, cols]
        return taps[0:1] * before + taps[1:2] * here + taps[2:3] * after

    signal = stream(0) * stream(2)
    sig_out[...] = signal.T.astype(bf16).reshape(blocks, mine, width)
    send_all(sig_out, sig_in, sig_send, sig_recv)
    second = stream(1)

    for load in loads[5:9]:
        load.wait()
    within[0] = within_whole[...].astype(bf16)
    cos, sin = twist[0], twist[1]

    def lane(x, c):
        return x[:, c * width : (c + 1) * width]

    def twisted(real, imag):
        return [real * cos + imag * sin, imag * cos - real * sin]

    def along(x):
        return dot32(x.astype(bf16), within[0])

    def forward(grid, mats):
        freq = dot32(mats[: 2 * blocks], grid)
        parts = []
        for c in range(mine):
            pair = twisted(lane(freq[:blocks], c), lane(freq[blocks:], c))
            parts.append(jnp.concatenate(pair, axis=1))
        return along(jnp.concatenate(parts, axis=0))

    arrived(filt_in, filt_recv)
    spread[...] = filt_in[...].astype(f32).reshape(2 * blocks * mine, width)
    grid = jnp.concatenate(
        [
            jnp.concatenate(
                [
                    spread[pl.ds(c, blocks, stride=2 * mine), :],
                    spread[pl.ds(mine + c, blocks, stride=2 * mine), :],
                ],
                axis=0,
            ).astype(bf16)
            for c in range(mine)
        ],
        axis=1,
    )
    spectrum[...] = forward(grid, across[...])

    arrived(sig_in, sig_recv)
    spread[0 : blocks * mine, :] = sig_in[...].astype(f32).reshape(blocks * mine, width)
    grid = jnp.concatenate(
        [spread[pl.ds(c, blocks, stride=mine), :].astype(bf16) for c in range(mine)], axis=1
    )
    sig = forward(grid, across[:, 0:blocks])
    s_real, s_imag = sig[:, :width], sig[:, width:]
    f_real, f_imag = spectrum[:, :width], spectrum[:, width:]
    product = jnp.concatenate(
        [s_real * f_real - s_imag * f_imag, -(s_real * f_imag + s_imag * f_real)], axis=1
    )
    turned = along(product)
    parts = []
    for c in range(mine):
        rows = turned[c * blocks : (c + 1) * blocks]
        parts.append(jnp.concatenate(twisted(rows[:, :width], rows[:, width:]), axis=0))
    conv = dot32(back[0:blocks, :], jnp.concatenate(parts, axis=1).astype(bf16))
    for c in range(mine):
        spread[pl.ds(c, blocks, stride=mine), :] = lane(conv, c)
    ret_out[...] = spread[0 : blocks * mine, :].astype(bf16).reshape(blocks, mine, width)
    send_all(ret_out, ret_in, ret_send, ret_recv)

    for load in loads[9:]:
        load.wait()
    direct = skip_gain[...] * signal
    arrived(ret_in, ret_recv)
    convolved = ret_in[...].astype(f32).reshape(channels, width).T + direct
    gated = (second * convolved).astype(bf16)
    out[...] = dot32(gated, w_out[...]).astype(bf16)
    sent(filt_out, filt_send)
    sent(sig_out, sig_send)
    sent(ret_out, ret_send)


def one_kernel(tokens, w_in, conv_taps, causal_taps, anticausal_taps, skip_gain, w_out):
    width, depth = tokens.shape
    channels = w_out.shape[0]
    groups = lax.axis_size("fft")
    blocks = lax.axis_size("blk") * groups
    mine = channels // blocks
    across, twist, within, back = grid_constants(blocks, width)
    f32, bf16 = jnp.float32, jnp.bfloat16
    vmem = pl.BlockSpec(memory_space=pltpu.VMEM)
    hbm = pl.BlockSpec(memory_space=pl.ANY)
    one = pltpu.SemaphoreType.DMA
    return pl.pallas_call(
        functools.partial(mixer_kernel, blocks, groups),
        out_shape=pltpu.VMEM((width, w_out.shape[1]), bf16),
        in_specs=[hbm] * 11,
        out_specs=vmem,
        scratch_shapes=[
            pltpu.VMEM(causal_taps.shape, bf16),
            pltpu.VMEM(anticausal_taps.shape, bf16),
            pltpu.VMEM(conv_taps.shape, f32),
            pltpu.VMEM((1, channels), f32),
            pltpu.VMEM(across.shape, bf16),
            pltpu.VMEM(twist.shape, f32),
            pltpu.VMEM(back.shape, bf16),
            pltpu.VMEM(w_in.shape, bf16),
            pltpu.VMEM(w_out.shape, bf16),
            pltpu.VMEM(within.shape, f32),
            pltpu.VMEM((2,) + within.shape, bf16),
            pltpu.VMEM((width + 16, depth), bf16),
            pltpu.VMEM((2, 1, depth), f32),
            pltpu.VMEM((2, 1, depth), f32),
            pltpu.VMEM((blocks, 2 * mine, width), bf16),
            pltpu.VMEM((blocks, 2 * mine, width), bf16),
            pltpu.VMEM((blocks, mine, width), bf16),
            pltpu.VMEM((blocks, mine, width), bf16),
            pltpu.VMEM((blocks, mine, width), bf16),
            pltpu.VMEM((blocks, mine, width), bf16),
            pltpu.VMEM((2 * blocks * mine, width), f32),
            pltpu.VMEM((blocks * mine, 2 * width), f32),
            one((11,)),
            one((2,)),
            one((2,)),
            one,
            one,
            one,
            one,
            one,
            one,
        ],
        compiler_params=pltpu.CompilerParams(
            collective_id=0, has_side_effects=True, vmem_limit_bytes=62 * 2**20
        ),
    )(
        tokens,
        causal_taps,
        anticausal_taps,
        conv_taps,
        skip_gain[None, :],
        jnp.asarray(across),
        jnp.asarray(twist),
        jnp.asarray(back),
        w_in,
        w_out,
        jnp.asarray(within),
    )


def mixer(tokens, w_in, conv_taps, causal_taps, anticausal_taps, skip_gain, w_out):
    devices = lax.axis_size("blk") * lax.axis_size("fft")
    fits = tokens.shape[0] == 128 and w_out.shape[0] == 16 * devices
    chosen = one_kernel if fits else body
    return chosen(tokens, w_in, conv_taps, causal_taps, anticausal_taps, skip_gain, w_out)


def solution(mesh):
    in_specs = (
        P(("blk", "fft"), None),
        P(),
        P(),
        P(("blk", "fft"), None),
        P(("blk", "fft"), None),
        P(),
        P(),
    )
    out_specs = P(("blk", "fft"), None)
    return jax.shard_map(mixer, mesh=mesh, in_specs=in_specs, out_specs=out_specs, check_vma=False)
```

```python
import functools
import math

import jax
import jax.numpy as jnp
import ml_dtypes
import numpy as np
from jax import lax
from jax.experimental import pallas as pl
from jax.experimental.pallas import tpu as pltpu
from jax.sharding import PartitionSpec as P

MESH = pl.DeviceIdType.MESH


def with_halo(cells, sides, width):
    for axis, dim in sides:
        count = lax.axis_size(axis)
        ends = count - 1
        head = lax.slice_in_dim(cells, 0, width, axis=dim)
        tail = lax.slice_in_dim(cells, cells.shape[dim] - width, cells.shape[dim], axis=dim)
        cells = jnp.concatenate(
            [
                lax.ppermute(tail, axis, [(i, (i + 1) % count) for i in range(ends)]),
                cells,
                lax.ppermute(head, axis, [((i + 1) % count, i) for i in range(ends)]),
            ],
            axis=dim,
        )
    return cells


def shortened(x):

    def short(part):
        return part.astype(jnp.bfloat16) if part.dtype == jnp.float32 else part

    return jax.tree.map(short, x)


def log_count(count):
    return count.bit_length() - 1


def dft_matrix(count, sign, scale):
    grid = jnp.arange(count, dtype=jnp.int32)
    angle = (
        sign * 2.0 * math.pi * (grid[:, None] * grid[None, :] % count).astype(jnp.float32) / count
    )
    return (jnp.cos(angle) * scale, jnp.sin(angle) * scale)


def local_convolution(signal_cols, causal_cols, anti_cols):
    seq_len = signal_cols.shape[0]
    width = signal_cols.shape[1]
    length = 2 * seq_len
    rows_p = 2 ** (log_count(length) // 2)
    cols_q = length // rows_p
    high = lax.Precision.HIGHEST
    p_real, p_imag = dft_matrix(rows_p, -1.0, 1.0)
    q_real, q_imag = dft_matrix(cols_q, -1.0, 1.0)
    pp_real, pp_imag = dft_matrix(rows_p, 1.0, 1.0 / length)
    qp_real, qp_imag = dft_matrix(cols_q, 1.0, 1.0)
    k_grid = jnp.arange(rows_p, dtype=jnp.int32)
    n_grid = jnp.arange(cols_q, dtype=jnp.int32)
    tw_angle = (
        -2.0 * math.pi * (k_grid[:, None] * n_grid[None, :] % length).astype(jnp.float32) / length
    )
    tw_cos = jnp.cos(tw_angle)
    tw_sin = jnp.sin(tw_angle)

    def forward(grid_rows):
        half = grid_rows.shape[1]
        b_real = jnp.einsum("kp,cpq->ckq", p_real[:, :half], grid_rows, precision=high)
        b_imag = jnp.einsum("kp,cpq->ckq", p_imag[:, :half], grid_rows, precision=high)
        c_real = b_real * tw_cos - b_imag * tw_sin
        c_imag = b_real * tw_sin + b_imag * tw_cos
        x_real = jnp.einsum("ckq,qr->ckr", c_real, q_real, precision=high) - jnp.einsum(
            "ckq,qr->ckr", c_imag, q_imag, precision=high
        )
        x_imag = jnp.einsum("ckq,qr->ckr", c_real, q_imag, precision=high) + jnp.einsum(
            "ckq,qr->ckr", c_imag, q_real, precision=high
        )
        return (x_real, x_imag)

    sig_grid = signal_cols.T.reshape(width, rows_p // 2, cols_q)
    filt_grid = jnp.concatenate([causal_cols, anti_cols], axis=0).T.reshape(width, rows_p, cols_q)
    s_real, s_imag = forward(sig_grid)
    f_real, f_imag = forward(filt_grid)
    y_real = s_real * f_real - s_imag * f_imag
    y_imag = s_real * f_imag + s_imag * f_real
    d_real = jnp.einsum("ckq,qr->ckr", y_real, qp_real, precision=high) - jnp.einsum(
        "ckq,qr->ckr", y_imag, qp_imag, precision=high
    )
    d_imag = jnp.einsum("ckq,qr->ckr", y_real, qp_imag, precision=high) + jnp.einsum(
        "ckq,qr->ckr", y_imag, qp_real, precision=high
    )
    e_real = d_real * tw_cos + d_imag * tw_sin
    e_imag = d_imag * tw_cos - d_real * tw_sin
    half_rows = rows_p // 2
    out_grid = jnp.einsum("nk,ckq->cnq", pp_real[:half_rows], e_real, precision=high) - jnp.einsum(
        "nk,ckq->cnq", pp_imag[:half_rows], e_imag, precision=high
    )
    return out_grid.reshape(width, seq_len).T


def body(tokens, w_in, conv_taps, causal_taps, anticausal_taps, skip_gain, w_out):
    tok_rows = tokens.shape[0]
    channels = w_out.shape[0]
    groups = lax.axis_size("fft")
    blk_index = lax.axis_index("blk")
    fft_index = lax.axis_index("fft")
    device_index = blk_index * groups + fft_index
    position = device_index * tok_rows + jnp.arange(tok_rows, dtype=jnp.int32)
    proj = jnp.dot(tokens, w_in, preferred_element_type=jnp.float32).astype(jnp.bfloat16)
    framed = with_halo(proj, ((("blk", "fft"), 0),), 1).astype(jnp.float32)
    short = conv_taps[0] * framed[:-2] + conv_taps[1] * framed[1:-1] + conv_taps[2] * framed[2:]
    first = short[:, :channels]
    second = short[:, channels : 2 * channels]
    value_part = short[:, 2 * channels :]
    signal = first * value_part
    anticausal = jnp.where(position[:, None] > 0, anticausal_taps.astype(jnp.float32), 0.0)
    causal = causal_taps.astype(jnp.float32)
    moved = (
        lax.all_to_all(
            signal.astype(jnp.bfloat16), "fft", split_axis=1, concat_axis=0, tiled=True
        ).astype(signal.dtype),
        lax.all_to_all(
            causal.astype(jnp.bfloat16), "fft", split_axis=1, concat_axis=0, tiled=True
        ).astype(causal.dtype),
        lax.all_to_all(
            anticausal.astype(jnp.bfloat16), "fft", split_axis=1, concat_axis=0, tiled=True
        ).astype(anticausal.dtype),
    )
    moved = (
        lax.all_to_all(
            moved[0].astype(jnp.bfloat16), "blk", split_axis=1, concat_axis=0, tiled=True
        ).astype(jnp.float32),
        lax.all_to_all(
            moved[1].astype(jnp.bfloat16), "blk", split_axis=1, concat_axis=0, tiled=True
        ).astype(jnp.float32),
        lax.all_to_all(
            moved[2].astype(jnp.bfloat16), "blk", split_axis=1, concat_axis=0, tiled=True
        ).astype(jnp.float32),
    )
    conv_cols = local_convolution(moved[0], moved[1], moved[2])
    returned = lax.all_to_all(
        shortened(conv_cols), "blk", split_axis=0, concat_axis=1, tiled=True
    ).astype(conv_cols.dtype)
    convolved = lax.all_to_all(
        shortened(returned), "fft", split_axis=0, concat_axis=1, tiled=True
    ).astype(returned.dtype)
    convolved = convolved + skip_gain * signal
    gated = (second * convolved).astype(jnp.bfloat16)
    return jnp.dot(gated, w_out, preferred_element_type=jnp.float32).astype(jnp.bfloat16)


def grid_constants(blocks, width):
    length = 2 * blocks * width
    half_freq = np.arange(blocks) + 0.5

    rows = np.outer(half_freq, np.arange(2 * blocks)) * (2.0 * np.pi / (2 * blocks))
    flip = np.where(np.arange(2 * blocks) < blocks, 1.0, -1.0)
    across = np.concatenate([np.cos(rows), -np.sin(rows)], axis=0) * flip
    across = across.astype(ml_dtypes.bfloat16)
    turn = np.outer(half_freq, np.arange(width)) * (2.0 * np.pi / length)
    twist = np.stack([np.cos(turn), np.sin(turn)]).astype(np.float32)
    grid = np.outer(np.arange(width), np.arange(width)) % width * (2.0 * np.pi / width)
    cos, sin = np.cos(grid), np.sin(grid)
    within = np.block([[cos, -sin], [sin, cos]]).astype(np.float32)
    back = rows[:, :blocks].T
    back = np.concatenate([np.cos(back), np.sin(back)], axis=1) * (2.0 / length)
    back = back.astype(ml_dtypes.bfloat16)
    return across, twist, within, back


def dot32(a, b):
    return jnp.dot(a, b, preferred_element_type=jnp.float32)


def mixer_kernel(
    blocks,
    groups,
    tokens_hbm,
    causal_hbm,
    anti_hbm,
    conv_taps_hbm,
    skip_gain_hbm,
    across_hbm,
    twist_hbm,
    back_hbm,
    w_in_hbm,
    w_out_hbm,
    within_hbm,
    out,
    causal,
    anti,
    conv_taps,
    skip_gain,
    across,
    twist,
    back,
    w_in,
    w_out,
    within_whole,
    within,
    framed,
    edge_out,
    edge_in,
    filt_out,
    filt_in,
    sig_out,
    sig_in,
    ret_out,
    ret_in,
    spread,
    gather,
    result,
    spectrum,
    gate,
    passed,
    gated,
    load_sem,
    edge_send,
    edge_recv,
    filt_send,
    filt_recv,
    sig_send,
    sig_recv,
    ret_send,
    ret_recv,
):
    f32, bf16 = jnp.float32, jnp.bfloat16
    width, depth = tokens_hbm.shape
    channels = w_out.shape[0]
    parts, _, some, _ = sig_out.shape
    tokens = framed.at[0:width]
    blk, fft = lax.axis_index("blk"), lax.axis_index("fft")
    me = blk * groups + fft
    levels = blocks // groups
    peers = []
    for turn in range(levels - 1, -1, -1):
        level = blk ^ turn
        for step in range(groups):
            if turn > 0 or step > 0:
                other = (fft + step) & (groups - 1)
                peers.append((turn, level * groups + other, (level, other)))

    barrier = pltpu.get_barrier_semaphore()
    for _, _, coords in peers:
        pl.semaphore_signal(barrier, inc=1, device_id=coords, device_id_type=MESH)

    loads = [
        pltpu.make_async_copy(src, dst, load_sem.at[i])
        for i, (src, dst) in enumerate(
            (
                (causal_hbm, causal),
                (anti_hbm, anti),
                (tokens_hbm, tokens),
                (w_in_hbm, w_in),
                (conv_taps_hbm, conv_taps),
                (across_hbm, across),
                (twist_hbm, twist),
                (within_hbm, within_whole),
                (back_hbm, back),
                (w_out_hbm, w_out),
                (skip_gain_hbm, skip_gain),
            )
        )
    ]
    for load in loads:
        load.start()

    def send_all(src, dst, send_sem, recv_sem):
        for turn, peer, coords in peers:
            pltpu.make_async_remote_copy(
                src_ref=src.at[peer],
                dst_ref=dst.at[me],
                send_sem=send_sem,
                recv_sem=recv_sem.at[turn],
                device_id=coords,
                device_id_type=MESH,
            ).start()
        pltpu.make_async_copy(src.at[me], dst.at[me], recv_sem.at[0]).start()

    def plane_of(dst, turn):
        return dst.at[pl.ds((blk ^ turn) * groups, groups)]

    def arrived(dst, recv_sem, turn):
        plane = plane_of(dst, turn)
        pltpu.make_async_copy(plane, plane, recv_sem.at[turn]).wait()

    def all_arrived(dst, recv_sem):
        for turn in range(levels):
            arrived(dst, recv_sem, turn)

    def sent(src, send_sem):
        most = src.at[pl.ds(0, blocks - 1)]
        pltpu.make_async_copy(most, most, send_sem).wait()

    def chunks(x):
        return x.T.reshape(blocks, parts, some, width)

    for load in loads[:3]:
        load.wait()
    edge_out[0] = tokens[width - 16 :, :].astype(f32)[15:16]
    edge_out[1] = tokens[0:16, :].astype(f32)[0:1]
    unused = (lax.broadcasted_iota(jnp.int32, anti.shape, 0) == 0) & (me == 0)
    causal_rows = chunks(causal[...].astype(f32))
    anti_rows = chunks(jnp.where(unused, 0.0, anti[...].astype(f32)))
    for part in range(parts):
        filt_out[part, :, 0:some, :] = causal_rows[:, part].astype(bf16)
        filt_out[part, :, some:, :] = anti_rows[:, part].astype(bf16)
    pl.semaphore_wait(barrier, blocks - 1)
    edges = [
        pltpu.make_async_remote_copy(
            src_ref=edge_out.at[i],
            dst_ref=edge_in.at[i],
            send_sem=edge_send.at[i],
            recv_sem=edge_recv.at[i],
            device_id=(at // groups, at % groups),
            device_id_type=MESH,
        )
        for i, at in enumerate(((me + 1) % blocks, (me + blocks - 1) % blocks))
    ]
    for edge in edges:
        edge.start()

    def send_part(bufs, part):
        src, dst, send_sem, recv_sem = bufs
        send_all(src.at[part], dst.at[part], send_sem.at[part], recv_sem.at[part])

    filt = (filt_out, filt_in, filt_send, filt_recv)
    sig = (sig_out, sig_in, sig_send, sig_recv)
    ret = (ret_out, ret_in, ret_send, ret_recv)
    send_part(filt, 0)

    for load in loads[3:5]:
        load.wait()
    for edge in edges:
        edge.wait()
    row16 = lax.broadcasted_iota(jnp.int32, (16, depth), 0)
    prev = jnp.where(me == 0, 0.0, edge_in[0])
    following = jnp.where(me == blocks - 1, 0.0, edge_in[1])
    framed[width:, :] = jnp.where(
        row16 == 0, prev, jnp.where(row16 == 1, following, 0.0)
    ).astype(bf16)
    row = lax.broadcasted_iota(jnp.int32, (width, channels), 0)

    def stream(which):
        cols = slice(which * channels, (which + 1) * channels)
        proj = dot32(framed[...], w_in[:, cols]).astype(bf16).astype(f32)
        here = proj[:width]
        before = jnp.where(row == 0, proj[width : width + 1], pltpu.roll(here, 1, 0))
        after = jnp.where(
            row == width - 1, proj[width + 1 : width + 2], pltpu.roll(here, width - 1, 0)
        )
        taps = conv_taps[:, cols]
        return taps[0:1] * before + taps[1:2] * here + taps[2:3] * after

    signal = stream(0) * stream(2)
    signal_rows = chunks(signal)
    for part in range(parts):
        sig_out[part] = signal_rows[:, part].astype(bf16)
        send_part(sig, part)
        if part + 1 < parts:
            send_part(filt, part + 1)

    for load in loads[5:]:
        load.wait()
    second = stream(1)
    direct = second * (skip_gain[...] * signal)
    span = channels // levels
    for level in range(levels):
        gate[level] = second[:, level * span : (level + 1) * span]
        passed[level] = direct[:, level * span : (level + 1) * span]
    within[...] = within_whole[...].astype(bf16)
    cos, sin = twist[0], twist[1]

    def twisted(real, imag, axis):
        return jnp.concatenate([real * cos + imag * sin, imag * cos - real * sin], axis=axis)

    def lane(x, c):
        return x[:, c * width : (c + 1) * width]

    def forward(columns, mats):
        freq = dot32(mats, jnp.concatenate(columns, axis=1))
        turned = [
            twisted(lane(freq[:blocks], c), lane(freq[blocks:], c), 1)
            for c in range(len(columns))
        ]
        return dot32(jnp.concatenate(turned, axis=0).astype(bf16), within[...])

    few = 4
    sets = [list(range(c, c + few)) for c in range(0, some, few)]
    for part in range(parts):
        all_arrived(filt_in.at[part], filt_recv.at[part])
        spread[...] = filt_in[part].astype(f32).reshape(2 * blocks * some, width)
        for n, members in enumerate(sets):
            columns = [
                jnp.concatenate(
                    [
                        spread[pl.ds(c, blocks, stride=2 * some), :],
                        spread[pl.ds(some + c, blocks, stride=2 * some), :],
                    ],
                    axis=0,
                ).astype(bf16)
                for c in members
            ]
            spectrum[n] = forward(columns, across[...])

        all_arrived(sig_in.at[part], sig_recv.at[part])
        gather[...] = sig_in[part].astype(f32).reshape(blocks * some, width)
        for n, members in enumerate(sets):
            columns = [
                gather[pl.ds(c, blocks, stride=some), :].astype(bf16) for c in members
            ]
            freq = forward(columns, across[:, 0:blocks])
            s_real, s_imag = freq[:, :width], freq[:, width:]
            f_real, f_imag = spectrum[n, :, :width], spectrum[n, :, width:]
            product = jnp.concatenate(
                [s_real * f_real - s_imag * f_imag, -(s_real * f_imag + s_imag * f_real)],
                axis=1,
            )
            turned = dot32(product.astype(bf16), within[...])
            pieces = [turned[i * blocks : (i + 1) * blocks] for i in range(few)]
            pieces = [twisted(x[:, :width], x[:, width:], 0) for x in pieces]
            conv = dot32(back[...], jnp.concatenate(pieces, axis=1).astype(bf16))
            for i, c in enumerate(members):
                result[pl.ds(c, blocks, stride=some), :] = lane(conv, i)
        ret_out[part] = result[...].astype(bf16).reshape(blocks, some, width)
        send_part(ret, part)

    for turn in range(levels):
        level = blk ^ turn
        for part in range(parts):
            arrived(ret_in.at[part], ret_recv.at[part], turn)
        landed = [plane_of(ret_in.at[part], turn)[...].astype(f32) for part in range(parts)]
        landed = jnp.concatenate(landed, axis=1).reshape(span, width).T
        cols = pl.ds(pl.multiple_of(level * span, span), span)
        gated[:, cols] = (gate[level] * landed + passed[level]).astype(bf16)
    out[...] = dot32(gated[...], w_out[...]).astype(bf16)
    for src, _, send_sem, _ in (filt, sig, ret):
        for part in range(parts):
            sent(src.at[part], send_sem.at[part])


def one_kernel(tokens, w_in, conv_taps, causal_taps, anticausal_taps, skip_gain, w_out):
    width, depth = tokens.shape
    channels = w_out.shape[0]
    groups = lax.axis_size("fft")
    blocks = lax.axis_size("blk") * groups
    levels = lax.axis_size("blk")
    parts = 1
    some = channels // blocks // parts
    across, twist, within, back = grid_constants(blocks, width)
    f32, bf16 = jnp.float32, jnp.bfloat16
    vmem = pl.BlockSpec(memory_space=pltpu.VMEM)
    hbm = pl.BlockSpec(memory_space=pl.ANY)
    one = pltpu.SemaphoreType.DMA
    return pl.pallas_call(
        functools.partial(mixer_kernel, blocks, groups),
        out_shape=pltpu.VMEM((width, w_out.shape[1]), bf16),
        in_specs=[hbm] * 11,
        out_specs=vmem,
        scratch_shapes=[
            pltpu.VMEM(causal_taps.shape, bf16),
            pltpu.VMEM(anticausal_taps.shape, bf16),
            pltpu.VMEM(conv_taps.shape, f32),
            pltpu.VMEM((1, channels), f32),
            pltpu.VMEM(across.shape, bf16),
            pltpu.VMEM(twist.shape, f32),
            pltpu.VMEM(back.shape, bf16),
            pltpu.VMEM(w_in.shape, bf16),
            pltpu.VMEM(w_out.shape, bf16),
            pltpu.VMEM(within.shape, f32),
            pltpu.VMEM(within.shape, bf16),
            pltpu.VMEM((width + 16, depth), bf16),
            pltpu.VMEM((2, 1, depth), f32),
            pltpu.VMEM((2, 1, depth), f32),
            pltpu.VMEM((parts, blocks, 2 * some, width), bf16),
            pltpu.VMEM((parts, blocks, 2 * some, width), bf16),
            pltpu.VMEM((parts, blocks, some, width), bf16),
            pltpu.VMEM((parts, blocks, some, width), bf16),
            pltpu.VMEM((parts, blocks, some, width), bf16),
            pltpu.VMEM((parts, blocks, some, width), bf16),
            pltpu.VMEM((2 * blocks * some, width), f32),
            pltpu.VMEM((blocks * some, width), f32),
            pltpu.VMEM((blocks * some, width), f32),
            pltpu.VMEM((some // 4, 4 * blocks, 2 * width), f32),
            pltpu.VMEM((levels, width, channels // levels), f32),
            pltpu.VMEM((levels, width, channels // levels), f32),
            pltpu.VMEM((width, channels), bf16),
            one((11,)),
            one((2,)),
            one((2,)),
            one((parts,)),
            one((parts, levels)),
            one((parts,)),
            one((parts, levels)),
            one((parts,)),
            one((parts, levels)),
        ],
        compiler_params=pltpu.CompilerParams(
            collective_id=0, has_side_effects=True, vmem_limit_bytes=62 * 2**20
        ),
    )(
        tokens,
        causal_taps,
        anticausal_taps,
        conv_taps,
        skip_gain[None, :],
        jnp.asarray(across),
        jnp.asarray(twist),
        jnp.asarray(back),
        w_in,
        w_out,
        jnp.asarray(within),
    )


def mixer(tokens, w_in, conv_taps, causal_taps, anticausal_taps, skip_gain, w_out):
    devices = lax.axis_size("blk") * lax.axis_size("fft")
    fits = tokens.shape[0] == 128 and w_out.shape[0] == 16 * devices
    chosen = one_kernel if fits else body
    return chosen(tokens, w_in, conv_taps, causal_taps, anticausal_taps, skip_gain, w_out)


def solution(mesh):
    in_specs = (
        P(("blk", "fft"), None),
        P(),
        P(),
        P(("blk", "fft"), None),
        P(("blk", "fft"), None),
        P(),
        P(),
    )
    out_specs = P(("blk", "fft"), None)
    return jax.shard_map(mixer, mesh=mesh, in_specs=in_specs, out_specs=out_specs, check_vma=False)
```

```python
import functools
import math

import jax
import jax.numpy as jnp
import ml_dtypes
import numpy as np
from jax import lax
from jax.experimental import pallas as pl
from jax.experimental.pallas import tpu as pltpu
from jax.sharding import PartitionSpec as P

MESH = pl.DeviceIdType.MESH


def with_halo(cells, sides, width):
    for axis, dim in sides:
        count = lax.axis_size(axis)
        ends = count - 1
        head = lax.slice_in_dim(cells, 0, width, axis=dim)
        tail = lax.slice_in_dim(cells, cells.shape[dim] - width, cells.shape[dim], axis=dim)
        cells = jnp.concatenate(
            [
                lax.ppermute(tail, axis, [(i, (i + 1) % count) for i in range(ends)]),
                cells,
                lax.ppermute(head, axis, [((i + 1) % count, i) for i in range(ends)]),
            ],
            axis=dim,
        )
    return cells


def shortened(x):

    def short(part):
        return part.astype(jnp.bfloat16) if part.dtype == jnp.float32 else part

    return jax.tree.map(short, x)


def log_count(count):
    return count.bit_length() - 1


def dft_matrix(count, sign, scale):
    grid = jnp.arange(count, dtype=jnp.int32)
    angle = (
        sign * 2.0 * math.pi * (grid[:, None] * grid[None, :] % count).astype(jnp.float32) / count
    )
    return (jnp.cos(angle) * scale, jnp.sin(angle) * scale)


def local_convolution(signal_cols, causal_cols, anti_cols):
    seq_len = signal_cols.shape[0]
    width = signal_cols.shape[1]
    length = 2 * seq_len
    rows_p = 2 ** (log_count(length) // 2)
    cols_q = length // rows_p
    high = lax.Precision.HIGHEST
    p_real, p_imag = dft_matrix(rows_p, -1.0, 1.0)
    q_real, q_imag = dft_matrix(cols_q, -1.0, 1.0)
    pp_real, pp_imag = dft_matrix(rows_p, 1.0, 1.0 / length)
    qp_real, qp_imag = dft_matrix(cols_q, 1.0, 1.0)
    k_grid = jnp.arange(rows_p, dtype=jnp.int32)
    n_grid = jnp.arange(cols_q, dtype=jnp.int32)
    tw_angle = (
        -2.0 * math.pi * (k_grid[:, None] * n_grid[None, :] % length).astype(jnp.float32) / length
    )
    tw_cos = jnp.cos(tw_angle)
    tw_sin = jnp.sin(tw_angle)

    def forward(grid_rows):
        half = grid_rows.shape[1]
        b_real = jnp.einsum("kp,cpq->ckq", p_real[:, :half], grid_rows, precision=high)
        b_imag = jnp.einsum("kp,cpq->ckq", p_imag[:, :half], grid_rows, precision=high)
        c_real = b_real * tw_cos - b_imag * tw_sin
        c_imag = b_real * tw_sin + b_imag * tw_cos
        x_real = jnp.einsum("ckq,qr->ckr", c_real, q_real, precision=high) - jnp.einsum(
            "ckq,qr->ckr", c_imag, q_imag, precision=high
        )
        x_imag = jnp.einsum("ckq,qr->ckr", c_real, q_imag, precision=high) + jnp.einsum(
            "ckq,qr->ckr", c_imag, q_real, precision=high
        )
        return (x_real, x_imag)

    sig_grid = signal_cols.T.reshape(width, rows_p // 2, cols_q)
    filt_grid = jnp.concatenate([causal_cols, anti_cols], axis=0).T.reshape(width, rows_p, cols_q)
    s_real, s_imag = forward(sig_grid)
    f_real, f_imag = forward(filt_grid)
    y_real = s_real * f_real - s_imag * f_imag
    y_imag = s_real * f_imag + s_imag * f_real
    d_real = jnp.einsum("ckq,qr->ckr", y_real, qp_real, precision=high) - jnp.einsum(
        "ckq,qr->ckr", y_imag, qp_imag, precision=high
    )
    d_imag = jnp.einsum("ckq,qr->ckr", y_real, qp_imag, precision=high) + jnp.einsum(
        "ckq,qr->ckr", y_imag, qp_real, precision=high
    )
    e_real = d_real * tw_cos + d_imag * tw_sin
    e_imag = d_imag * tw_cos - d_real * tw_sin
    half_rows = rows_p // 2
    out_grid = jnp.einsum("nk,ckq->cnq", pp_real[:half_rows], e_real, precision=high) - jnp.einsum(
        "nk,ckq->cnq", pp_imag[:half_rows], e_imag, precision=high
    )
    return out_grid.reshape(width, seq_len).T


def body(tokens, w_in, conv_taps, causal_taps, anticausal_taps, skip_gain, w_out):
    tok_rows = tokens.shape[0]
    channels = w_out.shape[0]
    groups = lax.axis_size("fft")
    blk_index = lax.axis_index("blk")
    fft_index = lax.axis_index("fft")
    device_index = blk_index * groups + fft_index
    position = device_index * tok_rows + jnp.arange(tok_rows, dtype=jnp.int32)
    proj = jnp.dot(tokens, w_in, preferred_element_type=jnp.float32).astype(jnp.bfloat16)
    framed = with_halo(proj, ((("blk", "fft"), 0),), 1).astype(jnp.float32)
    short = conv_taps[0] * framed[:-2] + conv_taps[1] * framed[1:-1] + conv_taps[2] * framed[2:]
    first = short[:, :channels]
    second = short[:, channels : 2 * channels]
    value_part = short[:, 2 * channels :]
    signal = first * value_part
    anticausal = jnp.where(position[:, None] > 0, anticausal_taps.astype(jnp.float32), 0.0)
    causal = causal_taps.astype(jnp.float32)
    moved = (
        lax.all_to_all(
            signal.astype(jnp.bfloat16), "fft", split_axis=1, concat_axis=0, tiled=True
        ).astype(signal.dtype),
        lax.all_to_all(
            causal.astype(jnp.bfloat16), "fft", split_axis=1, concat_axis=0, tiled=True
        ).astype(causal.dtype),
        lax.all_to_all(
            anticausal.astype(jnp.bfloat16), "fft", split_axis=1, concat_axis=0, tiled=True
        ).astype(anticausal.dtype),
    )
    moved = (
        lax.all_to_all(
            moved[0].astype(jnp.bfloat16), "blk", split_axis=1, concat_axis=0, tiled=True
        ).astype(jnp.float32),
        lax.all_to_all(
            moved[1].astype(jnp.bfloat16), "blk", split_axis=1, concat_axis=0, tiled=True
        ).astype(jnp.float32),
        lax.all_to_all(
            moved[2].astype(jnp.bfloat16), "blk", split_axis=1, concat_axis=0, tiled=True
        ).astype(jnp.float32),
    )
    conv_cols = local_convolution(moved[0], moved[1], moved[2])
    returned = lax.all_to_all(
        shortened(conv_cols), "blk", split_axis=0, concat_axis=1, tiled=True
    ).astype(conv_cols.dtype)
    convolved = lax.all_to_all(
        shortened(returned), "fft", split_axis=0, concat_axis=1, tiled=True
    ).astype(returned.dtype)
    convolved = convolved + skip_gain * signal
    gated = (second * convolved).astype(jnp.bfloat16)
    return jnp.dot(gated, w_out, preferred_element_type=jnp.float32).astype(jnp.bfloat16)


def grid_constants(blocks, width):
    length = 2 * blocks * width
    half_freq = np.arange(blocks) + 0.5

    rows = np.outer(half_freq, np.arange(2 * blocks)) * (2.0 * np.pi / (2 * blocks))
    flip = np.where(np.arange(2 * blocks) < blocks, 1.0, -1.0)
    across = np.concatenate([np.cos(rows), -np.sin(rows)], axis=0) * flip
    across = across.astype(ml_dtypes.bfloat16)
    turn = np.outer(half_freq, np.arange(width)) * (2.0 * np.pi / length)
    twist = np.stack([np.cos(turn), np.sin(turn)]).astype(np.float32)
    grid = np.outer(np.arange(width), np.arange(width)) % width * (2.0 * np.pi / width)
    cos, sin = np.cos(grid), np.sin(grid)
    within = np.block([[cos, -sin], [sin, cos]]).astype(np.float32)
    back = rows[:, :blocks].T
    back = np.concatenate([np.cos(back), np.sin(back)], axis=1) * (2.0 / length)
    back = back.astype(ml_dtypes.bfloat16)
    return across, twist, within, back


def dot32(a, b):
    return jnp.dot(a, b, preferred_element_type=jnp.float32)


def mixer_kernel(
    blocks,
    groups,
    tokens_hbm,
    causal_hbm,
    anti_hbm,
    conv_taps_hbm,
    skip_gain_hbm,
    across_hbm,
    twist_hbm,
    back_hbm,
    w_in_hbm,
    w_out_hbm,
    within_hbm,
    out,
    causal,
    anti,
    conv_taps,
    skip_gain,
    across,
    twist,
    back,
    w_in,
    w_out,
    within_whole,
    within,
    framed,
    edge_out,
    edge_in,
    filt_out,
    filt_in,
    sig_out,
    sig_in,
    ret_out,
    ret_in,
    spread,
    gather,
    result,
    spectrum,
    gate,
    passed,
    gated,
    load_sem,
    edge_send,
    edge_recv,
    filt_send,
    filt_recv,
    sig_send,
    sig_recv,
    ret_send,
    ret_recv,
):
    f32, bf16 = jnp.float32, jnp.bfloat16
    width, depth = tokens_hbm.shape
    channels = w_out.shape[0]
    parts, _, some, _ = sig_out.shape
    tokens = framed.at[0:width]
    blk, fft = lax.axis_index("blk"), lax.axis_index("fft")
    me = blk * groups + fft
    levels = blocks // groups
    peers = []
    for turn in range(levels - 1, -1, -1):
        level = blk ^ turn
        for step in range(groups):
            if turn > 0 or step > 0:
                other = (fft + step) & (groups - 1)
                peers.append((turn, level * groups + other, (level, other)))

    barrier = pltpu.get_barrier_semaphore()
    for _, _, coords in peers:
        pl.semaphore_signal(barrier, inc=1, device_id=coords, device_id_type=MESH)

    loads = [
        pltpu.make_async_copy(src, dst, load_sem.at[i])
        for i, (src, dst) in enumerate(
            (
                (causal_hbm, causal),
                (anti_hbm, anti),
                (tokens_hbm, tokens),
                (w_in_hbm, w_in),
                (conv_taps_hbm, conv_taps),
                (across_hbm, across),
                (twist_hbm, twist),
                (within_hbm, within_whole),
                (back_hbm, back),
                (w_out_hbm, w_out),
                (skip_gain_hbm, skip_gain),
            )
        )
    ]
    for load in loads:
        load.start()

    def send_all(src, dst, send_sem, recv_sem):
        for turn, peer, coords in peers:
            pltpu.make_async_remote_copy(
                src_ref=src.at[peer],
                dst_ref=dst.at[me],
                send_sem=send_sem,
                recv_sem=recv_sem.at[turn],
                device_id=coords,
                device_id_type=MESH,
            ).start()
        pltpu.make_async_copy(src.at[me], dst.at[me], recv_sem.at[0]).start()

    def plane_of(dst, turn):
        return dst.at[pl.ds((blk ^ turn) * groups, groups)]

    def arrived(dst, recv_sem, turn):
        plane = plane_of(dst, turn)
        pltpu.make_async_copy(plane, plane, recv_sem.at[turn]).wait()

    def all_arrived(dst, recv_sem):
        for turn in range(levels):
            arrived(dst, recv_sem, turn)

    def sent(src, send_sem):
        most = src.at[pl.ds(0, blocks - 1)]
        pltpu.make_async_copy(most, most, send_sem).wait()

    def chunks(x):
        return x.T.reshape(blocks, parts, some, width)

    for load in loads[:3]:
        load.wait()
    edge_out[0] = tokens[width - 16 :, :].astype(f32)[15:16]
    edge_out[1] = tokens[0:16, :].astype(f32)[0:1]
    unused = (lax.broadcasted_iota(jnp.int32, anti.shape, 0) == 0) & (me == 0)
    causal_rows = chunks(causal[...].astype(f32))
    anti_rows = chunks(jnp.where(unused, 0.0, anti[...].astype(f32)))
    for part in range(parts):
        filt_out[part, :, 0:some, :] = causal_rows[:, part].astype(bf16)
        filt_out[part, :, some:, :] = anti_rows[:, part].astype(bf16)
    pl.semaphore_wait(barrier, blocks - 1)
    edges = [
        pltpu.make_async_remote_copy(
            src_ref=edge_out.at[i],
            dst_ref=edge_in.at[i],
            send_sem=edge_send.at[i],
            recv_sem=edge_recv.at[i],
            device_id=(at // groups, at % groups),
            device_id_type=MESH,
        )
        for i, at in enumerate(((me + 1) % blocks, (me + blocks - 1) % blocks))
    ]
    for edge in edges:
        edge.start()

    def send_part(bufs, part):
        src, dst, send_sem, recv_sem = bufs
        send_all(src.at[part], dst.at[part], send_sem.at[part], recv_sem.at[part])

    filt = (filt_out, filt_in, filt_send, filt_recv)
    sig = (sig_out, sig_in, sig_send, sig_recv)
    ret = (ret_out, ret_in, ret_send, ret_recv)
    send_part(filt, 0)

    for load in loads[3:5]:
        load.wait()
    for edge in edges:
        edge.wait()
    row16 = lax.broadcasted_iota(jnp.int32, (16, depth), 0)
    prev = jnp.where(me == 0, 0.0, edge_in[0])
    following = jnp.where(me == blocks - 1, 0.0, edge_in[1])
    framed[width:, :] = jnp.where(
        row16 == 0, prev, jnp.where(row16 == 1, following, 0.0)
    ).astype(bf16)
    row = lax.broadcasted_iota(jnp.int32, (width, channels), 0)

    def stream(which):
        cols = slice(which * channels, (which + 1) * channels)
        proj = dot32(framed[...], w_in[:, cols]).astype(bf16).astype(f32)
        here = proj[:width]
        before = jnp.where(row == 0, proj[width : width + 1], pltpu.roll(here, 1, 0))
        after = jnp.where(
            row == width - 1, proj[width + 1 : width + 2], pltpu.roll(here, width - 1, 0)
        )
        taps = conv_taps[:, cols]
        return taps[0:1] * before + taps[1:2] * here + taps[2:3] * after

    signal = stream(0) * stream(2)
    signal_rows = chunks(signal)
    for part in range(parts):
        sig_out[part] = signal_rows[:, part].astype(bf16)
        send_part(sig, part)
        if part + 1 < parts:
            send_part(filt, part + 1)

    for load in loads[5:]:
        load.wait()
    second = stream(1)
    direct = second * (skip_gain[...] * signal)
    span = channels // levels
    for level in range(levels):
        gate[level] = second[:, level * span : (level + 1) * span]
        passed[level] = direct[:, level * span : (level + 1) * span]
    within[...] = within_whole[...].astype(bf16)
    cos, sin = twist[0], twist[1]

    def twisted(real, imag, axis):
        return jnp.concatenate([real * cos + imag * sin, imag * cos - real * sin], axis=axis)

    def lane(x, c):
        return x[:, c * width : (c + 1) * width]

    def forward(columns, mats):
        freq = dot32(mats, jnp.concatenate(columns, axis=1))
        turned = [
            twisted(lane(freq[:blocks], c), lane(freq[blocks:], c), 1)
            for c in range(len(columns))
        ]
        return dot32(jnp.concatenate(turned, axis=0).astype(bf16), within[...])

    few = 4
    sets = [list(range(c, c + few)) for c in range(0, some, few)]
    for part in range(parts):
        all_arrived(filt_in.at[part], filt_recv.at[part])
        spread[...] = filt_in[part].astype(f32).reshape(2 * blocks * some, width)
        for n, members in enumerate(sets):
            columns = [
                jnp.concatenate(
                    [
                        spread[pl.ds(c, blocks, stride=2 * some), :],
                        spread[pl.ds(some + c, blocks, stride=2 * some), :],
                    ],
                    axis=0,
                ).astype(bf16)
                for c in members
            ]
            spectrum[n] = forward(columns, across[...])

        all_arrived(sig_in.at[part], sig_recv.at[part])
        gather[...] = sig_in[part].astype(f32).reshape(blocks * some, width)
        for n, members in enumerate(sets):
            columns = [
                gather[pl.ds(c, blocks, stride=some), :].astype(bf16) for c in members
            ]
            freq = forward(columns, across[:, 0:blocks])
            s_real, s_imag = freq[:, :width], freq[:, width:]
            f_real, f_imag = spectrum[n, :, :width], spectrum[n, :, width:]
            product = jnp.concatenate(
                [s_real * f_real - s_imag * f_imag, -(s_real * f_imag + s_imag * f_real)],
                axis=1,
            )
            turned = dot32(product.astype(bf16), within[...])
            pieces = [turned[i * blocks : (i + 1) * blocks] for i in range(few)]
            pieces = [twisted(x[:, :width], x[:, width:], 0) for x in pieces]
            conv = dot32(back[...], jnp.concatenate(pieces, axis=1).astype(bf16))
            for i, c in enumerate(members):
                result[pl.ds(c, blocks, stride=some), :] = lane(conv, i)
        ret_out[part] = result[...].astype(bf16).reshape(blocks, some, width)
        send_part(ret, part)

    for turn in range(levels):
        level = blk ^ turn
        for part in range(parts):
            arrived(ret_in.at[part], ret_recv.at[part], turn)
        landed = [plane_of(ret_in.at[part], turn)[...].astype(f32) for part in range(parts)]
        landed = jnp.concatenate(landed, axis=1).reshape(span, width).T
        cols = pl.ds(pl.multiple_of(level * span, span), span)
        gated[:, cols] = (gate[level] * landed + passed[level]).astype(bf16)
    out[...] = dot32(gated[...], w_out[...]).astype(bf16)
    for src, _, send_sem, _ in (filt, sig, ret):
        for part in range(parts):
            sent(src.at[part], send_sem.at[part])


def one_kernel(tokens, w_in, conv_taps, causal_taps, anticausal_taps, skip_gain, w_out):
    width, depth = tokens.shape
    channels = w_out.shape[0]
    groups = lax.axis_size("fft")
    blocks = lax.axis_size("blk") * groups
    levels = lax.axis_size("blk")
    parts = 2
    some = channels // blocks // parts
    across, twist, within, back = grid_constants(blocks, width)
    f32, bf16 = jnp.float32, jnp.bfloat16
    vmem = pl.BlockSpec(memory_space=pltpu.VMEM)
    hbm = pl.BlockSpec(memory_space=pl.ANY)
    one = pltpu.SemaphoreType.DMA
    return pl.pallas_call(
        functools.partial(mixer_kernel, blocks, groups),
        out_shape=pltpu.VMEM((width, w_out.shape[1]), bf16),
        in_specs=[hbm] * 11,
        out_specs=vmem,
        scratch_shapes=[
            pltpu.VMEM(causal_taps.shape, bf16),
            pltpu.VMEM(anticausal_taps.shape, bf16),
            pltpu.VMEM(conv_taps.shape, f32),
            pltpu.VMEM((1, channels), f32),
            pltpu.VMEM(across.shape, bf16),
            pltpu.VMEM(twist.shape, f32),
            pltpu.VMEM(back.shape, bf16),
            pltpu.VMEM(w_in.shape, bf16),
            pltpu.VMEM(w_out.shape, bf16),
            pltpu.VMEM(within.shape, f32),
            pltpu.VMEM(within.shape, bf16),
            pltpu.VMEM((width + 16, depth), bf16),
            pltpu.VMEM((2, 1, depth), f32),
            pltpu.VMEM((2, 1, depth), f32),
            pltpu.VMEM((parts, blocks, 2 * some, width), bf16),
            pltpu.VMEM((parts, blocks, 2 * some, width), bf16),
            pltpu.VMEM((parts, blocks, some, width), bf16),
            pltpu.VMEM((parts, blocks, some, width), bf16),
            pltpu.VMEM((parts, blocks, some, width), bf16),
            pltpu.VMEM((parts, blocks, some, width), bf16),
            pltpu.VMEM((2 * blocks * some, width), f32),
            pltpu.VMEM((blocks * some, width), f32),
            pltpu.VMEM((blocks * some, width), f32),
            pltpu.VMEM((some // 4, 4 * blocks, 2 * width), f32),
            pltpu.VMEM((levels, width, channels // levels), f32),
            pltpu.VMEM((levels, width, channels // levels), f32),
            pltpu.VMEM((width, channels), bf16),
            one((11,)),
            one((2,)),
            one((2,)),
            one((parts,)),
            one((parts, levels)),
            one((parts,)),
            one((parts, levels)),
            one((parts,)),
            one((parts, levels)),
        ],
        compiler_params=pltpu.CompilerParams(
            collective_id=0, has_side_effects=True, vmem_limit_bytes=62 * 2**20
        ),
    )(
        tokens,
        causal_taps,
        anticausal_taps,
        conv_taps,
        skip_gain[None, :],
        jnp.asarray(across),
        jnp.asarray(twist),
        jnp.asarray(back),
        w_in,
        w_out,
        jnp.asarray(within),
    )


def mixer(tokens, w_in, conv_taps, causal_taps, anticausal_taps, skip_gain, w_out):
    devices = lax.axis_size("blk") * lax.axis_size("fft")
    fits = tokens.shape[0] == 128 and w_out.shape[0] == 16 * devices
    chosen = one_kernel if fits else body
    return chosen(tokens, w_in, conv_taps, causal_taps, anticausal_taps, skip_gain, w_out)


def solution(mesh):
    in_specs = (
        P(("blk", "fft"), None),
        P(),
        P(),
        P(("blk", "fft"), None),
        P(("blk", "fft"), None),
        P(),
        P(),
    )
    out_specs = P(("blk", "fft"), None)
    return jax.shard_map(mixer, mesh=mesh, in_specs=in_specs, out_specs=out_specs, check_vma=False)
```

```python
import functools
import math

import jax
import jax.numpy as jnp
import ml_dtypes
import numpy as np
from jax import lax
from jax.experimental import pallas as pl
from jax.experimental.pallas import tpu as pltpu
from jax.sharding import PartitionSpec as P

MESH = pl.DeviceIdType.MESH


def with_halo(cells, sides, width):
    for axis, dim in sides:
        count = lax.axis_size(axis)
        ends = count - 1
        head = lax.slice_in_dim(cells, 0, width, axis=dim)
        tail = lax.slice_in_dim(cells, cells.shape[dim] - width, cells.shape[dim], axis=dim)
        cells = jnp.concatenate(
            [
                lax.ppermute(tail, axis, [(i, (i + 1) % count) for i in range(ends)]),
                cells,
                lax.ppermute(head, axis, [((i + 1) % count, i) for i in range(ends)]),
            ],
            axis=dim,
        )
    return cells


def shortened(x):

    def short(part):
        return part.astype(jnp.bfloat16) if part.dtype == jnp.float32 else part

    return jax.tree.map(short, x)


def log_count(count):
    return count.bit_length() - 1


def dft_matrix(count, sign, scale):
    grid = jnp.arange(count, dtype=jnp.int32)
    angle = (
        sign * 2.0 * math.pi * (grid[:, None] * grid[None, :] % count).astype(jnp.float32) / count
    )
    return (jnp.cos(angle) * scale, jnp.sin(angle) * scale)


def local_convolution(signal_cols, causal_cols, anti_cols):
    seq_len = signal_cols.shape[0]
    width = signal_cols.shape[1]
    length = 2 * seq_len
    rows_p = 2 ** (log_count(length) // 2)
    cols_q = length // rows_p
    high = lax.Precision.HIGHEST
    p_real, p_imag = dft_matrix(rows_p, -1.0, 1.0)
    q_real, q_imag = dft_matrix(cols_q, -1.0, 1.0)
    pp_real, pp_imag = dft_matrix(rows_p, 1.0, 1.0 / length)
    qp_real, qp_imag = dft_matrix(cols_q, 1.0, 1.0)
    k_grid = jnp.arange(rows_p, dtype=jnp.int32)
    n_grid = jnp.arange(cols_q, dtype=jnp.int32)
    tw_angle = (
        -2.0 * math.pi * (k_grid[:, None] * n_grid[None, :] % length).astype(jnp.float32) / length
    )
    tw_cos = jnp.cos(tw_angle)
    tw_sin = jnp.sin(tw_angle)

    def forward(grid_rows):
        half = grid_rows.shape[1]
        b_real = jnp.einsum("kp,cpq->ckq", p_real[:, :half], grid_rows, precision=high)
        b_imag = jnp.einsum("kp,cpq->ckq", p_imag[:, :half], grid_rows, precision=high)
        c_real = b_real * tw_cos - b_imag * tw_sin
        c_imag = b_real * tw_sin + b_imag * tw_cos
        x_real = jnp.einsum("ckq,qr->ckr", c_real, q_real, precision=high) - jnp.einsum(
            "ckq,qr->ckr", c_imag, q_imag, precision=high
        )
        x_imag = jnp.einsum("ckq,qr->ckr", c_real, q_imag, precision=high) + jnp.einsum(
            "ckq,qr->ckr", c_imag, q_real, precision=high
        )
        return (x_real, x_imag)

    sig_grid = signal_cols.T.reshape(width, rows_p // 2, cols_q)
    filt_grid = jnp.concatenate([causal_cols, anti_cols], axis=0).T.reshape(width, rows_p, cols_q)
    s_real, s_imag = forward(sig_grid)
    f_real, f_imag = forward(filt_grid)
    y_real = s_real * f_real - s_imag * f_imag
    y_imag = s_real * f_imag + s_imag * f_real
    d_real = jnp.einsum("ckq,qr->ckr", y_real, qp_real, precision=high) - jnp.einsum(
        "ckq,qr->ckr", y_imag, qp_imag, precision=high
    )
    d_imag = jnp.einsum("ckq,qr->ckr", y_real, qp_imag, precision=high) + jnp.einsum(
        "ckq,qr->ckr", y_imag, qp_real, precision=high
    )
    e_real = d_real * tw_cos + d_imag * tw_sin
    e_imag = d_imag * tw_cos - d_real * tw_sin
    half_rows = rows_p // 2
    out_grid = jnp.einsum("nk,ckq->cnq", pp_real[:half_rows], e_real, precision=high) - jnp.einsum(
        "nk,ckq->cnq", pp_imag[:half_rows], e_imag, precision=high
    )
    return out_grid.reshape(width, seq_len).T


def body(tokens, w_in, conv_taps, causal_taps, anticausal_taps, skip_gain, w_out):
    tok_rows = tokens.shape[0]
    channels = w_out.shape[0]
    groups = lax.axis_size("fft")
    blk_index = lax.axis_index("blk")
    fft_index = lax.axis_index("fft")
    device_index = blk_index * groups + fft_index
    position = device_index * tok_rows + jnp.arange(tok_rows, dtype=jnp.int32)
    proj = jnp.dot(tokens, w_in, preferred_element_type=jnp.float32).astype(jnp.bfloat16)
    framed = with_halo(proj, ((("blk", "fft"), 0),), 1).astype(jnp.float32)
    short = conv_taps[0] * framed[:-2] + conv_taps[1] * framed[1:-1] + conv_taps[2] * framed[2:]
    first = short[:, :channels]
    second = short[:, channels : 2 * channels]
    value_part = short[:, 2 * channels :]
    signal = first * value_part
    anticausal = jnp.where(position[:, None] > 0, anticausal_taps.astype(jnp.float32), 0.0)
    causal = causal_taps.astype(jnp.float32)
    moved = (
        lax.all_to_all(
            signal.astype(jnp.bfloat16), "fft", split_axis=1, concat_axis=0, tiled=True
        ).astype(signal.dtype),
        lax.all_to_all(
            causal.astype(jnp.bfloat16), "fft", split_axis=1, concat_axis=0, tiled=True
        ).astype(causal.dtype),
        lax.all_to_all(
            anticausal.astype(jnp.bfloat16), "fft", split_axis=1, concat_axis=0, tiled=True
        ).astype(anticausal.dtype),
    )
    moved = (
        lax.all_to_all(
            moved[0].astype(jnp.bfloat16), "blk", split_axis=1, concat_axis=0, tiled=True
        ).astype(jnp.float32),
        lax.all_to_all(
            moved[1].astype(jnp.bfloat16), "blk", split_axis=1, concat_axis=0, tiled=True
        ).astype(jnp.float32),
        lax.all_to_all(
            moved[2].astype(jnp.bfloat16), "blk", split_axis=1, concat_axis=0, tiled=True
        ).astype(jnp.float32),
    )
    conv_cols = local_convolution(moved[0], moved[1], moved[2])
    returned = lax.all_to_all(
        shortened(conv_cols), "blk", split_axis=0, concat_axis=1, tiled=True
    ).astype(conv_cols.dtype)
    convolved = lax.all_to_all(
        shortened(returned), "fft", split_axis=0, concat_axis=1, tiled=True
    ).astype(returned.dtype)
    convolved = convolved + skip_gain * signal
    gated = (second * convolved).astype(jnp.bfloat16)
    return jnp.dot(gated, w_out, preferred_element_type=jnp.float32).astype(jnp.bfloat16)


def grid_constants(blocks, width):
    length = 2 * blocks * width
    half_freq = np.arange(blocks) + 0.5

    rows = np.outer(half_freq, np.arange(2 * blocks)) * (2.0 * np.pi / (2 * blocks))
    flip = np.where(np.arange(2 * blocks) < blocks, 1.0, -1.0)
    across = np.concatenate([np.cos(rows), -np.sin(rows)], axis=0) * flip
    across = across.astype(ml_dtypes.bfloat16)
    turn = np.outer(half_freq, np.arange(width)) * (2.0 * np.pi / length)
    twist = np.stack([np.cos(turn), np.sin(turn)]).astype(np.float32)
    grid = np.outer(np.arange(width), np.arange(width)) % width * (2.0 * np.pi / width)
    cos, sin = np.cos(grid), np.sin(grid)
    within = np.block([[cos, -sin], [sin, cos]]).astype(np.float32)
    back = rows[:, :blocks].T
    back = np.concatenate([np.cos(back), np.sin(back)], axis=1) * (2.0 / length)
    back = back.astype(ml_dtypes.bfloat16)
    return across, twist, within, back


def dot32(a, b):
    return jnp.dot(a, b, preferred_element_type=jnp.float32)


def mixer_kernel(
    blocks,
    groups,
    tokens_hbm,
    causal_hbm,
    anti_hbm,
    conv_taps_hbm,
    skip_gain_hbm,
    across_hbm,
    twist_hbm,
    back_hbm,
    w_in_hbm,
    w_out_hbm,
    within_hbm,
    out,
    causal,
    anti,
    conv_taps,
    skip_gain,
    across,
    twist,
    back,
    w_in,
    w_out,
    within_whole,
    within,
    framed,
    edge_out,
    edge_in,
    filt_out,
    filt_in,
    sig_out,
    sig_in,
    ret_out,
    ret_in,
    spread,
    gather,
    result,
    spectrum,
    gate,
    passed,
    gated,
    load_sem,
    edge_send,
    edge_recv,
    filt_send,
    filt_recv,
    sig_send,
    sig_recv,
    ret_send,
    ret_recv,
):
    f32, bf16 = jnp.float32, jnp.bfloat16
    width, depth = tokens_hbm.shape
    channels = w_out.shape[0]
    parts, _, some, _ = sig_out.shape
    tokens = framed.at[0:width]
    blk, fft = lax.axis_index("blk"), lax.axis_index("fft")
    me = blk * groups + fft
    levels = blocks // groups
    peers = []
    for turn in range(levels - 1, -1, -1):
        level = blk ^ turn
        for step in range(groups):
            if turn > 0 or step > 0:
                other = (fft + step) & (groups - 1)
                peers.append((turn, level * groups + other, (level, other)))

    barrier = pltpu.get_barrier_semaphore()
    for _, _, coords in peers:
        pl.semaphore_signal(barrier, inc=1, device_id=coords, device_id_type=MESH)

    loads = [
        pltpu.make_async_copy(src, dst, load_sem.at[i])
        for i, (src, dst) in enumerate(
            (
                (causal_hbm, causal),
                (anti_hbm, anti),
                (tokens_hbm, tokens),
                (w_in_hbm, w_in),
                (conv_taps_hbm, conv_taps),
                (across_hbm, across),
                (twist_hbm, twist),
                (within_hbm, within_whole),
                (back_hbm, back),
                (w_out_hbm, w_out),
                (skip_gain_hbm, skip_gain),
            )
        )
    ]
    for load in loads:
        load.start()

    def send_all(src, dst, send_sem, recv_sem):
        for turn, peer, coords in peers:
            pltpu.make_async_remote_copy(
                src_ref=src.at[peer],
                dst_ref=dst.at[me],
                send_sem=send_sem,
                recv_sem=recv_sem.at[turn],
                device_id=coords,
                device_id_type=MESH,
            ).start()
        pltpu.make_async_copy(src.at[me], dst.at[me], recv_sem.at[0]).start()

    def plane_of(dst, turn):
        return dst.at[pl.ds((blk ^ turn) * groups, groups)]

    def arrived(dst, recv_sem, turn):
        plane = plane_of(dst, turn)
        pltpu.make_async_copy(plane, plane, recv_sem.at[turn]).wait()

    def all_arrived(dst, recv_sem):
        for turn in range(levels):
            arrived(dst, recv_sem, turn)

    def sent(src, send_sem):
        most = src.at[pl.ds(0, blocks - 1)]
        pltpu.make_async_copy(most, most, send_sem).wait()

    def chunks(x):
        return x.T.reshape(blocks, parts, some, width)

    for load in loads[:3]:
        load.wait()
    edge_out[0] = tokens[width - 16 :, :].astype(f32)[15:16]
    edge_out[1] = tokens[0:16, :].astype(f32)[0:1]
    unused = (lax.broadcasted_iota(jnp.int32, anti.shape, 0) == 0) & (me == 0)
    causal_rows = chunks(causal[...].astype(f32))
    anti_rows = chunks(jnp.where(unused, 0.0, anti[...].astype(f32)))
    for part in range(parts):
        filt_out[part, :, 0:some, :] = causal_rows[:, part].astype(bf16)
        filt_out[part, :, some:, :] = anti_rows[:, part].astype(bf16)
    pl.semaphore_wait(barrier, blocks - 1)
    edges = [
        pltpu.make_async_remote_copy(
            src_ref=edge_out.at[i],
            dst_ref=edge_in.at[i],
            send_sem=edge_send.at[i],
            recv_sem=edge_recv.at[i],
            device_id=(at // groups, at % groups),
            device_id_type=MESH,
        )
        for i, at in enumerate(((me + 1) % blocks, (me + blocks - 1) % blocks))
    ]
    for edge in edges:
        edge.start()

    def send_part(bufs, part):
        src, dst, send_sem, recv_sem = bufs
        send_all(src.at[part], dst.at[part], send_sem.at[part], recv_sem.at[part])

    filt = (filt_out, filt_in, filt_send, filt_recv)
    sig = (sig_out, sig_in, sig_send, sig_recv)
    ret = (ret_out, ret_in, ret_send, ret_recv)
    send_part(filt, 0)

    for load in loads[3:5]:
        load.wait()
    for edge in edges:
        edge.wait()
    row16 = lax.broadcasted_iota(jnp.int32, (16, depth), 0)
    prev = jnp.where(me == 0, 0.0, edge_in[0])
    following = jnp.where(me == blocks - 1, 0.0, edge_in[1])
    framed[width:, :] = jnp.where(
        row16 == 0, prev, jnp.where(row16 == 1, following, 0.0)
    ).astype(bf16)
    row = lax.broadcasted_iota(jnp.int32, (width, channels), 0)

    def stream(which):
        cols = slice(which * channels, (which + 1) * channels)
        proj = dot32(framed[...], w_in[:, cols]).astype(bf16).astype(f32)
        here = proj[:width]
        before = jnp.where(row == 0, proj[width : width + 1], pltpu.roll(here, 1, 0))
        after = jnp.where(
            row == width - 1, proj[width + 1 : width + 2], pltpu.roll(here, width - 1, 0)
        )
        taps = conv_taps[:, cols]
        return taps[0:1] * before + taps[1:2] * here + taps[2:3] * after

    signal = stream(0) * stream(2)
    signal_rows = chunks(signal)
    for part in range(parts):
        sig_out[part] = signal_rows[:, part].astype(bf16)
        send_part(sig, part)
        if part + 1 < parts:
            send_part(filt, part + 1)

    for load in loads[5:]:
        load.wait()
    second = stream(1)
    direct = second * (skip_gain[...] * signal)
    span = channels // levels
    for level in range(levels):
        gate[level] = second[:, level * span : (level + 1) * span]
        passed[level] = direct[:, level * span : (level + 1) * span]
    within[...] = within_whole[...].astype(bf16)
    cos, sin = twist[0], twist[1]

    def twisted(real, imag, axis):
        return jnp.concatenate([real * cos + imag * sin, imag * cos - real * sin], axis=axis)

    def lane(x, c):
        return x[:, c * width : (c + 1) * width]

    def forward(columns, mats):
        freq = dot32(mats, jnp.concatenate(columns, axis=1))
        turned = [
            twisted(lane(freq[:blocks], c), lane(freq[blocks:], c), 1)
            for c in range(len(columns))
        ]
        return dot32(jnp.concatenate(turned, axis=0).astype(bf16), within[...])

    for part in range(parts):
        all_arrived(filt_in.at[part], filt_recv.at[part])
        spread[...] = filt_in[part].astype(f32).reshape(2 * blocks * some, width)
        columns = [
            jnp.concatenate(
                [
                    spread[pl.ds(c, blocks, stride=2 * some), :],
                    spread[pl.ds(some + c, blocks, stride=2 * some), :],
                ],
                axis=0,
            ).astype(bf16)
            for c in range(some)
        ]
        spectrum[...] = forward(columns, across[...])

        all_arrived(sig_in.at[part], sig_recv.at[part])
        gather[...] = sig_in[part].astype(f32).reshape(blocks * some, width)
        columns = [
            gather[pl.ds(c, blocks, stride=some), :].astype(bf16) for c in range(some)
        ]
        freq = forward(columns, across[:, 0:blocks])
        s_real, s_imag = freq[:, :width], freq[:, width:]
        f_real, f_imag = spectrum[:, :width], spectrum[:, width:]
        product = jnp.concatenate(
            [s_real * f_real - s_imag * f_imag, -(s_real * f_imag + s_imag * f_real)],
            axis=1,
        )
        turned = dot32(product.astype(bf16), within[...])
        pieces = [turned[i * blocks : (i + 1) * blocks] for i in range(some)]
        pieces = [twisted(x[:, :width], x[:, width:], 0) for x in pieces]
        conv = dot32(back[...], jnp.concatenate(pieces, axis=1).astype(bf16))
        for c in range(some):
            result[pl.ds(c, blocks, stride=some), :] = lane(conv, c)
        ret_out[part] = result[...].astype(bf16).reshape(blocks, some, width)
        send_part(ret, part)

    for turn in range(levels):
        level = blk ^ turn
        for part in range(parts):
            arrived(ret_in.at[part], ret_recv.at[part], turn)
        landed = [plane_of(ret_in.at[part], turn)[...].astype(f32) for part in range(parts)]
        landed = jnp.concatenate(landed, axis=1).reshape(span, width).T
        cols = pl.ds(pl.multiple_of(level * span, span), span)
        gated[:, cols] = (gate[level] * landed + passed[level]).astype(bf16)
    out[...] = dot32(gated[...], w_out[...]).astype(bf16)
    for src, _, send_sem, _ in (filt, sig, ret):
        for part in range(parts):
            sent(src.at[part], send_sem.at[part])


def one_kernel(tokens, w_in, conv_taps, causal_taps, anticausal_taps, skip_gain, w_out):
    width, depth = tokens.shape
    channels = w_out.shape[0]
    groups = lax.axis_size("fft")
    blocks = lax.axis_size("blk") * groups
    levels = lax.axis_size("blk")
    parts = 2
    some = channels // blocks // parts
    across, twist, within, back = grid_constants(blocks, width)
    f32, bf16 = jnp.float32, jnp.bfloat16
    vmem = pl.BlockSpec(memory_space=pltpu.VMEM)
    hbm = pl.BlockSpec(memory_space=pl.ANY)
    one = pltpu.SemaphoreType.DMA
    return pl.pallas_call(
        functools.partial(mixer_kernel, blocks, groups),
        out_shape=pltpu.VMEM((width, w_out.shape[1]), bf16),
        in_specs=[hbm] * 11,
        out_specs=vmem,
        scratch_shapes=[
            pltpu.VMEM(causal_taps.shape, bf16),
            pltpu.VMEM(anticausal_taps.shape, bf16),
            pltpu.VMEM(conv_taps.shape, f32),
            pltpu.VMEM((1, channels), f32),
            pltpu.VMEM(across.shape, bf16),
            pltpu.VMEM(twist.shape, f32),
            pltpu.VMEM(back.shape, bf16),
            pltpu.VMEM(w_in.shape, bf16),
            pltpu.VMEM(w_out.shape, bf16),
            pltpu.VMEM(within.shape, f32),
            pltpu.VMEM(within.shape, bf16),
            pltpu.VMEM((width + 16, depth), bf16),
            pltpu.VMEM((2, 1, depth), f32),
            pltpu.VMEM((2, 1, depth), f32),
            pltpu.VMEM((parts, blocks, 2 * some, width), bf16),
            pltpu.VMEM((parts, blocks, 2 * some, width), bf16),
            pltpu.VMEM((parts, blocks, some, width), bf16),
            pltpu.VMEM((parts, blocks, some, width), bf16),
            pltpu.VMEM((parts, blocks, some, width), bf16),
            pltpu.VMEM((parts, blocks, some, width), bf16),
            pltpu.VMEM((2 * blocks * some, width), f32),
            pltpu.VMEM((blocks * some, width), f32),
            pltpu.VMEM((blocks * some, width), f32),
            pltpu.VMEM((some * blocks, 2 * width), f32),
            pltpu.VMEM((levels, width, channels // levels), f32),
            pltpu.VMEM((levels, width, channels // levels), f32),
            pltpu.VMEM((width, channels), bf16),
            one((11,)),
            one((2,)),
            one((2,)),
            one((parts,)),
            one((parts, levels)),
            one((parts,)),
            one((parts, levels)),
            one((parts,)),
            one((parts, levels)),
        ],
        compiler_params=pltpu.CompilerParams(
            collective_id=0, has_side_effects=True, vmem_limit_bytes=62 * 2**20
        ),
    )(
        tokens,
        causal_taps,
        anticausal_taps,
        conv_taps,
        skip_gain[None, :],
        jnp.asarray(across),
        jnp.asarray(twist),
        jnp.asarray(back),
        w_in,
        w_out,
        jnp.asarray(within),
    )


def mixer(tokens, w_in, conv_taps, causal_taps, anticausal_taps, skip_gain, w_out):
    devices = lax.axis_size("blk") * lax.axis_size("fft")
    fits = tokens.shape[0] == 128 and w_out.shape[0] == 16 * devices
    chosen = one_kernel if fits else body
    return chosen(tokens, w_in, conv_taps, causal_taps, anticausal_taps, skip_gain, w_out)


def solution(mesh):
    in_specs = (
        P(("blk", "fft"), None),
        P(),
        P(),
        P(("blk", "fft"), None),
        P(("blk", "fft"), None),
        P(),
        P(),
    )
    out_specs = P(("blk", "fft"), None)
    return jax.shard_map(mixer, mesh=mesh, in_specs=in_specs, out_specs=out_specs, check_vma=False)
```

```python
import functools
import math

import jax
import jax.numpy as jnp
import ml_dtypes
import numpy as np
from jax import lax
from jax.experimental import pallas as pl
from jax.experimental.pallas import tpu as pltpu
from jax.sharding import PartitionSpec as P

MESH = pl.DeviceIdType.MESH


def with_halo(cells, sides, width):
    for axis, dim in sides:
        count = lax.axis_size(axis)
        ends = count - 1
        head = lax.slice_in_dim(cells, 0, width, axis=dim)
        tail = lax.slice_in_dim(cells, cells.shape[dim] - width, cells.shape[dim], axis=dim)
        cells = jnp.concatenate(
            [
                lax.ppermute(tail, axis, [(i, (i + 1) % count) for i in range(ends)]),
                cells,
                lax.ppermute(head, axis, [((i + 1) % count, i) for i in range(ends)]),
            ],
            axis=dim,
        )
    return cells


def shortened(x):

    def short(part):
        return part.astype(jnp.bfloat16) if part.dtype == jnp.float32 else part

    return jax.tree.map(short, x)


def log_count(count):
    return count.bit_length() - 1


def dft_matrix(count, sign, scale):
    grid = jnp.arange(count, dtype=jnp.int32)
    angle = (
        sign * 2.0 * math.pi * (grid[:, None] * grid[None, :] % count).astype(jnp.float32) / count
    )
    return (jnp.cos(angle) * scale, jnp.sin(angle) * scale)


def local_convolution(signal_cols, causal_cols, anti_cols):
    seq_len = signal_cols.shape[0]
    width = signal_cols.shape[1]
    length = 2 * seq_len
    rows_p = 2 ** (log_count(length) // 2)
    cols_q = length // rows_p
    high = lax.Precision.HIGHEST
    p_real, p_imag = dft_matrix(rows_p, -1.0, 1.0)
    q_real, q_imag = dft_matrix(cols_q, -1.0, 1.0)
    pp_real, pp_imag = dft_matrix(rows_p, 1.0, 1.0 / length)
    qp_real, qp_imag = dft_matrix(cols_q, 1.0, 1.0)
    k_grid = jnp.arange(rows_p, dtype=jnp.int32)
    n_grid = jnp.arange(cols_q, dtype=jnp.int32)
    tw_angle = (
        -2.0 * math.pi * (k_grid[:, None] * n_grid[None, :] % length).astype(jnp.float32) / length
    )
    tw_cos = jnp.cos(tw_angle)
    tw_sin = jnp.sin(tw_angle)

    def forward(grid_rows):
        half = grid_rows.shape[1]
        b_real = jnp.einsum("kp,cpq->ckq", p_real[:, :half], grid_rows, precision=high)
        b_imag = jnp.einsum("kp,cpq->ckq", p_imag[:, :half], grid_rows, precision=high)
        c_real = b_real * tw_cos - b_imag * tw_sin
        c_imag = b_real * tw_sin + b_imag * tw_cos
        x_real = jnp.einsum("ckq,qr->ckr", c_real, q_real, precision=high) - jnp.einsum(
            "ckq,qr->ckr", c_imag, q_imag, precision=high
        )
        x_imag = jnp.einsum("ckq,qr->ckr", c_real, q_imag, precision=high) + jnp.einsum(
            "ckq,qr->ckr", c_imag, q_real, precision=high
        )
        return (x_real, x_imag)

    sig_grid = signal_cols.T.reshape(width, rows_p // 2, cols_q)
    filt_grid = jnp.concatenate([causal_cols, anti_cols], axis=0).T.reshape(width, rows_p, cols_q)
    s_real, s_imag = forward(sig_grid)
    f_real, f_imag = forward(filt_grid)
    y_real = s_real * f_real - s_imag * f_imag
    y_imag = s_real * f_imag + s_imag * f_real
    d_real = jnp.einsum("ckq,qr->ckr", y_real, qp_real, precision=high) - jnp.einsum(
        "ckq,qr->ckr", y_imag, qp_imag, precision=high
    )
    d_imag = jnp.einsum("ckq,qr->ckr", y_real, qp_imag, precision=high) + jnp.einsum(
        "ckq,qr->ckr", y_imag, qp_real, precision=high
    )
    e_real = d_real * tw_cos + d_imag * tw_sin
    e_imag = d_imag * tw_cos - d_real * tw_sin
    half_rows = rows_p // 2
    out_grid = jnp.einsum("nk,ckq->cnq", pp_real[:half_rows], e_real, precision=high) - jnp.einsum(
        "nk,ckq->cnq", pp_imag[:half_rows], e_imag, precision=high
    )
    return out_grid.reshape(width, seq_len).T


def body(tokens, w_in, conv_taps, causal_taps, anticausal_taps, skip_gain, w_out):
    tok_rows = tokens.shape[0]
    channels = w_out.shape[0]
    groups = lax.axis_size("fft")
    blk_index = lax.axis_index("blk")
    fft_index = lax.axis_index("fft")
    device_index = blk_index * groups + fft_index
    position = device_index * tok_rows + jnp.arange(tok_rows, dtype=jnp.int32)
    proj = jnp.dot(tokens, w_in, preferred_element_type=jnp.float32).astype(jnp.bfloat16)
    framed = with_halo(proj, ((("blk", "fft"), 0),), 1).astype(jnp.float32)
    short = conv_taps[0] * framed[:-2] + conv_taps[1] * framed[1:-1] + conv_taps[2] * framed[2:]
    first = short[:, :channels]
    second = short[:, channels : 2 * channels]
    value_part = short[:, 2 * channels :]
    signal = first * value_part
    anticausal = jnp.where(position[:, None] > 0, anticausal_taps.astype(jnp.float32), 0.0)
    causal = causal_taps.astype(jnp.float32)
    moved = (
        lax.all_to_all(
            signal.astype(jnp.bfloat16), "fft", split_axis=1, concat_axis=0, tiled=True
        ).astype(signal.dtype),
        lax.all_to_all(
            causal.astype(jnp.bfloat16), "fft", split_axis=1, concat_axis=0, tiled=True
        ).astype(causal.dtype),
        lax.all_to_all(
            anticausal.astype(jnp.bfloat16), "fft", split_axis=1, concat_axis=0, tiled=True
        ).astype(anticausal.dtype),
    )
    moved = (
        lax.all_to_all(
            moved[0].astype(jnp.bfloat16), "blk", split_axis=1, concat_axis=0, tiled=True
        ).astype(jnp.float32),
        lax.all_to_all(
            moved[1].astype(jnp.bfloat16), "blk", split_axis=1, concat_axis=0, tiled=True
        ).astype(jnp.float32),
        lax.all_to_all(
            moved[2].astype(jnp.bfloat16), "blk", split_axis=1, concat_axis=0, tiled=True
        ).astype(jnp.float32),
    )
    conv_cols = local_convolution(moved[0], moved[1], moved[2])
    returned = lax.all_to_all(
        shortened(conv_cols), "blk", split_axis=0, concat_axis=1, tiled=True
    ).astype(conv_cols.dtype)
    convolved = lax.all_to_all(
        shortened(returned), "fft", split_axis=0, concat_axis=1, tiled=True
    ).astype(returned.dtype)
    convolved = convolved + skip_gain * signal
    gated = (second * convolved).astype(jnp.bfloat16)
    return jnp.dot(gated, w_out, preferred_element_type=jnp.float32).astype(jnp.bfloat16)


def grid_constants(blocks, width, some):
    length = 2 * blocks * width
    half_freq = np.arange(blocks) + 0.5
    each = np.eye(some)
    rows = np.outer(half_freq, np.arange(2 * blocks)) * (2.0 * np.pi / (2 * blocks))
    flip = np.where(np.arange(2 * blocks) < blocks, 1.0, -1.0)
    across = np.concatenate([np.cos(rows), -np.sin(rows)], axis=0) * flip
    paired = across.reshape(2 * blocks, 2, blocks).transpose(0, 2, 1).reshape(across.shape)
    turn = np.outer(half_freq, np.arange(width)) * (2.0 * np.pi / length)
    twist = np.stack([np.cos(turn), np.sin(turn)]).astype(np.float32)
    grid = np.outer(np.arange(width), np.arange(width)) % width * (2.0 * np.pi / width)
    cos, sin = np.cos(grid), np.sin(grid)
    within = np.block([[cos, -sin], [sin, cos]])
    back = rows[:, :blocks].T
    back = np.concatenate([np.cos(back), np.sin(back)], axis=1) * (2.0 / length)
    mats = [np.kron(paired, each), np.kron(across[:, :blocks], each), within, np.kron(back, each)]
    tiles = [np.split(mat, mat.shape[1] // 128, axis=1) for mat in mats]
    packed = np.concatenate([tile for mat in tiles for tile in mat], axis=0)
    shapes = [mat.shape for mat in mats]
    return packed.astype(ml_dtypes.bfloat16), shapes, np.repeat(twist, some, axis=1)


def dot32(a, b):
    return jnp.dot(a, b, preferred_element_type=jnp.float32)


def mixer_kernel(
    blocks,
    groups,
    tokens_hbm,
    causal_hbm,
    anti_hbm,
    conv_taps_hbm,
    skip_gain_hbm,
    twist_hbm,
    mats_hbm,
    w_in_hbm,
    w_out_hbm,
    out,
    causal,
    anti,
    conv_taps,
    skip_gain,
    twist,
    over_filt,
    over_sig,
    within,
    back,
    w_in,
    w_out,
    framed,
    edge_out,
    edge_in,
    filt_out,
    filt_in,
    sig_out,
    sig_in,
    ret_out,
    ret_in,
    spectrum,
    load_sem,
    edge_send,
    edge_recv,
    filt_send,
    filt_recv,
    sig_send,
    sig_recv,
    ret_send,
    ret_recv,
):
    f32, bf16 = jnp.float32, jnp.bfloat16
    width, depth = tokens_hbm.shape
    channels = w_out.shape[0]
    parts, _, some, _ = sig_out.shape
    tokens = framed.at[0:width]
    blk, fft = lax.axis_index("blk"), lax.axis_index("fft")
    me = blk * groups + fft
    levels = blocks // groups
    peers = []
    for turn in range(levels - 1, -1, -1):
        level = blk ^ turn
        for step in range(groups):
            if turn > 0 or step > 0:
                other = (fft + step) & (groups - 1)
                peers.append((level * groups + other, (level, other)))

    barrier = pltpu.get_barrier_semaphore()
    for _, coords in peers:
        pl.semaphore_signal(barrier, inc=1, device_id=coords, device_id_type=MESH)

    pairs = [
        (causal_hbm, causal),
        (anti_hbm, anti),
        (tokens_hbm, tokens),
        (w_in_hbm, w_in),
        (conv_taps_hbm, conv_taps),
        (skip_gain_hbm, skip_gain),
        (twist_hbm, twist),
        (w_out_hbm, w_out),
    ]
    taken = 0
    for mat in (over_filt, over_sig, within, back):
        tall, wide = mat.shape
        for start in range(0, wide, 128):
            pairs.append((mats_hbm.at[pl.ds(taken, tall)], mat.at[:, pl.ds(start, 128)]))
            taken += tall
    loads = [
        pltpu.make_async_copy(src, dst, load_sem.at[i]) for i, (src, dst) in enumerate(pairs)
    ]
    for load in loads:
        load.start()

    def send_all(src, dst, send_sem, recv_sem):
        for peer, coords in peers:
            pltpu.make_async_remote_copy(
                src_ref=src.at[peer],
                dst_ref=dst.at[me],
                send_sem=send_sem,
                recv_sem=recv_sem,
                device_id=coords,
                device_id_type=MESH,
            ).start()
        pltpu.make_async_copy(src.at[me], dst.at[me], recv_sem).start()

    def all_arrived(dst, recv_sem):
        pltpu.make_async_copy(dst, dst, recv_sem).wait()

    def sent(src, send_sem):
        most = src.at[pl.ds(0, blocks - 1)]
        pltpu.make_async_copy(most, most, send_sem).wait()

    def chunks(x):
        return x.T.reshape(blocks, parts, some, width)

    for load in loads[:3]:
        load.wait()
    edge_out[0] = tokens[width - 16 :, :].astype(f32)[15:16]
    edge_out[1] = tokens[0:16, :].astype(f32)[0:1]
    unused = (lax.broadcasted_iota(jnp.int32, anti.shape, 0) == 0) & (me == 0)
    causal_rows = chunks(causal[...].astype(f32))
    anti_rows = chunks(jnp.where(unused, 0.0, anti[...].astype(f32)))
    for part in range(parts):
        filt_out[part, :, 0:some, :] = causal_rows[:, part].astype(bf16)
        filt_out[part, :, some:, :] = anti_rows[:, part].astype(bf16)
    pl.semaphore_wait(barrier, blocks - 1)
    edges = [
        pltpu.make_async_remote_copy(
            src_ref=edge_out.at[i],
            dst_ref=edge_in.at[i],
            send_sem=edge_send.at[i],
            recv_sem=edge_recv.at[i],
            device_id=(at // groups, at % groups),
            device_id_type=MESH,
        )
        for i, at in enumerate(((me + 1) % blocks, (me + blocks - 1) % blocks))
    ]
    for edge in edges:
        edge.start()

    def send_part(bufs, part):
        src, dst, send_sem, recv_sem = bufs
        send_all(src.at[part], dst.at[part], send_sem.at[part], recv_sem.at[part])

    filt = (filt_out, filt_in, filt_send, filt_recv)
    sig = (sig_out, sig_in, sig_send, sig_recv)
    ret = (ret_out, ret_in, ret_send, ret_recv)
    send_part(filt, 0)

    for load in loads[3:5]:
        load.wait()
    for edge in edges:
        edge.wait()
    row16 = lax.broadcasted_iota(jnp.int32, (16, depth), 0)
    prev = jnp.where(me == 0, 0.0, edge_in[0])
    following = jnp.where(me == blocks - 1, 0.0, edge_in[1])
    framed[width:, :] = jnp.where(
        row16 == 0, prev, jnp.where(row16 == 1, following, 0.0)
    ).astype(bf16)
    row = lax.broadcasted_iota(jnp.int32, (width, channels), 0)

    def stream(which):
        cols = slice(which * channels, (which + 1) * channels)
        proj = dot32(framed[...], w_in[:, cols]).astype(bf16).astype(f32)
        here = proj[:width]
        before = jnp.where(row == 0, proj[width : width + 1], pltpu.roll(here, 1, 0))
        after = jnp.where(
            row == width - 1, proj[width + 1 : width + 2], pltpu.roll(here, width - 1, 0)
        )
        taps = conv_taps[:, cols]
        return taps[0:1] * before + taps[1:2] * here + taps[2:3] * after

    signal = stream(0) * stream(2)
    signal_rows = chunks(signal)
    for part in range(parts):
        sig_out[part] = signal_rows[:, part].astype(bf16)
        send_part(sig, part)
        if part + 1 < parts:
            send_part(filt, part + 1)

    for load in loads[5:]:
        load.wait()
    second = stream(1)
    direct = skip_gain[...] * signal
    cos, sin = twist[0], twist[1]
    half = blocks * some

    def twisted(real, imag, axis):
        return jnp.concatenate(
            [real * cos + imag * sin, imag * cos - real * sin], axis=axis
        ).astype(bf16)

    def forward(rows, mat):
        freq = dot32(mat[...], rows)
        return dot32(twisted(freq[:half], freq[half:], 1), within[...])

    for part in range(parts):
        all_arrived(filt_in.at[part], filt_recv.at[part])
        spectrum[...] = forward(filt_in[part].reshape(2 * half, width), over_filt)
        all_arrived(sig_in.at[part], sig_recv.at[part])
        freq = forward(sig_in[part].reshape(half, width), over_sig)
        s_real, s_imag = freq[:, :width], freq[:, width:]
        f_real, f_imag = spectrum[:, :width], spectrum[:, width:]
        product = jnp.concatenate(
            [s_real * f_real - s_imag * f_imag, -(s_real * f_imag + s_imag * f_real)],
            axis=1,
        )
        turned = dot32(product.astype(bf16), within[...])
        conv = dot32(back[...], twisted(turned[:, :width], turned[:, width:], 0))
        ret_out[part] = conv.astype(bf16).reshape(blocks, some, width)
        send_part(ret, part)

    for part in range(parts):
        all_arrived(ret_in.at[part], ret_recv.at[part])
    landed = jnp.concatenate([ret_in[part].astype(f32) for part in range(parts)], axis=1)
    convolved = landed.reshape(channels, width).T + direct
    out[...] = dot32((second * convolved).astype(bf16), w_out[...]).astype(bf16)
    for src, _, send_sem, _ in (filt, sig, ret):
        for part in range(parts):
            sent(src.at[part], send_sem.at[part])


def one_kernel(tokens, w_in, conv_taps, causal_taps, anticausal_taps, skip_gain, w_out):
    width, depth = tokens.shape
    channels = w_out.shape[0]
    groups = lax.axis_size("fft")
    blocks = lax.axis_size("blk") * groups
    parts = 2
    some = channels // blocks // parts
    packed, shapes, twist = grid_constants(blocks, width, some)
    f32, bf16 = jnp.float32, jnp.bfloat16
    vmem = pl.BlockSpec(memory_space=pltpu.VMEM)
    hbm = pl.BlockSpec(memory_space=pl.ANY)
    one = pltpu.SemaphoreType.DMA
    return pl.pallas_call(
        functools.partial(mixer_kernel, blocks, groups),
        out_shape=pltpu.VMEM((width, w_out.shape[1]), bf16),
        in_specs=[hbm] * 9,
        out_specs=vmem,
        scratch_shapes=[
            pltpu.VMEM(causal_taps.shape, bf16),
            pltpu.VMEM(anticausal_taps.shape, bf16),
            pltpu.VMEM(conv_taps.shape, f32),
            pltpu.VMEM((1, channels), f32),
            pltpu.VMEM(twist.shape, f32),
            pltpu.VMEM(shapes[0], bf16),
            pltpu.VMEM(shapes[1], bf16),
            pltpu.VMEM(shapes[2], bf16),
            pltpu.VMEM(shapes[3], bf16),
            pltpu.VMEM(w_in.shape, bf16),
            pltpu.VMEM(w_out.shape, bf16),
            pltpu.VMEM((width + 16, depth), bf16),
            pltpu.VMEM((2, 1, depth), f32),
            pltpu.VMEM((2, 1, depth), f32),
            pltpu.VMEM((parts, blocks, 2 * some, width), bf16),
            pltpu.VMEM((parts, blocks, 2 * some, width), bf16),
            pltpu.VMEM((parts, blocks, some, width), bf16),
            pltpu.VMEM((parts, blocks, some, width), bf16),
            pltpu.VMEM((parts, blocks, some, width), bf16),
            pltpu.VMEM((parts, blocks, some, width), bf16),
            pltpu.VMEM((some * blocks, 2 * width), f32),
            one((8 + sum(wide // 128 for _, wide in shapes),)),
            one((2,)),
            one((2,)),
            one((parts,)),
            one((parts,)),
            one((parts,)),
            one((parts,)),
            one((parts,)),
            one((parts,)),
        ],
        compiler_params=pltpu.CompilerParams(
            collective_id=0, has_side_effects=True, vmem_limit_bytes=62 * 2**20
        ),
    )(
        tokens,
        causal_taps,
        anticausal_taps,
        conv_taps,
        skip_gain[None, :],
        jnp.asarray(twist),
        jnp.asarray(packed),
        w_in,
        w_out,
    )


def mixer(tokens, w_in, conv_taps, causal_taps, anticausal_taps, skip_gain, w_out):
    devices = lax.axis_size("blk") * lax.axis_size("fft")
    fits = tokens.shape[0] == 128 and w_out.shape[0] == 16 * devices
    chosen = one_kernel if fits else body
    return chosen(tokens, w_in, conv_taps, causal_taps, anticausal_taps, skip_gain, w_out)


def solution(mesh):
    in_specs = (
        P(("blk", "fft"), None),
        P(),
        P(),
        P(("blk", "fft"), None),
        P(("blk", "fft"), None),
        P(),
        P(),
    )
    out_specs = P(("blk", "fft"), None)
    return jax.shard_map(mixer, mesh=mesh, in_specs=in_specs, out_specs=out_specs, check_vma=False)
```

```python
import functools
import math

import jax
import jax.numpy as jnp
import ml_dtypes
import numpy as np
from jax import lax
from jax.experimental import pallas as pl
from jax.experimental.pallas import tpu as pltpu
from jax.sharding import PartitionSpec as P

MESH = pl.DeviceIdType.MESH


def with_halo(cells, sides, width):
    for axis, dim in sides:
        count = lax.axis_size(axis)
        ends = count - 1
        head = lax.slice_in_dim(cells, 0, width, axis=dim)
        tail = lax.slice_in_dim(cells, cells.shape[dim] - width, cells.shape[dim], axis=dim)
        cells = jnp.concatenate(
            [
                lax.ppermute(tail, axis, [(i, (i + 1) % count) for i in range(ends)]),
                cells,
                lax.ppermute(head, axis, [((i + 1) % count, i) for i in range(ends)]),
            ],
            axis=dim,
        )
    return cells


def shortened(x):

    def short(part):
        return part.astype(jnp.bfloat16) if part.dtype == jnp.float32 else part

    return jax.tree.map(short, x)


def log_count(count):
    return count.bit_length() - 1


def dft_matrix(count, sign, scale):
    grid = jnp.arange(count, dtype=jnp.int32)
    angle = (
        sign * 2.0 * math.pi * (grid[:, None] * grid[None, :] % count).astype(jnp.float32) / count
    )
    return (jnp.cos(angle) * scale, jnp.sin(angle) * scale)


def local_convolution(signal_cols, causal_cols, anti_cols):
    seq_len = signal_cols.shape[0]
    width = signal_cols.shape[1]
    length = 2 * seq_len
    rows_p = 2 ** (log_count(length) // 2)
    cols_q = length // rows_p
    high = lax.Precision.HIGHEST
    p_real, p_imag = dft_matrix(rows_p, -1.0, 1.0)
    q_real, q_imag = dft_matrix(cols_q, -1.0, 1.0)
    pp_real, pp_imag = dft_matrix(rows_p, 1.0, 1.0 / length)
    qp_real, qp_imag = dft_matrix(cols_q, 1.0, 1.0)
    k_grid = jnp.arange(rows_p, dtype=jnp.int32)
    n_grid = jnp.arange(cols_q, dtype=jnp.int32)
    tw_angle = (
        -2.0 * math.pi * (k_grid[:, None] * n_grid[None, :] % length).astype(jnp.float32) / length
    )
    tw_cos = jnp.cos(tw_angle)
    tw_sin = jnp.sin(tw_angle)

    def forward(grid_rows):
        half = grid_rows.shape[1]
        b_real = jnp.einsum("kp,cpq->ckq", p_real[:, :half], grid_rows, precision=high)
        b_imag = jnp.einsum("kp,cpq->ckq", p_imag[:, :half], grid_rows, precision=high)
        c_real = b_real * tw_cos - b_imag * tw_sin
        c_imag = b_real * tw_sin + b_imag * tw_cos
        x_real = jnp.einsum("ckq,qr->ckr", c_real, q_real, precision=high) - jnp.einsum(
            "ckq,qr->ckr", c_imag, q_imag, precision=high
        )
        x_imag = jnp.einsum("ckq,qr->ckr", c_real, q_imag, precision=high) + jnp.einsum(
            "ckq,qr->ckr", c_imag, q_real, precision=high
        )
        return (x_real, x_imag)

    sig_grid = signal_cols.T.reshape(width, rows_p // 2, cols_q)
    filt_grid = jnp.concatenate([causal_cols, anti_cols], axis=0).T.reshape(width, rows_p, cols_q)
    s_real, s_imag = forward(sig_grid)
    f_real, f_imag = forward(filt_grid)
    y_real = s_real * f_real - s_imag * f_imag
    y_imag = s_real * f_imag + s_imag * f_real
    d_real = jnp.einsum("ckq,qr->ckr", y_real, qp_real, precision=high) - jnp.einsum(
        "ckq,qr->ckr", y_imag, qp_imag, precision=high
    )
    d_imag = jnp.einsum("ckq,qr->ckr", y_real, qp_imag, precision=high) + jnp.einsum(
        "ckq,qr->ckr", y_imag, qp_real, precision=high
    )
    e_real = d_real * tw_cos + d_imag * tw_sin
    e_imag = d_imag * tw_cos - d_real * tw_sin
    half_rows = rows_p // 2
    out_grid = jnp.einsum("nk,ckq->cnq", pp_real[:half_rows], e_real, precision=high) - jnp.einsum(
        "nk,ckq->cnq", pp_imag[:half_rows], e_imag, precision=high
    )
    return out_grid.reshape(width, seq_len).T


def body(tokens, w_in, conv_taps, causal_taps, anticausal_taps, skip_gain, w_out):
    tok_rows = tokens.shape[0]
    channels = w_out.shape[0]
    groups = lax.axis_size("fft")
    blk_index = lax.axis_index("blk")
    fft_index = lax.axis_index("fft")
    device_index = blk_index * groups + fft_index
    position = device_index * tok_rows + jnp.arange(tok_rows, dtype=jnp.int32)
    proj = jnp.dot(tokens, w_in, preferred_element_type=jnp.float32).astype(jnp.bfloat16)
    framed = with_halo(proj, ((("blk", "fft"), 0),), 1).astype(jnp.float32)
    short = conv_taps[0] * framed[:-2] + conv_taps[1] * framed[1:-1] + conv_taps[2] * framed[2:]
    first = short[:, :channels]
    second = short[:, channels : 2 * channels]
    value_part = short[:, 2 * channels :]
    signal = first * value_part
    anticausal = jnp.where(position[:, None] > 0, anticausal_taps.astype(jnp.float32), 0.0)
    causal = causal_taps.astype(jnp.float32)
    moved = (
        lax.all_to_all(
            signal.astype(jnp.bfloat16), "fft", split_axis=1, concat_axis=0, tiled=True
        ).astype(signal.dtype),
        lax.all_to_all(
            causal.astype(jnp.bfloat16), "fft", split_axis=1, concat_axis=0, tiled=True
        ).astype(causal.dtype),
        lax.all_to_all(
            anticausal.astype(jnp.bfloat16), "fft", split_axis=1, concat_axis=0, tiled=True
        ).astype(anticausal.dtype),
    )
    moved = (
        lax.all_to_all(
            moved[0].astype(jnp.bfloat16), "blk", split_axis=1, concat_axis=0, tiled=True
        ).astype(jnp.float32),
        lax.all_to_all(
            moved[1].astype(jnp.bfloat16), "blk", split_axis=1, concat_axis=0, tiled=True
        ).astype(jnp.float32),
        lax.all_to_all(
            moved[2].astype(jnp.bfloat16), "blk", split_axis=1, concat_axis=0, tiled=True
        ).astype(jnp.float32),
    )
    conv_cols = local_convolution(moved[0], moved[1], moved[2])
    returned = lax.all_to_all(
        shortened(conv_cols), "blk", split_axis=0, concat_axis=1, tiled=True
    ).astype(conv_cols.dtype)
    convolved = lax.all_to_all(
        shortened(returned), "fft", split_axis=0, concat_axis=1, tiled=True
    ).astype(returned.dtype)
    convolved = convolved + skip_gain * signal
    gated = (second * convolved).astype(jnp.bfloat16)
    return jnp.dot(gated, w_out, preferred_element_type=jnp.float32).astype(jnp.bfloat16)


def grid_constants(blocks, width, some):
    length = 2 * blocks * width
    half_freq = np.arange(blocks) + 0.5
    each = np.eye(some)
    rows = np.outer(half_freq, np.arange(2 * blocks)) * (2.0 * np.pi / (2 * blocks))
    flip = np.where(np.arange(2 * blocks) < blocks, 1.0, -1.0)
    across = np.concatenate([np.cos(rows), -np.sin(rows)], axis=0) * flip
    paired = across.reshape(2 * blocks, 2, blocks).transpose(0, 2, 1).reshape(across.shape)
    turn = np.outer(half_freq, np.arange(width)) * (2.0 * np.pi / length)
    twist = np.stack([np.cos(turn), np.sin(turn)]).astype(np.float32)
    grid = np.outer(np.arange(width), np.arange(width)) % width * (2.0 * np.pi / width)
    cos, sin = np.cos(grid), np.sin(grid)
    within = np.block([[cos, -sin], [sin, cos]])
    back = rows[:, :blocks].T
    back = np.concatenate([np.cos(back), np.sin(back)], axis=1) * (2.0 / length)
    mats = [np.kron(paired, each), np.kron(across[:, :blocks], each), within, np.kron(back, each)]
    tiles = [np.split(mat, mat.shape[1] // 128, axis=1) for mat in mats]
    packed = np.concatenate([tile for mat in tiles for tile in mat], axis=0)
    shapes = [mat.shape for mat in mats]
    return packed.astype(ml_dtypes.bfloat16), shapes, np.repeat(twist, some, axis=1)


def dot32(a, b):
    return jnp.dot(a, b, preferred_element_type=jnp.float32)


def mixer_kernel(
    blocks,
    groups,
    tokens_hbm,
    causal_hbm,
    anti_hbm,
    conv_taps_hbm,
    skip_gain_hbm,
    twist_hbm,
    mats_hbm,
    w_in_hbm,
    w_out_hbm,
    out,
    causal,
    anti,
    conv_taps,
    skip_gain,
    twist,
    over_filt,
    over_sig,
    within,
    back,
    w_in,
    w_out,
    framed,
    edge_out,
    edge_in,
    filt_out,
    filt_in,
    sig_out,
    sig_in,
    ret_out,
    ret_in,
    spectrum,
    load_sem,
    edge_send,
    edge_recv,
    filt_send,
    filt_recv,
    sig_send,
    sig_recv,
    ret_send,
    ret_recv,
):
    f32, bf16 = jnp.float32, jnp.bfloat16
    width, depth = tokens_hbm.shape
    channels = w_out.shape[0]
    parts, _, some, _ = sig_out.shape
    tokens = framed.at[0:width]
    blk, fft = lax.axis_index("blk"), lax.axis_index("fft")
    me = blk * groups + fft
    levels = blocks // groups
    peers = []
    for turn in range(levels - 1, -1, -1):
        level = blk ^ turn
        for step in range(groups):
            if turn > 0 or step > 0:
                other = (fft + step) & (groups - 1)
                peers.append((level * groups + other, (level, other)))

    barrier = pltpu.get_barrier_semaphore()
    for _, coords in peers:
        pl.semaphore_signal(barrier, inc=1, device_id=coords, device_id_type=MESH)

    pairs = [
        (causal_hbm, causal),
        (anti_hbm, anti),
        (tokens_hbm, tokens),
        (w_in_hbm, w_in),
        (conv_taps_hbm, conv_taps),
        (skip_gain_hbm, skip_gain),
        (twist_hbm, twist),
        (w_out_hbm, w_out),
    ]
    taken = 0
    for mat in (over_filt, over_sig, within, back):
        tall, wide = mat.shape
        for start in range(0, wide, 128):
            pairs.append((mats_hbm.at[pl.ds(taken, tall)], mat.at[:, pl.ds(start, 128)]))
            taken += tall
    loads = [
        pltpu.make_async_copy(src, dst, load_sem.at[i]) for i, (src, dst) in enumerate(pairs)
    ]
    for load in loads:
        load.start()

    def send_all(src, dst, send_sem, recv_sem):
        for peer, coords in peers:
            pltpu.make_async_remote_copy(
                src_ref=src.at[peer],
                dst_ref=dst.at[me],
                send_sem=send_sem,
                recv_sem=recv_sem,
                device_id=coords,
                device_id_type=MESH,
            ).start()
        pltpu.make_async_copy(src.at[me], dst.at[me], recv_sem).start()

    def all_arrived(dst, recv_sem):
        pltpu.make_async_copy(dst, dst, recv_sem).wait()

    def sent(src, send_sem):
        most = src.at[pl.ds(0, blocks - 1)]
        pltpu.make_async_copy(most, most, send_sem).wait()

    def chunks(x):
        return x.T.reshape(blocks, parts, some, width)

    for load in loads[:3]:
        load.wait()
    edge_out[0] = tokens[width - 16 :, :].astype(f32)[15:16]
    edge_out[1] = tokens[0:16, :].astype(f32)[0:1]
    unused = (lax.broadcasted_iota(jnp.int32, anti.shape, 0) == 0) & (me == 0)
    causal_rows = chunks(causal[...].astype(f32))
    anti_rows = chunks(jnp.where(unused, 0.0, anti[...].astype(f32)))
    for part in range(parts):
        filt_out[part, :, 0:some, :] = causal_rows[:, part].astype(bf16)
        filt_out[part, :, some:, :] = anti_rows[:, part].astype(bf16)
    pl.semaphore_wait(barrier, blocks - 1)
    edges = [
        pltpu.make_async_remote_copy(
            src_ref=edge_out.at[i],
            dst_ref=edge_in.at[i],
            send_sem=edge_send.at[i],
            recv_sem=edge_recv.at[i],
            device_id=(at // groups, at % groups),
            device_id_type=MESH,
        )
        for i, at in enumerate(((me + 1) % blocks, (me + blocks - 1) % blocks))
    ]
    for edge in edges:
        edge.start()

    def send_part(bufs, part):
        src, dst, send_sem, recv_sem = bufs
        send_all(src.at[part], dst.at[part], send_sem.at[part], recv_sem.at[part])

    filt = (filt_out, filt_in, filt_send, filt_recv)
    sig = (sig_out, sig_in, sig_send, sig_recv)
    ret = (ret_out, ret_in, ret_send, ret_recv)
    send_part(filt, 0)

    for load in loads[3:5]:
        load.wait()
    for edge in edges:
        edge.wait()
    row16 = lax.broadcasted_iota(jnp.int32, (16, depth), 0)
    prev = jnp.where(me == 0, 0.0, edge_in[0])
    following = jnp.where(me == blocks - 1, 0.0, edge_in[1])
    framed[width:, :] = jnp.where(
        row16 == 0, prev, jnp.where(row16 == 1, following, 0.0)
    ).astype(bf16)
    row = lax.broadcasted_iota(jnp.int32, (width, channels), 0)

    def stream(which):
        cols = slice(which * channels, (which + 1) * channels)
        proj = dot32(framed[...], w_in[:, cols]).astype(bf16).astype(f32)
        here = proj[:width]
        before = jnp.where(row == 0, proj[width : width + 1], pltpu.roll(here, 1, 0))
        after = jnp.where(
            row == width - 1, proj[width + 1 : width + 2], pltpu.roll(here, width - 1, 0)
        )
        taps = conv_taps[:, cols]
        return taps[0:1] * before + taps[1:2] * here + taps[2:3] * after

    signal = stream(0) * stream(2)
    signal_rows = chunks(signal)
    for part in range(parts):
        sig_out[part] = signal_rows[:, part].astype(bf16)
        send_part(sig, part)
        if part + 1 < parts:
            send_part(filt, part + 1)

    for load in loads[5:]:
        load.wait()
    second = stream(1)
    direct = skip_gain[...] * signal
    cos, sin = twist[0], twist[1]
    half = blocks * some

    def twisted(real, imag, axis):
        return jnp.concatenate(
            [real * cos + imag * sin, imag * cos - real * sin], axis=axis
        ).astype(bf16)

    def forward(rows, mat):
        freq = dot32(mat[...], rows)
        return dot32(twisted(freq[:half], freq[half:], 1), within[...])

    for part in range(parts):
        all_arrived(filt_in.at[part], filt_recv.at[part])
        spectrum[...] = forward(filt_in[part].reshape(2 * half, width), over_filt)
        all_arrived(sig_in.at[part], sig_recv.at[part])
        freq = forward(sig_in[part].reshape(half, width), over_sig)
        s_real, s_imag = freq[:, :width], freq[:, width:]
        f_real, f_imag = spectrum[:, :width], spectrum[:, width:]
        product = jnp.concatenate(
            [s_real * f_real - s_imag * f_imag, -(s_real * f_imag + s_imag * f_real)],
            axis=1,
        )
        turned = dot32(product.astype(bf16), within[...])
        conv = dot32(back[...], twisted(turned[:, :width], turned[:, width:], 0))
        ret_out[part] = conv.astype(bf16).reshape(blocks, some, width)
        send_part(ret, part)

    for part in range(parts):
        all_arrived(ret_in.at[part], ret_recv.at[part])
    landed = jnp.concatenate([ret_in[part].astype(f32) for part in range(parts)], axis=1)
    convolved = landed.reshape(channels, width).T + direct
    out[...] = dot32((second * convolved).astype(bf16), w_out[...]).astype(bf16)
    for src, _, send_sem, _ in (filt, sig, ret):
        for part in range(parts):
            sent(src.at[part], send_sem.at[part])


def one_kernel(tokens, w_in, conv_taps, causal_taps, anticausal_taps, skip_gain, w_out):
    width, depth = tokens.shape
    channels = w_out.shape[0]
    groups = lax.axis_size("fft")
    blocks = lax.axis_size("blk") * groups
    parts = 1
    some = channels // blocks // parts
    packed, shapes, twist = grid_constants(blocks, width, some)
    f32, bf16 = jnp.float32, jnp.bfloat16
    vmem = pl.BlockSpec(memory_space=pltpu.VMEM)
    hbm = pl.BlockSpec(memory_space=pl.ANY)
    one = pltpu.SemaphoreType.DMA
    return pl.pallas_call(
        functools.partial(mixer_kernel, blocks, groups),
        out_shape=pltpu.VMEM((width, w_out.shape[1]), bf16),
        in_specs=[hbm] * 9,
        out_specs=vmem,
        scratch_shapes=[
            pltpu.VMEM(causal_taps.shape, bf16),
            pltpu.VMEM(anticausal_taps.shape, bf16),
            pltpu.VMEM(conv_taps.shape, f32),
            pltpu.VMEM((1, channels), f32),
            pltpu.VMEM(twist.shape, f32),
            pltpu.VMEM(shapes[0], bf16),
            pltpu.VMEM(shapes[1], bf16),
            pltpu.VMEM(shapes[2], bf16),
            pltpu.VMEM(shapes[3], bf16),
            pltpu.VMEM(w_in.shape, bf16),
            pltpu.VMEM(w_out.shape, bf16),
            pltpu.VMEM((width + 16, depth), bf16),
            pltpu.VMEM((2, 1, depth), f32),
            pltpu.VMEM((2, 1, depth), f32),
            pltpu.VMEM((parts, blocks, 2 * some, width), bf16),
            pltpu.VMEM((parts, blocks, 2 * some, width), bf16),
            pltpu.VMEM((parts, blocks, some, width), bf16),
            pltpu.VMEM((parts, blocks, some, width), bf16),
            pltpu.VMEM((parts, blocks, some, width), bf16),
            pltpu.VMEM((parts, blocks, some, width), bf16),
            pltpu.VMEM((some * blocks, 2 * width), f32),
            one((8 + sum(wide // 128 for _, wide in shapes),)),
            one((2,)),
            one((2,)),
            one((parts,)),
            one((parts,)),
            one((parts,)),
            one((parts,)),
            one((parts,)),
            one((parts,)),
        ],
        compiler_params=pltpu.CompilerParams(
            collective_id=0, has_side_effects=True, vmem_limit_bytes=62 * 2**20
        ),
    )(
        tokens,
        causal_taps,
        anticausal_taps,
        conv_taps,
        skip_gain[None, :],
        jnp.asarray(twist),
        jnp.asarray(packed),
        w_in,
        w_out,
    )


def mixer(tokens, w_in, conv_taps, causal_taps, anticausal_taps, skip_gain, w_out):
    devices = lax.axis_size("blk") * lax.axis_size("fft")
    fits = tokens.shape[0] == 128 and w_out.shape[0] == 16 * devices
    chosen = one_kernel if fits else body
    return chosen(tokens, w_in, conv_taps, causal_taps, anticausal_taps, skip_gain, w_out)


def solution(mesh):
    in_specs = (
        P(("blk", "fft"), None),
        P(),
        P(),
        P(("blk", "fft"), None),
        P(("blk", "fft"), None),
        P(),
        P(),
    )
    out_specs = P(("blk", "fft"), None)
    return jax.shard_map(mixer, mesh=mesh, in_specs=in_specs, out_specs=out_specs, check_vma=False)
```

```python
import functools
import math

import jax
import jax.numpy as jnp
import ml_dtypes
import numpy as np
from jax import lax
from jax.experimental import pallas as pl
from jax.experimental.pallas import tpu as pltpu
from jax.sharding import PartitionSpec as P

MESH = pl.DeviceIdType.MESH


def with_halo(cells, sides, width):
    for axis, dim in sides:
        count = lax.axis_size(axis)
        ends = count - 1
        head = lax.slice_in_dim(cells, 0, width, axis=dim)
        tail = lax.slice_in_dim(cells, cells.shape[dim] - width, cells.shape[dim], axis=dim)
        cells = jnp.concatenate(
            [
                lax.ppermute(tail, axis, [(i, (i + 1) % count) for i in range(ends)]),
                cells,
                lax.ppermute(head, axis, [((i + 1) % count, i) for i in range(ends)]),
            ],
            axis=dim,
        )
    return cells


def shortened(x):

    def short(part):
        return part.astype(jnp.bfloat16) if part.dtype == jnp.float32 else part

    return jax.tree.map(short, x)


def log_count(count):
    return count.bit_length() - 1


def dft_matrix(count, sign, scale):
    grid = jnp.arange(count, dtype=jnp.int32)
    angle = (
        sign * 2.0 * math.pi * (grid[:, None] * grid[None, :] % count).astype(jnp.float32) / count
    )
    return (jnp.cos(angle) * scale, jnp.sin(angle) * scale)


def local_convolution(signal_cols, causal_cols, anti_cols):
    seq_len = signal_cols.shape[0]
    width = signal_cols.shape[1]
    length = 2 * seq_len
    rows_p = 2 ** (log_count(length) // 2)
    cols_q = length // rows_p
    high = lax.Precision.HIGHEST
    p_real, p_imag = dft_matrix(rows_p, -1.0, 1.0)
    q_real, q_imag = dft_matrix(cols_q, -1.0, 1.0)
    pp_real, pp_imag = dft_matrix(rows_p, 1.0, 1.0 / length)
    qp_real, qp_imag = dft_matrix(cols_q, 1.0, 1.0)
    k_grid = jnp.arange(rows_p, dtype=jnp.int32)
    n_grid = jnp.arange(cols_q, dtype=jnp.int32)
    tw_angle = (
        -2.0 * math.pi * (k_grid[:, None] * n_grid[None, :] % length).astype(jnp.float32) / length
    )
    tw_cos = jnp.cos(tw_angle)
    tw_sin = jnp.sin(tw_angle)

    def forward(grid_rows):
        half = grid_rows.shape[1]
        b_real = jnp.einsum("kp,cpq->ckq", p_real[:, :half], grid_rows, precision=high)
        b_imag = jnp.einsum("kp,cpq->ckq", p_imag[:, :half], grid_rows, precision=high)
        c_real = b_real * tw_cos - b_imag * tw_sin
        c_imag = b_real * tw_sin + b_imag * tw_cos
        x_real = jnp.einsum("ckq,qr->ckr", c_real, q_real, precision=high) - jnp.einsum(
            "ckq,qr->ckr", c_imag, q_imag, precision=high
        )
        x_imag = jnp.einsum("ckq,qr->ckr", c_real, q_imag, precision=high) + jnp.einsum(
            "ckq,qr->ckr", c_imag, q_real, precision=high
        )
        return (x_real, x_imag)

    sig_grid = signal_cols.T.reshape(width, rows_p // 2, cols_q)
    filt_grid = jnp.concatenate([causal_cols, anti_cols], axis=0).T.reshape(width, rows_p, cols_q)
    s_real, s_imag = forward(sig_grid)
    f_real, f_imag = forward(filt_grid)
    y_real = s_real * f_real - s_imag * f_imag
    y_imag = s_real * f_imag + s_imag * f_real
    d_real = jnp.einsum("ckq,qr->ckr", y_real, qp_real, precision=high) - jnp.einsum(
        "ckq,qr->ckr", y_imag, qp_imag, precision=high
    )
    d_imag = jnp.einsum("ckq,qr->ckr", y_real, qp_imag, precision=high) + jnp.einsum(
        "ckq,qr->ckr", y_imag, qp_real, precision=high
    )
    e_real = d_real * tw_cos + d_imag * tw_sin
    e_imag = d_imag * tw_cos - d_real * tw_sin
    half_rows = rows_p // 2
    out_grid = jnp.einsum("nk,ckq->cnq", pp_real[:half_rows], e_real, precision=high) - jnp.einsum(
        "nk,ckq->cnq", pp_imag[:half_rows], e_imag, precision=high
    )
    return out_grid.reshape(width, seq_len).T


def body(tokens, w_in, conv_taps, causal_taps, anticausal_taps, skip_gain, w_out):
    tok_rows = tokens.shape[0]
    channels = w_out.shape[0]
    groups = lax.axis_size("fft")
    blk_index = lax.axis_index("blk")
    fft_index = lax.axis_index("fft")
    device_index = blk_index * groups + fft_index
    position = device_index * tok_rows + jnp.arange(tok_rows, dtype=jnp.int32)
    proj = jnp.dot(tokens, w_in, preferred_element_type=jnp.float32).astype(jnp.bfloat16)
    framed = with_halo(proj, ((("blk", "fft"), 0),), 1).astype(jnp.float32)
    short = conv_taps[0] * framed[:-2] + conv_taps[1] * framed[1:-1] + conv_taps[2] * framed[2:]
    first = short[:, :channels]
    second = short[:, channels : 2 * channels]
    value_part = short[:, 2 * channels :]
    signal = first * value_part
    anticausal = jnp.where(position[:, None] > 0, anticausal_taps.astype(jnp.float32), 0.0)
    causal = causal_taps.astype(jnp.float32)
    moved = (
        lax.all_to_all(
            signal.astype(jnp.bfloat16), "fft", split_axis=1, concat_axis=0, tiled=True
        ).astype(signal.dtype),
        lax.all_to_all(
            causal.astype(jnp.bfloat16), "fft", split_axis=1, concat_axis=0, tiled=True
        ).astype(causal.dtype),
        lax.all_to_all(
            anticausal.astype(jnp.bfloat16), "fft", split_axis=1, concat_axis=0, tiled=True
        ).astype(anticausal.dtype),
    )
    moved = (
        lax.all_to_all(
            moved[0].astype(jnp.bfloat16), "blk", split_axis=1, concat_axis=0, tiled=True
        ).astype(jnp.float32),
        lax.all_to_all(
            moved[1].astype(jnp.bfloat16), "blk", split_axis=1, concat_axis=0, tiled=True
        ).astype(jnp.float32),
        lax.all_to_all(
            moved[2].astype(jnp.bfloat16), "blk", split_axis=1, concat_axis=0, tiled=True
        ).astype(jnp.float32),
    )
    conv_cols = local_convolution(moved[0], moved[1], moved[2])
    returned = lax.all_to_all(
        shortened(conv_cols), "blk", split_axis=0, concat_axis=1, tiled=True
    ).astype(conv_cols.dtype)
    convolved = lax.all_to_all(
        shortened(returned), "fft", split_axis=0, concat_axis=1, tiled=True
    ).astype(returned.dtype)
    convolved = convolved + skip_gain * signal
    gated = (second * convolved).astype(jnp.bfloat16)
    return jnp.dot(gated, w_out, preferred_element_type=jnp.float32).astype(jnp.bfloat16)


def grid_constants(blocks, width):
    length = 2 * blocks * width
    half_freq = np.arange(blocks) + 0.5

    rows = np.outer(half_freq, np.arange(2 * blocks)) * (2.0 * np.pi / (2 * blocks))
    flip = np.where(np.arange(2 * blocks) < blocks, 1.0, -1.0)
    across = np.concatenate([np.cos(rows), -np.sin(rows)], axis=0) * flip
    across = across.astype(ml_dtypes.bfloat16)
    turn = np.outer(half_freq, np.arange(width)) * (2.0 * np.pi / length)
    twist = np.stack([np.cos(turn), np.sin(turn)]).astype(np.float32)
    grid = np.outer(np.arange(width), np.arange(width)) % width * (2.0 * np.pi / width)
    cos, sin = np.cos(grid), np.sin(grid)
    within = np.block([[cos, -sin], [sin, cos]]).astype(np.float32)
    back = rows[:, :blocks].T
    back = np.concatenate([np.cos(back), np.sin(back)], axis=1) * (2.0 / length)
    back = back.astype(ml_dtypes.bfloat16)
    return across, twist, within, back


def dot32(a, b):
    return jnp.dot(a, b, preferred_element_type=jnp.float32)


def mixer_kernel(
    blocks,
    groups,
    tokens_hbm,
    causal_hbm,
    anti_hbm,
    conv_taps_hbm,
    skip_gain_hbm,
    across_hbm,
    twist_hbm,
    back_hbm,
    w_in_hbm,
    w_out_hbm,
    within_hbm,
    out,
    causal,
    anti,
    conv_taps,
    skip_gain,
    across,
    twist,
    back,
    w_in,
    w_out,
    within_whole,
    within,
    framed,
    edge_out,
    edge_in,
    filt_out,
    filt_in,
    sig_out,
    sig_in,
    ret_out,
    ret_in,
    spread,
    gather,
    result,
    spectrum,
    load_sem,
    edge_send,
    edge_recv,
    filt_send,
    filt_recv,
    sig_send,
    sig_recv,
    ret_send,
    ret_recv,
):
    f32, bf16 = jnp.float32, jnp.bfloat16
    width, depth = tokens_hbm.shape
    channels = w_out.shape[0]
    parts, _, some, _ = sig_out.shape
    tokens = framed.at[0:width]
    blk, fft = lax.axis_index("blk"), lax.axis_index("fft")
    me = blk * groups + fft
    levels = blocks // groups
    peers = []
    for turn in range(levels - 1, -1, -1):
        level = blk ^ turn
        for step in range(groups):
            if turn > 0 or step > 0:
                other = (fft + step) & (groups - 1)
                peers.append((level * groups + other, (level, other)))

    barrier = pltpu.get_barrier_semaphore()
    for _, coords in peers:
        pl.semaphore_signal(barrier, inc=1, device_id=coords, device_id_type=MESH)

    loads = [
        pltpu.make_async_copy(src, dst, load_sem.at[i])
        for i, (src, dst) in enumerate(
            (
                (causal_hbm, causal),
                (anti_hbm, anti),
                (tokens_hbm, tokens),
                (w_in_hbm, w_in),
                (conv_taps_hbm, conv_taps),
                (across_hbm, across),
                (twist_hbm, twist),
                (within_hbm, within_whole),
                (back_hbm, back),
                (w_out_hbm, w_out),
                (skip_gain_hbm, skip_gain),
            )
        )
    ]
    for load in loads:
        load.start()

    def send_all(src, dst, send_sem, recv_sem):
        for peer, coords in peers:
            pltpu.make_async_remote_copy(
                src_ref=src.at[peer],
                dst_ref=dst.at[me],
                send_sem=send_sem,
                recv_sem=recv_sem,
                device_id=coords,
                device_id_type=MESH,
            ).start()
        pltpu.make_async_copy(src.at[me], dst.at[me], recv_sem).start()

    def all_arrived(dst, recv_sem):
        pltpu.make_async_copy(dst, dst, recv_sem).wait()

    def sent(src, send_sem):
        most = src.at[pl.ds(0, blocks - 1)]
        pltpu.make_async_copy(most, most, send_sem).wait()

    def chunks(x):
        return x.T.reshape(blocks, parts, some, width)

    for load in loads[:3]:
        load.wait()
    edge_out[0] = tokens[width - 16 :, :].astype(f32)[15:16]
    edge_out[1] = tokens[0:16, :].astype(f32)[0:1]
    unused = (lax.broadcasted_iota(jnp.int32, anti.shape, 0) == 0) & (me == 0)
    causal_rows = chunks(causal[...].astype(f32))
    anti_rows = chunks(jnp.where(unused, 0.0, anti[...].astype(f32)))
    for part in range(parts):
        filt_out[part, :, 0:some, :] = causal_rows[:, part].astype(bf16)
        filt_out[part, :, some:, :] = anti_rows[:, part].astype(bf16)
    pl.semaphore_wait(barrier, blocks - 1)
    edges = [
        pltpu.make_async_remote_copy(
            src_ref=edge_out.at[i],
            dst_ref=edge_in.at[i],
            send_sem=edge_send.at[i],
            recv_sem=edge_recv.at[i],
            device_id=(at // groups, at % groups),
            device_id_type=MESH,
        )
        for i, at in enumerate(((me + 1) % blocks, (me + blocks - 1) % blocks))
    ]
    for edge in edges:
        edge.start()

    def send_part(bufs, part):
        src, dst, send_sem, recv_sem = bufs
        send_all(src.at[part], dst.at[part], send_sem.at[part], recv_sem.at[part])

    filt = (filt_out, filt_in, filt_send, filt_recv)
    sig = (sig_out, sig_in, sig_send, sig_recv)
    ret = (ret_out, ret_in, ret_send, ret_recv)
    send_part(filt, 0)

    for load in loads[3:5]:
        load.wait()
    for edge in edges:
        edge.wait()
    row16 = lax.broadcasted_iota(jnp.int32, (16, depth), 0)
    prev = jnp.where(me == 0, 0.0, edge_in[0])
    following = jnp.where(me == blocks - 1, 0.0, edge_in[1])
    framed[width:, :] = jnp.where(
        row16 == 0, prev, jnp.where(row16 == 1, following, 0.0)
    ).astype(bf16)
    row = lax.broadcasted_iota(jnp.int32, (width, channels), 0)

    def stream(which):
        cols = slice(which * channels, (which + 1) * channels)
        proj = dot32(framed[...], w_in[:, cols]).astype(bf16).astype(f32)
        here = proj[:width]
        before = jnp.where(row == 0, proj[width : width + 1], pltpu.roll(here, 1, 0))
        after = jnp.where(
            row == width - 1, proj[width + 1 : width + 2], pltpu.roll(here, width - 1, 0)
        )
        taps = conv_taps[:, cols]
        return taps[0:1] * before + taps[1:2] * here + taps[2:3] * after

    signal = stream(0) * stream(2)
    signal_rows = chunks(signal)
    for part in range(parts):
        sig_out[part] = signal_rows[:, part].astype(bf16)
        send_part(sig, part)
        if part + 1 < parts:
            send_part(filt, part + 1)

    for load in loads[5:]:
        load.wait()
    second = stream(1)
    direct = skip_gain[...] * signal
    within[...] = within_whole[...].astype(bf16)
    cos, sin = twist[0], twist[1]

    def twisted(real, imag, axis):
        return jnp.concatenate([real * cos + imag * sin, imag * cos - real * sin], axis=axis)

    def lane(x, c):
        return x[:, c * width : (c + 1) * width]

    def forward(columns, mats):
        freq = dot32(mats, jnp.concatenate(columns, axis=1))
        turned = [
            twisted(lane(freq[:blocks], c), lane(freq[blocks:], c), 1)
            for c in range(len(columns))
        ]
        return dot32(jnp.concatenate(turned, axis=0).astype(bf16), within[...])

    for part in range(parts):
        all_arrived(filt_in.at[part], filt_recv.at[part])
        spread[...] = filt_in[part].astype(f32).reshape(2 * blocks * some, width)
        columns = [
            jnp.concatenate(
                [
                    spread[pl.ds(c, blocks, stride=2 * some), :],
                    spread[pl.ds(some + c, blocks, stride=2 * some), :],
                ],
                axis=0,
            ).astype(bf16)
            for c in range(some)
        ]
        spectrum[...] = forward(columns, across[...])

        all_arrived(sig_in.at[part], sig_recv.at[part])
        gather[...] = sig_in[part].astype(f32).reshape(blocks * some, width)
        columns = [
            gather[pl.ds(c, blocks, stride=some), :].astype(bf16) for c in range(some)
        ]
        freq = forward(columns, across[:, 0:blocks])
        s_real, s_imag = freq[:, :width], freq[:, width:]
        f_real, f_imag = spectrum[:, :width], spectrum[:, width:]
        product = jnp.concatenate(
            [s_real * f_real - s_imag * f_imag, -(s_real * f_imag + s_imag * f_real)],
            axis=1,
        )
        turned = dot32(product.astype(bf16), within[...])
        pieces = [turned[i * blocks : (i + 1) * blocks] for i in range(some)]
        pieces = [twisted(x[:, :width], x[:, width:], 0) for x in pieces]
        conv = dot32(back[...], jnp.concatenate(pieces, axis=1).astype(bf16))
        for c in range(some):
            result[pl.ds(c, blocks, stride=some), :] = lane(conv, c)
        ret_out[part] = result[...].astype(bf16).reshape(blocks, some, width)
        send_part(ret, part)

    for part in range(parts):
        all_arrived(ret_in.at[part], ret_recv.at[part])
    landed = jnp.concatenate([ret_in[part].astype(f32) for part in range(parts)], axis=1)
    convolved = landed.reshape(channels, width).T + direct
    out[...] = dot32((second * convolved).astype(bf16), w_out[...]).astype(bf16)
    for src, _, send_sem, _ in (filt, sig, ret):
        for part in range(parts):
            sent(src.at[part], send_sem.at[part])


def one_kernel(tokens, w_in, conv_taps, causal_taps, anticausal_taps, skip_gain, w_out):
    width, depth = tokens.shape
    channels = w_out.shape[0]
    groups = lax.axis_size("fft")
    blocks = lax.axis_size("blk") * groups
    parts = 2
    some = channels // blocks // parts
    across, twist, within, back = grid_constants(blocks, width)
    f32, bf16 = jnp.float32, jnp.bfloat16
    vmem = pl.BlockSpec(memory_space=pltpu.VMEM)
    hbm = pl.BlockSpec(memory_space=pl.ANY)
    one = pltpu.SemaphoreType.DMA
    return pl.pallas_call(
        functools.partial(mixer_kernel, blocks, groups),
        out_shape=pltpu.VMEM((width, w_out.shape[1]), bf16),
        in_specs=[hbm] * 11,
        out_specs=vmem,
        scratch_shapes=[
            pltpu.VMEM(causal_taps.shape, bf16),
            pltpu.VMEM(anticausal_taps.shape, bf16),
            pltpu.VMEM(conv_taps.shape, f32),
            pltpu.VMEM((1, channels), f32),
            pltpu.VMEM(across.shape, bf16),
            pltpu.VMEM(twist.shape, f32),
            pltpu.VMEM(back.shape, bf16),
            pltpu.VMEM(w_in.shape, bf16),
            pltpu.VMEM(w_out.shape, bf16),
            pltpu.VMEM(within.shape, f32),
            pltpu.VMEM(within.shape, bf16),
            pltpu.VMEM((width + 16, depth), bf16),
            pltpu.VMEM((2, 1, depth), f32),
            pltpu.VMEM((2, 1, depth), f32),
            pltpu.VMEM((parts, blocks, 2 * some, width), bf16),
            pltpu.VMEM((parts, blocks, 2 * some, width), bf16),
            pltpu.VMEM((parts, blocks, some, width), bf16),
            pltpu.VMEM((parts, blocks, some, width), bf16),
            pltpu.VMEM((parts, blocks, some, width), bf16),
            pltpu.VMEM((parts, blocks, some, width), bf16),
            pltpu.VMEM((2 * blocks * some, width), f32),
            pltpu.VMEM((blocks * some, width), f32),
            pltpu.VMEM((blocks * some, width), f32),
            pltpu.VMEM((some * blocks, 2 * width), f32),
            one((11,)),
            one((2,)),
            one((2,)),
            one((parts,)),
            one((parts,)),
            one((parts,)),
            one((parts,)),
            one((parts,)),
            one((parts,)),
        ],
        compiler_params=pltpu.CompilerParams(
            collective_id=0, has_side_effects=True, vmem_limit_bytes=62 * 2**20
        ),
    )(
        tokens,
        causal_taps,
        anticausal_taps,
        conv_taps,
        skip_gain[None, :],
        jnp.asarray(across),
        jnp.asarray(twist),
        jnp.asarray(back),
        w_in,
        w_out,
        jnp.asarray(within),
    )


def mixer(tokens, w_in, conv_taps, causal_taps, anticausal_taps, skip_gain, w_out):
    devices = lax.axis_size("blk") * lax.axis_size("fft")
    fits = tokens.shape[0] == 128 and w_out.shape[0] == 16 * devices
    chosen = one_kernel if fits else body
    return chosen(tokens, w_in, conv_taps, causal_taps, anticausal_taps, skip_gain, w_out)


def solution(mesh):
    in_specs = (
        P(("blk", "fft"), None),
        P(),
        P(),
        P(("blk", "fft"), None),
        P(("blk", "fft"), None),
        P(),
        P(),
    )
    out_specs = P(("blk", "fft"), None)
    return jax.shard_map(mixer, mesh=mesh, in_specs=in_specs, out_specs=out_specs, check_vma=False)
```

```python
import functools
import math

import jax
import jax.numpy as jnp
import ml_dtypes
import numpy as np
from jax import lax
from jax.experimental import pallas as pl
from jax.experimental.pallas import tpu as pltpu
from jax.sharding import PartitionSpec as P

MESH = pl.DeviceIdType.MESH


def with_halo(cells, sides, width):
    for axis, dim in sides:
        count = lax.axis_size(axis)
        ends = count - 1
        head = lax.slice_in_dim(cells, 0, width, axis=dim)
        tail = lax.slice_in_dim(cells, cells.shape[dim] - width, cells.shape[dim], axis=dim)
        cells = jnp.concatenate(
            [
                lax.ppermute(tail, axis, [(i, (i + 1) % count) for i in range(ends)]),
                cells,
                lax.ppermute(head, axis, [((i + 1) % count, i) for i in range(ends)]),
            ],
            axis=dim,
        )
    return cells


def shortened(x):

    def short(part):
        return part.astype(jnp.bfloat16) if part.dtype == jnp.float32 else part

    return jax.tree.map(short, x)


def log_count(count):
    return count.bit_length() - 1


def dft_matrix(count, sign, scale):
    grid = jnp.arange(count, dtype=jnp.int32)
    angle = (
        sign * 2.0 * math.pi * (grid[:, None] * grid[None, :] % count).astype(jnp.float32) / count
    )
    return (jnp.cos(angle) * scale, jnp.sin(angle) * scale)


def local_convolution(signal_cols, causal_cols, anti_cols):
    seq_len = signal_cols.shape[0]
    width = signal_cols.shape[1]
    length = 2 * seq_len
    rows_p = 2 ** (log_count(length) // 2)
    cols_q = length // rows_p
    high = lax.Precision.HIGHEST
    p_real, p_imag = dft_matrix(rows_p, -1.0, 1.0)
    q_real, q_imag = dft_matrix(cols_q, -1.0, 1.0)
    pp_real, pp_imag = dft_matrix(rows_p, 1.0, 1.0 / length)
    qp_real, qp_imag = dft_matrix(cols_q, 1.0, 1.0)
    k_grid = jnp.arange(rows_p, dtype=jnp.int32)
    n_grid = jnp.arange(cols_q, dtype=jnp.int32)
    tw_angle = (
        -2.0 * math.pi * (k_grid[:, None] * n_grid[None, :] % length).astype(jnp.float32) / length
    )
    tw_cos = jnp.cos(tw_angle)
    tw_sin = jnp.sin(tw_angle)

    def forward(grid_rows):
        half = grid_rows.shape[1]
        b_real = jnp.einsum("kp,cpq->ckq", p_real[:, :half], grid_rows, precision=high)
        b_imag = jnp.einsum("kp,cpq->ckq", p_imag[:, :half], grid_rows, precision=high)
        c_real = b_real * tw_cos - b_imag * tw_sin
        c_imag = b_real * tw_sin + b_imag * tw_cos
        x_real = jnp.einsum("ckq,qr->ckr", c_real, q_real, precision=high) - jnp.einsum(
            "ckq,qr->ckr", c_imag, q_imag, precision=high
        )
        x_imag = jnp.einsum("ckq,qr->ckr", c_real, q_imag, precision=high) + jnp.einsum(
            "ckq,qr->ckr", c_imag, q_real, precision=high
        )
        return (x_real, x_imag)

    sig_grid = signal_cols.T.reshape(width, rows_p // 2, cols_q)
    filt_grid = jnp.concatenate([causal_cols, anti_cols], axis=0).T.reshape(width, rows_p, cols_q)
    s_real, s_imag = forward(sig_grid)
    f_real, f_imag = forward(filt_grid)
    y_real = s_real * f_real - s_imag * f_imag
    y_imag = s_real * f_imag + s_imag * f_real
    d_real = jnp.einsum("ckq,qr->ckr", y_real, qp_real, precision=high) - jnp.einsum(
        "ckq,qr->ckr", y_imag, qp_imag, precision=high
    )
    d_imag = jnp.einsum("ckq,qr->ckr", y_real, qp_imag, precision=high) + jnp.einsum(
        "ckq,qr->ckr", y_imag, qp_real, precision=high
    )
    e_real = d_real * tw_cos + d_imag * tw_sin
    e_imag = d_imag * tw_cos - d_real * tw_sin
    half_rows = rows_p // 2
    out_grid = jnp.einsum("nk,ckq->cnq", pp_real[:half_rows], e_real, precision=high) - jnp.einsum(
        "nk,ckq->cnq", pp_imag[:half_rows], e_imag, precision=high
    )
    return out_grid.reshape(width, seq_len).T


def body(tokens, w_in, conv_taps, causal_taps, anticausal_taps, skip_gain, w_out):
    tok_rows = tokens.shape[0]
    channels = w_out.shape[0]
    groups = lax.axis_size("fft")
    blk_index = lax.axis_index("blk")
    fft_index = lax.axis_index("fft")
    device_index = blk_index * groups + fft_index
    position = device_index * tok_rows + jnp.arange(tok_rows, dtype=jnp.int32)
    proj = jnp.dot(tokens, w_in, preferred_element_type=jnp.float32).astype(jnp.bfloat16)
    framed = with_halo(proj, ((("blk", "fft"), 0),), 1).astype(jnp.float32)
    short = conv_taps[0] * framed[:-2] + conv_taps[1] * framed[1:-1] + conv_taps[2] * framed[2:]
    first = short[:, :channels]
    second = short[:, channels : 2 * channels]
    value_part = short[:, 2 * channels :]
    signal = first * value_part
    anticausal = jnp.where(position[:, None] > 0, anticausal_taps.astype(jnp.float32), 0.0)
    causal = causal_taps.astype(jnp.float32)
    moved = (
        lax.all_to_all(
            signal.astype(jnp.bfloat16), "fft", split_axis=1, concat_axis=0, tiled=True
        ).astype(signal.dtype),
        lax.all_to_all(
            causal.astype(jnp.bfloat16), "fft", split_axis=1, concat_axis=0, tiled=True
        ).astype(causal.dtype),
        lax.all_to_all(
            anticausal.astype(jnp.bfloat16), "fft", split_axis=1, concat_axis=0, tiled=True
        ).astype(anticausal.dtype),
    )
    moved = (
        lax.all_to_all(
            moved[0].astype(jnp.bfloat16), "blk", split_axis=1, concat_axis=0, tiled=True
        ).astype(jnp.float32),
        lax.all_to_all(
            moved[1].astype(jnp.bfloat16), "blk", split_axis=1, concat_axis=0, tiled=True
        ).astype(jnp.float32),
        lax.all_to_all(
            moved[2].astype(jnp.bfloat16), "blk", split_axis=1, concat_axis=0, tiled=True
        ).astype(jnp.float32),
    )
    conv_cols = local_convolution(moved[0], moved[1], moved[2])
    returned = lax.all_to_all(
        shortened(conv_cols), "blk", split_axis=0, concat_axis=1, tiled=True
    ).astype(conv_cols.dtype)
    convolved = lax.all_to_all(
        shortened(returned), "fft", split_axis=0, concat_axis=1, tiled=True
    ).astype(returned.dtype)
    convolved = convolved + skip_gain * signal
    gated = (second * convolved).astype(jnp.bfloat16)
    return jnp.dot(gated, w_out, preferred_element_type=jnp.float32).astype(jnp.bfloat16)


def grid_constants(blocks, width):
    length = 2 * blocks * width
    half_freq = np.arange(blocks) + 0.5

    rows = np.outer(half_freq, np.arange(2 * blocks)) * (2.0 * np.pi / (2 * blocks))
    flip = np.where(np.arange(2 * blocks) < blocks, 1.0, -1.0)
    across = np.concatenate([np.cos(rows), -np.sin(rows)], axis=0) * flip
    across = across.astype(ml_dtypes.bfloat16)
    turn = np.outer(half_freq, np.arange(width)) * (2.0 * np.pi / length)
    twist = np.stack([np.cos(turn), np.sin(turn)]).astype(np.float32)
    grid = np.outer(np.arange(width), np.arange(width)) % width * (2.0 * np.pi / width)
    cos, sin = np.cos(grid), np.sin(grid)
    within = np.block([[cos, -sin], [sin, cos]]).astype(np.float32)
    back = rows[:, :blocks].T
    back = np.concatenate([np.cos(back), np.sin(back)], axis=1) * (2.0 / length)
    back = back.astype(ml_dtypes.bfloat16)
    return across, twist, within, back


def dot32(a, b):
    return jnp.dot(a, b, preferred_element_type=jnp.float32)


def mixer_kernel(
    blocks,
    groups,
    tokens_hbm,
    causal_hbm,
    anti_hbm,
    conv_taps_hbm,
    skip_gain_hbm,
    across_hbm,
    twist_hbm,
    back_hbm,
    w_in_hbm,
    w_out_hbm,
    within_hbm,
    out,
    causal,
    anti,
    conv_taps,
    skip_gain,
    across,
    twist,
    back,
    w_in,
    w_out,
    within_whole,
    within,
    framed,
    edge_out,
    edge_in,
    filt_out,
    filt_in,
    sig_out,
    sig_in,
    ret_out,
    ret_in,
    spread,
    gather,
    result,
    spectrum,
    load_sem,
    edge_send,
    edge_recv,
    filt_send,
    filt_recv,
    sig_send,
    sig_recv,
    ret_send,
    ret_recv,
):
    f32, bf16 = jnp.float32, jnp.bfloat16
    width, depth = tokens_hbm.shape
    channels = w_out.shape[0]
    parts, _, some, _ = sig_out.shape
    tokens = framed.at[0:width]
    blk, fft = lax.axis_index("blk"), lax.axis_index("fft")
    me = blk * groups + fft
    levels = blocks // groups
    peers = []
    for turn in range(levels - 1, -1, -1):
        level = blk ^ turn
        for step in range(groups):
            if turn > 0 or step > 0:
                other = (fft + step) & (groups - 1)
                peers.append((level * groups + other, (level, other)))

    barrier = pltpu.get_barrier_semaphore()
    for _, coords in peers:
        pl.semaphore_signal(barrier, inc=1, device_id=coords, device_id_type=MESH)

    loads = [
        pltpu.make_async_copy(src, dst, load_sem.at[i])
        for i, (src, dst) in enumerate(
            (
                (causal_hbm, causal),
                (anti_hbm, anti),
                (tokens_hbm, tokens),
                (w_in_hbm, w_in),
                (conv_taps_hbm, conv_taps),
                (across_hbm, across),
                (twist_hbm, twist),
                (within_hbm, within_whole),
                (back_hbm, back),
                (w_out_hbm, w_out),
                (skip_gain_hbm, skip_gain),
            )
        )
    ]
    for load in loads:
        load.start()

    def send_all(src, dst, send_sem, recv_sem):
        for peer, coords in peers:
            pltpu.make_async_remote_copy(
                src_ref=src.at[peer],
                dst_ref=dst.at[me],
                send_sem=send_sem,
                recv_sem=recv_sem,
                device_id=coords,
                device_id_type=MESH,
            ).start()
        pltpu.make_async_copy(src.at[me], dst.at[me], recv_sem).start()

    def all_arrived(dst, recv_sem):
        pltpu.make_async_copy(dst, dst, recv_sem).wait()

    def sent(src, send_sem):
        most = src.at[pl.ds(0, blocks - 1)]
        pltpu.make_async_copy(most, most, send_sem).wait()

    def chunks(x):
        return x.T.reshape(blocks, parts, some, width)

    for load in loads[:3]:
        load.wait()
    edge_out[0] = tokens[width - 16 :, :].astype(f32)[15:16]
    edge_out[1] = tokens[0:16, :].astype(f32)[0:1]
    unused = (lax.broadcasted_iota(jnp.int32, anti.shape, 0) == 0) & (me == 0)
    causal_rows = chunks(causal[...].astype(f32))
    anti_rows = chunks(jnp.where(unused, 0.0, anti[...].astype(f32)))
    for part in range(parts):
        filt_out[part, :, 0:some, :] = causal_rows[:, part].astype(bf16)
        filt_out[part, :, some:, :] = anti_rows[:, part].astype(bf16)
    pl.semaphore_wait(barrier, blocks - 1)
    edges = [
        pltpu.make_async_remote_copy(
            src_ref=edge_out.at[i],
            dst_ref=edge_in.at[i],
            send_sem=edge_send.at[i],
            recv_sem=edge_recv.at[i],
            device_id=(at // groups, at % groups),
            device_id_type=MESH,
        )
        for i, at in enumerate(((me + 1) % blocks, (me + blocks - 1) % blocks))
    ]
    for edge in edges:
        edge.start()

    def send_part(bufs, part):
        src, dst, send_sem, recv_sem = bufs
        send_all(src.at[part], dst.at[part], send_sem.at[part], recv_sem.at[part])

    filt = (filt_out, filt_in, filt_send, filt_recv)
    sig = (sig_out, sig_in, sig_send, sig_recv)
    ret = (ret_out, ret_in, ret_send, ret_recv)
    for part in range(parts):
        send_part(filt, part)

    for load in loads[3:5]:
        load.wait()
    for edge in edges:
        edge.wait()
    row16 = lax.broadcasted_iota(jnp.int32, (16, depth), 0)
    prev = jnp.where(me == 0, 0.0, edge_in[0])
    following = jnp.where(me == blocks - 1, 0.0, edge_in[1])
    framed[width:, :] = jnp.where(
        row16 == 0, prev, jnp.where(row16 == 1, following, 0.0)
    ).astype(bf16)
    row = lax.broadcasted_iota(jnp.int32, (width, channels), 0)

    def stream(which):
        cols = slice(which * channels, (which + 1) * channels)
        proj = dot32(framed[...], w_in[:, cols]).astype(bf16).astype(f32)
        here = proj[:width]
        before = jnp.where(row == 0, proj[width : width + 1], pltpu.roll(here, 1, 0))
        after = jnp.where(
            row == width - 1, proj[width + 1 : width + 2], pltpu.roll(here, width - 1, 0)
        )
        taps = conv_taps[:, cols]
        return taps[0:1] * before + taps[1:2] * here + taps[2:3] * after

    signal = stream(0) * stream(2)
    signal_rows = chunks(signal)
    for part in range(parts):
        sig_out[part] = signal_rows[:, part].astype(bf16)
        send_part(sig, part)

    for load in loads[5:]:
        load.wait()
    second = stream(1)
    direct = skip_gain[...] * signal
    within[...] = within_whole[...].astype(bf16)
    cos, sin = twist[0], twist[1]

    def twisted(real, imag, axis):
        return jnp.concatenate([real * cos + imag * sin, imag * cos - real * sin], axis=axis)

    def lane(x, c):
        return x[:, c * width : (c + 1) * width]

    def forward(columns, mats):
        freq = dot32(mats, jnp.concatenate(columns, axis=1))
        turned = [
            twisted(lane(freq[:blocks], c), lane(freq[blocks:], c), 1)
            for c in range(len(columns))
        ]
        return dot32(jnp.concatenate(turned, axis=0).astype(bf16), within[...])

    for part in range(parts):
        all_arrived(filt_in.at[part], filt_recv.at[part])
        spread[...] = filt_in[part].astype(f32).reshape(2 * blocks * some, width)
        columns = [
            jnp.concatenate(
                [
                    spread[pl.ds(c, blocks, stride=2 * some), :],
                    spread[pl.ds(some + c, blocks, stride=2 * some), :],
                ],
                axis=0,
            ).astype(bf16)
            for c in range(some)
        ]
        spectrum[...] = forward(columns, across[...])

        all_arrived(sig_in.at[part], sig_recv.at[part])
        gather[...] = sig_in[part].astype(f32).reshape(blocks * some, width)
        columns = [
            gather[pl.ds(c, blocks, stride=some), :].astype(bf16) for c in range(some)
        ]
        freq = forward(columns, across[:, 0:blocks])
        s_real, s_imag = freq[:, :width], freq[:, width:]
        f_real, f_imag = spectrum[:, :width], spectrum[:, width:]
        product = jnp.concatenate(
            [s_real * f_real - s_imag * f_imag, -(s_real * f_imag + s_imag * f_real)],
            axis=1,
        )
        turned = dot32(product.astype(bf16), within[...])
        pieces = [turned[i * blocks : (i + 1) * blocks] for i in range(some)]
        pieces = [twisted(x[:, :width], x[:, width:], 0) for x in pieces]
        conv = dot32(back[...], jnp.concatenate(pieces, axis=1).astype(bf16))
        for c in range(some):
            result[pl.ds(c, blocks, stride=some), :] = lane(conv, c)
        ret_out[part] = result[...].astype(bf16).reshape(blocks, some, width)
        send_part(ret, part)

    for part in range(parts):
        all_arrived(ret_in.at[part], ret_recv.at[part])
    landed = jnp.concatenate([ret_in[part].astype(f32) for part in range(parts)], axis=1)
    convolved = landed.reshape(channels, width).T + direct
    out[...] = dot32((second * convolved).astype(bf16), w_out[...]).astype(bf16)
    for src, _, send_sem, _ in (filt, sig, ret):
        for part in range(parts):
            sent(src.at[part], send_sem.at[part])


def one_kernel(tokens, w_in, conv_taps, causal_taps, anticausal_taps, skip_gain, w_out):
    width, depth = tokens.shape
    channels = w_out.shape[0]
    groups = lax.axis_size("fft")
    blocks = lax.axis_size("blk") * groups
    parts = 2
    some = channels // blocks // parts
    across, twist, within, back = grid_constants(blocks, width)
    f32, bf16 = jnp.float32, jnp.bfloat16
    vmem = pl.BlockSpec(memory_space=pltpu.VMEM)
    hbm = pl.BlockSpec(memory_space=pl.ANY)
    one = pltpu.SemaphoreType.DMA
    return pl.pallas_call(
        functools.partial(mixer_kernel, blocks, groups),
        out_shape=pltpu.VMEM((width, w_out.shape[1]), bf16),
        in_specs=[hbm] * 11,
        out_specs=vmem,
        scratch_shapes=[
            pltpu.VMEM(causal_taps.shape, bf16),
            pltpu.VMEM(anticausal_taps.shape, bf16),
            pltpu.VMEM(conv_taps.shape, f32),
            pltpu.VMEM((1, channels), f32),
            pltpu.VMEM(across.shape, bf16),
            pltpu.VMEM(twist.shape, f32),
            pltpu.VMEM(back.shape, bf16),
            pltpu.VMEM(w_in.shape, bf16),
            pltpu.VMEM(w_out.shape, bf16),
            pltpu.VMEM(within.shape, f32),
            pltpu.VMEM(within.shape, bf16),
            pltpu.VMEM((width + 16, depth), bf16),
            pltpu.VMEM((2, 1, depth), f32),
            pltpu.VMEM((2, 1, depth), f32),
            pltpu.VMEM((parts, blocks, 2 * some, width), bf16),
            pltpu.VMEM((parts, blocks, 2 * some, width), bf16),
            pltpu.VMEM((parts, blocks, some, width), bf16),
            pltpu.VMEM((parts, blocks, some, width), bf16),
            pltpu.VMEM((parts, blocks, some, width), bf16),
            pltpu.VMEM((parts, blocks, some, width), bf16),
            pltpu.VMEM((2 * blocks * some, width), f32),
            pltpu.VMEM((blocks * some, width), f32),
            pltpu.VMEM((blocks * some, width), f32),
            pltpu.VMEM((some * blocks, 2 * width), f32),
            one((11,)),
            one((2,)),
            one((2,)),
            one((parts,)),
            one((parts,)),
            one((parts,)),
            one((parts,)),
            one((parts,)),
            one((parts,)),
        ],
        compiler_params=pltpu.CompilerParams(
            collective_id=0, has_side_effects=True, vmem_limit_bytes=62 * 2**20
        ),
    )(
        tokens,
        causal_taps,
        anticausal_taps,
        conv_taps,
        skip_gain[None, :],
        jnp.asarray(across),
        jnp.asarray(twist),
        jnp.asarray(back),
        w_in,
        w_out,
        jnp.asarray(within),
    )


def mixer(tokens, w_in, conv_taps, causal_taps, anticausal_taps, skip_gain, w_out):
    devices = lax.axis_size("blk") * lax.axis_size("fft")
    fits = tokens.shape[0] == 128 and w_out.shape[0] == 16 * devices
    chosen = one_kernel if fits else body
    return chosen(tokens, w_in, conv_taps, causal_taps, anticausal_taps, skip_gain, w_out)


def solution(mesh):
    in_specs = (
        P(("blk", "fft"), None),
        P(),
        P(),
        P(("blk", "fft"), None),
        P(("blk", "fft"), None),
        P(),
        P(),
    )
    out_specs = P(("blk", "fft"), None)
    return jax.shard_map(mixer, mesh=mesh, in_specs=in_specs, out_specs=out_specs, check_vma=False)
```
